32 devices in a mesh: grp: 2 (over core), fsdp: 4 (over y, x), dp: 4 (over z).
Axes of the slice: x: 2, y: 2, z: 4, core: 2. Of those that a mesh axis runs over, the one named last changes fastest.
Arguments:
- acts: bfloat16 [2, 2432, 1024], P('grp', None, 'dp'), may hold values from -12 to 12
- modulation: float32 [2, 3, 2432], P('grp'), may hold values from -3 to 3
- w_in: bfloat16 [2, 9728, 2432], P('grp', 'fsdp'), may hold values from -0.125 to 0.125
- w_out: bfloat16 [2, 9728, 2432], P('grp', 'fsdp'), may hold values from -0.0625 to 0.0625
- zero_weight: bfloat16 [2432, 2432], P('fsdp'), may hold values from -0.125 to 0.125
- cotangent: bfloat16 [2, 2432, 1024], P('grp', 'fsdp', 'dp'), may hold values from -0.75 to 0.75
Outputs:
- block_out: bfloat16 [2, 2432, 1024], P('grp', 'fsdp', 'dp')
- input_grad: float32 [2, 2432, 1024], P('grp', 'fsdp', 'dp')
- zero_grad: float32 [2432, 2432], P('fsdp')
The draws below stay inside these ranges and needn't reach their ends.
All inputs are finite; a program needn't handle non-finite values.
Results may differ from the reference program's by a relative error of at most 0.0048.
Values may be sent and summed in bfloat16 or wider, within the bound.
No kernel may reach another device: no remote copies, remote signals or barrier semaphores. Data moves between devices by JAX's collectives and lax.ppermute only.
A program may use at most 128 MiB of HBM per device.

```python
import math
from functools import partial
import jax
import jax.numpy as jnp
from jax import lax

D = 2432
HID = 9728
SEQ = 1024


def draw_acts(key, part):
    key = jax.random.fold_in(key, 17)
    noise_key, feature_key, token_key = jax.random.split(key, 3)
    feature_scale = jnp.exp(jax.random.uniform(feature_key, (2, D, 1), jnp.float32, math.log(0.3), math.log(3.0)))
    token_scale = jnp.exp(jax.random.uniform(token_key, (2, 1, SEQ), jnp.float32, math.log(0.3), math.log(3.0)))
    noise = jax.random.normal(noise_key, (2, D, SEQ), jnp.float32)
    return jnp.clip(noise * feature_scale * token_scale, -12.0, 12.0).astype(jnp.bfloat16)


def block_scale(key, extent, pieces, least, largest):
    level, own = 1.0, jax.random.fold_in(key, 6)
    for dim, blocks in pieces:
        draws = jnp.exp(jax.random.uniform(jax.random.fold_in(own, dim), (blocks,), jnp.float32, least / len(pieces), largest / len(pieces)))
        level = level * jnp.repeat(draws, extent[dim] // blocks).reshape([-1 if axis == dim else 1 for axis in range(len(extent))])
    return level


def normal_values(rng, shape, scale, bound, pieces=(), dtype=jnp.bfloat16):
    entries = scale * jax.random.normal(rng, shape, jnp.float32)
    if pieces:
        entries = entries * block_scale(rng, shape, pieces, -0.22, 0.18)
    return jnp.clip(entries, -bound, bound).astype(dtype)


def setup_inputs(seed: int = 0) -> dict:
    arg_keys = jax.random.split(jax.random.key(seed), 7)
    return {
        "acts": draw_acts(jax.random.fold_in(arg_keys[6], 71), 0),
        "modulation": normal_values(arg_keys[1], (2, 3, D), 1.0, 3.0, ((0, 2),), jnp.float32),
        "w_in": normal_values(arg_keys[2], (2, HID, D), D ** -0.5, 0.125, ((0, 2), (1, 4))),
        "w_out": normal_values(arg_keys[3], (2, HID, D), HID ** -0.5, 0.0625, ((0, 2), (1, 4))),
        "zero_weight": normal_values(arg_keys[4], (D, D), D ** -0.5, 0.125, ((0, 4),)),
        "cotangent": normal_values(arg_keys[5], (2, D, SEQ), 0.125, 0.75, ((0, 2), (1, 4), (2, 4))),
    }


EPSILON = 1e-06

def layer_norm(values, mod_shift, mod_scale):
    token_mean = lax.optimization_barrier(jnp.mean(values, axis=0, keepdims=True))
    centred = values - token_mean
    variance = lax.optimization_barrier(jnp.mean(centred * centred, axis=0, keepdims=True))
    return centred * lax.rsqrt(variance + EPSILON) * (1.0 + mod_scale[:, None]) + mod_shift[:, None]

def gelu_tanh(values):
    return jax.nn.gelu(values, approximate=True)

def contract_rows(weights, columns):
    return lax.dot_general(weights, columns, (((0,), (0,)), ((), ())), preferred_element_type=jnp.float32)

def reference(acts, modulation, w_in, w_out, zero_weight, cotangent):
    saved = []
    sums = []
    for group in range(2):
        values = acts[group].astype(jnp.float32)
        normed = layer_norm(values, modulation[group, 0], modulation[group, 1]).astype(jnp.bfloat16)
        pre_act = jnp.dot(w_in[group], normed, preferred_element_type=jnp.float32)
        hidden = gelu_tanh(pre_act).astype(jnp.bfloat16)
        branch = contract_rows(w_out[group], hidden)
        saved.append((values, pre_act))
        sums.append(values + modulation[group, 2][:, None] * branch)
    control_out = sums[0].astype(jnp.bfloat16)
    residual = jnp.dot(zero_weight, control_out, preferred_element_type=jnp.float32)
    base_out = (sums[1] + residual).astype(jnp.bfloat16)
    zero_grad = lax.dot_general(cotangent[1], control_out, (((1,), (1,)), ((), ())), preferred_element_type=jnp.float32)
    control_up = contract_rows(zero_weight, cotangent[1]) + cotangent[0].astype(jnp.float32)
    upstreams = (control_up, cotangent[1].astype(jnp.float32))
    grads = []
    for group in range(2):
        values, pre_act = saved[group]
        gate_grad = (modulation[group, 2][:, None] * upstreams[group]).astype(jnp.bfloat16)
        hidden_grad = jnp.dot(w_out[group], gate_grad, preferred_element_type=jnp.float32)
        pre_grad = jax.vjp(gelu_tanh, pre_act)[1](hidden_grad)[0].astype(jnp.bfloat16)
        norm_grad = contract_rows(w_in[group], pre_grad)
        norm_map = partial(layer_norm, mod_shift=modulation[group, 0], mod_scale=modulation[group, 1])
        norm_back = jax.vjp(norm_map, values)[1]
        grads.append(upstreams[group] + norm_back(norm_grad)[0])
    return (jnp.stack([control_out, base_out]), jnp.stack(grads), zero_grad)
```

```python
import jax
import jax.numpy as jnp
from jax import lax
from jax.sharding import PartitionSpec as P

EPSILON = 1e-06
SQRT_2_OVER_PI = 0.7978845608028654


def contract_rows(weights, columns):
    return lax.dot_general(
        weights, columns, (((0,), (0,)), ((), ())), preferred_element_type=jnp.float32
    )


def swap_fsdp(value, mask):
    length = lax.axis_size("fsdp")
    return lax.ppermute(value, "fsdp", [(i, i ^ mask) for i in range(length)])


def swap_grp(value):
    return lax.ppermute(value, "grp", [(0, 1), (1, 0)])


def block_of(value, index, rows):
    return lax.dynamic_slice_in_dim(value, index * rows, rows, 0)


def scatter_sum(term, rows, me):
    total = block_of(term, me, rows)
    for mask in range(1, lax.axis_size("fsdp")):
        sent = block_of(term, me ^ mask, rows).astype(jnp.bfloat16)
        total = total + swap_fsdp(sent, mask).astype(jnp.float32)
    return total


def gather_rows(value, me):
    length = lax.axis_size("fsdp")
    rows = value.shape[0]
    full = jnp.zeros((length * rows,) + value.shape[1:], value.dtype)
    full = lax.dynamic_update_slice_in_dim(full, value, me * rows, 0)
    for mask in range(1, length):
        full = lax.dynamic_update_slice_in_dim(full, swap_fsdp(value, mask), (me ^ mask) * rows, 0)
    return full


def gelu_and_slope(v):
    inner = SQRT_2_OVER_PI * (v + 0.044715 * v * v * v)
    t = jnp.tanh(inner)
    slope = 0.5 * (1.0 + t) + 0.5 * v * (1.0 - t * t) * SQRT_2_OVER_PI * (1.0 + 3 * 0.044715 * v * v)
    return 0.5 * v * (1.0 + t), slope


def local(acts, modulation, w_in, w_out, zero_weight, cotangent):
    inputs = acts[0]
    shift, scale, gate = modulation[0, 0], modulation[0, 1], modulation[0, 2]
    w_first, w_second = w_in[0], w_out[0]
    own_cot = cotangent[0]
    features, tokens = inputs.shape
    rows = own_cot.shape[0]
    half = tokens // 2
    group = lax.axis_index("grp")
    is_control = group == 0
    me = lax.axis_index("fsdp")

    mine = lax.dynamic_slice_in_dim(own_cot, group * half, half, 1)
    other = lax.dynamic_slice_in_dim(own_cot, (1 - group) * half, half, 1)
    arrived = swap_grp(other)
    cot1 = jnp.where(is_control, arrived, mine)
    cot0 = jnp.where(is_control, mine, arrived)
    gate0 = jnp.where(is_control, gate, swap_grp(gate))
    own_gate = block_of(gate, me, rows)
    own_gate0 = block_of(gate0, me, rows)

    up_term = contract_rows(zero_weight, cot1)
    up_half = scatter_sum(up_term, rows, me) + cot0.astype(jnp.float32)
    gated = gather_rows((own_gate0[:, None] * up_half).astype(jnp.bfloat16), me)
    cot1_full = gather_rows(cot1, me)
    crossed = swap_grp(jnp.where(is_control, cot1_full, gated))
    gate_grad = jnp.where(
        is_control,
        jnp.concatenate([gated, crossed], 1),
        (gate[:, None] * jnp.concatenate([crossed, cot1_full], 1).astype(jnp.float32)).astype(jnp.bfloat16),
    )
    up_rows = jnp.where(
        is_control,
        jnp.concatenate([up_half, swap_grp(up_half)], 1),
        own_cot.astype(jnp.float32),
    )

    values = inputs.astype(jnp.float32)
    mean = jnp.mean(values, axis=0, keepdims=True)
    centred = values - mean
    inv = lax.rsqrt(jnp.mean(centred * centred, axis=0, keepdims=True) + EPSILON)
    xhat = centred * inv
    normed = (xhat * (1.0 + scale[:, None]) + shift[:, None]).astype(jnp.bfloat16)
    pre_act = jnp.dot(w_first, normed, preferred_element_type=jnp.float32)
    hidden, slope = gelu_and_slope(pre_act)
    branch_term = contract_rows(w_second, hidden.astype(jnp.bfloat16))
    branch = scatter_sum(branch_term, rows, me)
    own_values = block_of(inputs, me, rows).astype(jnp.float32)
    sums = own_values + own_gate[:, None] * branch
    out_rows = sums.astype(jnp.bfloat16)

    out_half = jnp.where(is_control, out_rows[:, :half], swap_grp(out_rows[:, half:]))
    out_full = gather_rows(out_half, me)
    residual = jnp.dot(zero_weight, out_full, preferred_element_type=jnp.float32)
    residual = jnp.concatenate([swap_grp(residual), residual], 1)
    block_rows = jnp.where(is_control, out_rows, (sums + residual).astype(jnp.bfloat16))

    cot_all = lax.all_gather(cot1, "dp")
    out_all = lax.all_gather(out_half, "dp")
    out_all = gather_rows(jnp.swapaxes(out_all, 0, 1), me)
    cot_other, out_other = swap_grp(cot_all), swap_grp(out_all)
    zero_grad = jnp.einsum("dit,jdt->ij", cot_all, out_all, preferred_element_type=jnp.float32)
    zero_other = jnp.einsum("dit,jdt->ij", cot_other, out_other, preferred_element_type=jnp.float32)
    zero_grad = zero_grad + zero_other

    hidden_grad = jnp.dot(w_second, gate_grad, preferred_element_type=jnp.float32)
    pre_grad = (hidden_grad * slope).astype(jnp.bfloat16)
    norm_term = contract_rows(w_first, pre_grad)
    scaled = norm_term * (1.0 + scale[:, None])
    token_sums = jnp.stack([jnp.sum(scaled, 0), jnp.sum(scaled * xhat, 0)])
    total_sums = token_sums
    for mask in range(1, lax.axis_size("fsdp")):
        total_sums = total_sums + swap_fsdp(token_sums, mask)
    norm_grad = scatter_sum(norm_term, rows, me)
    own_xhat = (own_values - mean) * inv
    own_scale = block_of(scale, me, rows)
    total_sums = total_sums / features
    back = inv * (
        norm_grad * (1.0 + own_scale[:, None]) - total_sums[0:1] - own_xhat * total_sums[1:2]
    )
    return (block_rows[None], (up_rows + back)[None], zero_grad)


def solution(mesh):
    placed = (
        P("grp", None, "dp"),
        P("grp", None, None),
        P("grp", "fsdp", None),
        P("grp", "fsdp", None),
        P("fsdp", None),
        P("grp", "fsdp", "dp"),
    )
    return jax.shard_map(
        local,
        mesh=mesh,
        in_specs=placed,
        out_specs=(P("grp", "fsdp", "dp"), P("grp", "fsdp", "dp"), P("fsdp", None)),
        check_vma=False,
    )
```

```python
import functools

import jax
import jax.numpy as jnp
from jax import lax
from jax.experimental import pallas as pl
from jax.experimental.pallas import tpu as pltpu
from jax.sharding import PartitionSpec as P

EPSILON = 1e-06
SQRT_2_OVER_PI = 0.7978845608028654
CHUNK = 256
AHEAD = 6
VMEM_LIMIT = 50 * 1024 * 1024


def pieces(extent, size=CHUNK):
    return [(start, min(size, extent - start)) for start in range(0, extent, size)]


def swap_grp(value):
    return lax.ppermute(value, "grp", [(0, 1), (1, 0)])


def trade(blocks, axis):
    return lax.all_to_all(blocks, axis, 0, 0)


def spread(value, axis):
    return trade(jnp.broadcast_to(value[None], (lax.axis_size(axis),) + value.shape), axis)


def block_of(value, index, rows):
    return lax.dynamic_slice_in_dim(value, index * rows, rows, 0)


def split_three(value):
    high = value.astype(jnp.bfloat16)
    rest = value - high.astype(jnp.float32)
    middle = rest.astype(jnp.bfloat16)
    low = (rest - middle.astype(jnp.float32)).astype(jnp.bfloat16)
    return high, middle, low


def gelu_and_slope(v):
    square = v * v
    t = jnp.tanh(SQRT_2_OVER_PI * (v + 0.044715 * (square * v)))
    rise = 0.5 * (1.0 + t)
    slope = rise + 0.5 * v * (1.0 - t * t) * (SQRT_2_OVER_PI * (1.0 + (3 * 0.044715) * square))
    return v * rise, slope


def transposed_product(lhs, rhs):
    return lax.dot_general(lhs, rhs, (((0,), (0,)), ((), ())), preferred_element_type=jnp.float32)


def weight_copies(first, first_buf, second, second_buf, sems):
    copies = []
    for start, size in pieces(first_buf.shape[0]):
        rows = pl.ds(start, size)
        copies.append((first.at[0, rows, :], first_buf.at[rows, :]))
    for start, size in pieces(second_buf.shape[1]):
        columns = pl.ds(start, size)
        copies.append((second.at[0, :, columns], second_buf.at[:, columns]))
    return [pltpu.make_async_copy(a, b, sems.at[k]) for k, (a, b) in enumerate(copies)]


class Stream:
    def __init__(self, copies):
        self.copies, self.next = copies, 0
        for copy in copies[:AHEAD]:
            copy.start()

    def take(self):
        k = self.next
        self.copies[k].wait()
        if k + AHEAD < len(self.copies):
            self.copies[k + AHEAD].start()
        self.next = k + 1


def forward_kernel(acts, mod, w_in, w_out, branch, slope_out, stats, in_buf, out_buf, normed, turned, sems):
    features, tokens = acts.shape[1:]
    stream = Stream(weight_copies(w_in, in_buf, w_out, out_buf, sems))
    parts = pieces(features, 128)
    total = jnp.zeros((1, tokens), jnp.float32)
    for start, size in parts:
        total += jnp.sum(acts[0, pl.ds(start, size), :].astype(jnp.float32), 0, keepdims=True)
    mean = total / features
    total = jnp.zeros((1, tokens), jnp.float32)
    for start, size in parts:
        centred = acts[0, pl.ds(start, size), :].astype(jnp.float32) - mean
        total += jnp.sum(centred * centred, 0, keepdims=True)
    inv = lax.rsqrt(total / features + EPSILON)
    stats[0:1, :] = mean
    stats[1:2, :] = inv
    for start, size in parts:
        rows = pl.ds(start, size)
        xhat = (acts[0, rows, :].astype(jnp.float32) - mean) * inv
        normed[rows, :] = (xhat * (1.0 + mod[rows, 1:2]) + mod[rows, 0:1]).astype(jnp.bfloat16)
    for start, size in pieces(in_buf.shape[0]):
        stream.take()
        rows = pl.ds(start, size)
        pre = jnp.dot(in_buf[rows, :], normed[...], preferred_element_type=jnp.float32)
        hidden, slope = gelu_and_slope(pre)
        slope_out[rows, :] = slope
        turned[:, rows] = hidden.T.astype(jnp.bfloat16)
    for start, size in pieces(features):
        stream.take()
        columns = pl.ds(start, size)
        part = jnp.dot(turned[...], out_buf[:, columns], preferred_element_type=jnp.float32)
        branch[columns, :] = part.T.astype(jnp.bfloat16)


def forward(acts, mod, w_in, w_out):
    features, tokens = acts.shape[1:]
    hidden = w_in.shape[1]
    count = len(pieces(hidden)) + len(pieces(features))
    whole = pl.BlockSpec(memory_space=pltpu.VMEM)
    return pl.pallas_call(
        forward_kernel,
        out_shape=(
            jax.ShapeDtypeStruct((features, tokens), jnp.bfloat16),
            jax.ShapeDtypeStruct((hidden, tokens), jnp.float32),
            jax.ShapeDtypeStruct((2, tokens), jnp.float32),
        ),
        in_specs=[whole, whole, pl.BlockSpec(memory_space=pl.ANY), pl.BlockSpec(memory_space=pl.ANY)],
        out_specs=(whole, whole, whole),
        scratch_shapes=[
            pltpu.VMEM((hidden, features), jnp.bfloat16),
            pltpu.VMEM((hidden, features), jnp.bfloat16),
            pltpu.VMEM((features, tokens), jnp.bfloat16),
            pltpu.VMEM((tokens, hidden), jnp.bfloat16),
            pltpu.SemaphoreType.DMA((count,)),
        ],
        compiler_params=pltpu.CompilerParams(vmem_limit_bytes=VMEM_LIMIT),
        cost_estimate=pl.CostEstimate(
            flops=4 * hidden * features * tokens,
            bytes_accessed=4 * hidden * features + 4 * hidden * tokens + 4 * features * tokens,
            transcendentals=hidden * tokens,
        ),
        name="forward_layers",
    )(acts, mod, w_in, w_out)


def backward_kernel(
    group, rows_each, own, crossed, factor, slope, acts, stats, mod, w_in, w_out,
    sent, in_buf, out_buf, grad, turned, norm, sems,
):
    features, tokens = acts.shape[1:]
    half = tokens // 2
    stream = Stream(weight_copies(w_out, out_buf, w_in, in_buf, sems))
    mine = pl.multiple_of(group[0] * half, half)
    theirs = pl.multiple_of((1 - group[0]) * half, half)
    for start, size in pieces(features, 128):
        rows = pl.ds(start, size)
        grad[rows, pl.ds(mine, half)] = (own[rows, :].astype(jnp.float32) * factor[rows, 0:1]).astype(jnp.bfloat16)
        grad[rows, pl.ds(theirs, half)] = (
            crossed[rows, :].astype(jnp.float32) * factor[rows, 0:1]
        ).astype(jnp.bfloat16)
    for start, size in pieces(out_buf.shape[0]):
        stream.take()
        rows = pl.ds(start, size)
        hidden_grad = jnp.dot(out_buf[rows, :], grad[...], preferred_element_type=jnp.float32)
        turned[:, rows] = (hidden_grad * slope[rows, :]).T.astype(jnp.bfloat16)
    mean, inv = stats[0:1, :], stats[1:2, :]
    plain = jnp.zeros((1, tokens), jnp.float32)
    along = jnp.zeros((1, tokens), jnp.float32)
    for start, size in pieces(features):
        stream.take()
        columns = pl.ds(start, size)
        part = jnp.dot(turned[...], in_buf[:, columns], preferred_element_type=jnp.float32).T
        norm[columns, :] = part
        scaled = part * (1.0 + mod[columns, 1:2])
        xhat = (acts[0, columns, :].astype(jnp.float32) - mean) * inv
        plain += jnp.sum(scaled, 0, keepdims=True)
        along += jnp.sum(scaled * xhat, 0, keepdims=True)
    tail = [part.astype(jnp.float32) for part in split_three(plain) + split_three(along)]
    tail = jnp.concatenate(tail + [jnp.zeros((10, tokens), jnp.float32)], 0).astype(jnp.bfloat16)
    padded = sent.shape[1] - 16
    for block in range(sent.shape[0]):
        rows = norm[pl.ds(block * rows_each, rows_each), :]
        if padded > rows_each:
            rows = jnp.concatenate([rows, jnp.zeros((padded - rows_each, tokens), jnp.float32)], 0)
        sent[block, 0:padded, :] = rows.astype(jnp.bfloat16)
        sent[block, padded:, :] = tail


def backward(group, own, crossed, factor, slope, acts, stats, mod, w_in, w_out, blocks):
    features, tokens = acts.shape[1:]
    hidden = w_in.shape[1]
    count = len(pieces(hidden)) + len(pieces(features))
    rows = features // blocks
    whole = pl.BlockSpec(memory_space=pltpu.VMEM)
    held = pl.BlockSpec(memory_space=pl.ANY)

    def kernel(group, *refs):
        backward_kernel(group, rows, *refs)

    return pl.pallas_call(
        kernel,
        out_shape=jax.ShapeDtypeStruct((blocks, -(-rows // 16) * 16 + 16, tokens), jnp.bfloat16),
        in_specs=[pl.BlockSpec(memory_space=pltpu.SMEM)] + [whole] * 7 + [held] * 2,
        out_specs=whole,
        scratch_shapes=[
            pltpu.VMEM((hidden, features), jnp.bfloat16),
            pltpu.VMEM((hidden, features), jnp.bfloat16),
            pltpu.VMEM((features, tokens), jnp.bfloat16),
            pltpu.VMEM((tokens, hidden), jnp.bfloat16),
            pltpu.VMEM((features, tokens), jnp.float32),
            pltpu.SemaphoreType.DMA((count,)),
        ],
        compiler_params=pltpu.CompilerParams(vmem_limit_bytes=VMEM_LIMIT),
        cost_estimate=pl.CostEstimate(
            flops=4 * hidden * features * tokens,
            bytes_accessed=4 * hidden * features + 4 * hidden * tokens + 6 * features * tokens,
            transcendentals=0,
        ),
        name="backward_layers",
    )(group, own, crossed, factor, slope, acts, stats, mod, w_in, w_out)


def zero_grad_kernel(group, cot, cot_other, out, out_other, grad, lhs, rhs):
    parts, rows, half = cot.shape
    blocks = out.shape[0]
    mine = group[0] * half
    theirs = (1 - group[0]) * half
    for part in range(parts):
        for offset, left, right in ((mine, cot, out), (theirs, cot_other, out_other)):
            lanes = pl.ds(pl.multiple_of(part * 2 * half + offset, half), half)
            lhs[:, lanes] = left[part]
            for block in range(blocks):
                rhs[pl.ds(block * rows, rows), lanes] = right[block, part]
    for start, size in pieces(rhs.shape[0]):
        columns = pl.ds(start, size)
        grad[:, columns] = lax.dot_general(
            lhs[...], rhs[columns, :], (((1,), (1,)), ((), ())), preferred_element_type=jnp.float32
        )


def zero_projection_grad(group, cot, cot_other, out, out_other):
    parts, rows, half = cot.shape
    features = out.shape[0] * rows
    whole = pl.BlockSpec(memory_space=pltpu.VMEM)
    return pl.pallas_call(
        zero_grad_kernel,
        out_shape=jax.ShapeDtypeStruct((rows, features), jnp.float32),
        in_specs=[pl.BlockSpec(memory_space=pltpu.SMEM)] + [whole] * 4,
        out_specs=whole,
        scratch_shapes=[
            pltpu.VMEM((rows, parts * 2 * half), jnp.bfloat16),
            pltpu.VMEM((features, parts * 2 * half), jnp.bfloat16),
        ],
        compiler_params=pltpu.CompilerParams(vmem_limit_bytes=VMEM_LIMIT),
        cost_estimate=pl.CostEstimate(
            flops=4 * parts * half * rows * features,
            bytes_accessed=4 * rows * features + 4 * parts * half * (rows + features),
            transcendentals=0,
        ),
        name="zero_projection_grad",
    )(group, cot, cot_other, out, out_other)


def upstream_kernel(weight, cot, sent):
    blocks, rows, tokens = sent.shape
    full = transposed_product(cot[...], weight[...]).T
    for block in range(blocks):
        sent[block] = full[block * rows : (block + 1) * rows, :].astype(jnp.bfloat16)


def upstream_terms(weight, cot, blocks):
    rows, tokens = cot.shape
    whole = pl.BlockSpec(memory_space=pltpu.VMEM)
    return pl.pallas_call(
        upstream_kernel,
        out_shape=jax.ShapeDtypeStruct((blocks, rows, tokens), jnp.bfloat16),
        in_specs=[whole] * 2,
        out_specs=whole,
        compiler_params=pltpu.CompilerParams(vmem_limit_bytes=VMEM_LIMIT),
        cost_estimate=pl.CostEstimate(
            flops=2 * weight.size * tokens, bytes_accessed=2 * weight.size + 2 * blocks * rows * tokens, transcendentals=0
        ),
        name="upstream_terms",
    )(weight, cot)


def local(acts, modulation, w_in, w_out, zero_weight, cotangent):
    own_cot = cotangent[0]
    features, tokens = acts.shape[1:]
    rows = own_cot.shape[0]
    half = tokens // 2
    blocks = lax.axis_size("fsdp")
    group = lax.axis_index("grp")
    is_control = group == 0
    group_ref = group.astype(jnp.int32)[None]
    me = lax.axis_index("fsdp")
    mod = modulation[0].T
    gate = mod[:, 2:3]

    mine = lax.dynamic_slice_in_dim(own_cot, group * half, half, 1)
    other = lax.dynamic_slice_in_dim(own_cot, (1 - group) * half, half, 1)
    arrived = swap_grp(other)
    cot1 = jnp.where(is_control, arrived, mine)
    cot0 = jnp.where(is_control, mine, arrived)
    own_gate = block_of(gate, me, rows)
    own_gate0 = jnp.where(is_control, own_gate, swap_grp(own_gate))

    up_sent = upstream_terms(zero_weight, cot1, blocks)
    up_got = trade(jnp.concatenate([up_sent, jnp.broadcast_to(cot1[None], up_sent.shape)], 1), "fsdp")
    up_half = jnp.sum(up_got[:, :rows].astype(jnp.float32), 0) + cot0.astype(jnp.float32)
    cot1_full = up_got[:, rows:].reshape(features, half)
    gated = spread((own_gate0 * up_half).astype(jnp.bfloat16), "fsdp").reshape(features, half)
    crossed = swap_grp(jnp.where(is_control, cot1_full, gated))
    kept = jnp.where(is_control, gated, cot1_full)
    factor = jnp.where(is_control, 1.0, gate)
    up_rows = jnp.where(
        is_control,
        jnp.concatenate([up_half, swap_grp(up_half)], 1),
        own_cot.astype(jnp.float32),
    )

    branch_term, slope, stats = forward(acts, mod, w_in, w_out)
    branch = jnp.sum(trade(branch_term.reshape(blocks, rows, tokens), "fsdp").astype(jnp.float32), 0)
    own_values = block_of(acts[0], me, rows).astype(jnp.float32)
    sums = own_values + own_gate * branch
    out_rows = sums.astype(jnp.bfloat16)

    out_half = jnp.where(is_control, out_rows[:, :half], swap_grp(out_rows[:, half:]))
    out_full = spread(out_half, "fsdp").reshape(features, half)
    residual = jnp.dot(zero_weight, out_full, preferred_element_type=jnp.float32)
    residual = jnp.concatenate([swap_grp(residual), residual], 1)
    block_rows = jnp.where(is_control, out_rows, (sums + residual).astype(jnp.bfloat16))

    parts = lax.axis_size("dp")
    all_tokens = spread(jnp.concatenate([cot1, out_half], 0), "dp")
    cot_all = all_tokens[:, :rows]
    out_all = spread(all_tokens[:, rows:], "fsdp")
    zero_grad = zero_projection_grad(group_ref, cot_all, swap_grp(cot_all), out_all, swap_grp(out_all))

    norm_sent = backward(group_ref, kept, crossed, factor, slope, acts, stats, mod, w_in, w_out, blocks)
    norm_got = trade(norm_sent, "fsdp").astype(jnp.float32)
    norm_grad = jnp.sum(norm_got[:, :rows], 0)
    tail = jnp.sum(norm_got[:, -16:], 0)
    plain = (tail[0:1] + tail[1:2] + tail[2:3]) / features
    along = (tail[3:4] + tail[4:5] + tail[5:6]) / features
    mean, inv = stats[0:1], stats[1:2]
    own_scale = block_of(mod[:, 1:2], me, rows)
    back = inv * (norm_grad * (1.0 + own_scale) - plain - (own_values - mean) * inv * along)
    return (block_rows[None], (up_rows + back)[None], zero_grad)


def solution(mesh):
    placed = (
        P("grp", None, "dp"),
        P("grp", None, None),
        P("grp", "fsdp", None),
        P("grp", "fsdp", None),
        P("fsdp", None),
        P("grp", "fsdp", "dp"),
    )
    return jax.shard_map(
        local,
        mesh=mesh,
        in_specs=placed,
        out_specs=(P("grp", "fsdp", "dp"), P("grp", "fsdp", "dp"), P("fsdp", None)),
        check_vma=False,
    )
```

```python
import functools

import jax
import jax.numpy as jnp
from jax import lax
from jax.experimental import pallas as pl
from jax.experimental.pallas import tpu as pltpu
from jax.sharding import PartitionSpec as P

EPSILON = 1e-06
SQRT_2_OVER_PI = 0.7978845608028654
CHUNK = 256
WIDE = 2
AHEAD = 4
MIB = 1024 * 1024
F32, BF16 = jnp.float32, jnp.bfloat16
WHOLE = pl.BlockSpec(memory_space=pltpu.VMEM)
HELD = pl.BlockSpec(memory_space=pltpu.HBM)
SCALARS = pl.BlockSpec(memory_space=pltpu.SMEM)


def pieces(start, stop, size=CHUNK):
    return [(at, min(size, stop - at)) for at in range(start, stop, size)]


def middle(extent):
    step = CHUNK * WIDE
    return max(extent // 2 // step, 1) * step if extent > step else extent // 2 // 128 * 128


def after(value, *others):
    return lax.optimization_barrier((value,) + others)[0]


def swap_grp(value):
    return lax.ppermute(value, "grp", [(0, 1), (1, 0)])


def stages():
    return (lax.axis_size("fsdp") - 1).bit_length()


def step(value, stage):
    length, bits = lax.axis_size("fsdp"), stages()
    pairs = []
    for group, bit in ((0, stage), (1, bits - 1 - stage)):
        pairs += [(group * length + i, group * length + (i ^ (1 << bit))) for i in range(length)]
    return lax.ppermute(value, ("grp", "fsdp"), pairs)


def block_order(group, me):
    length, bits = lax.axis_size("fsdp"), stages()
    turned = [sum(((v >> b) & 1) << (bits - 1 - b) for b in range(bits)) for v in range(length)]
    up, down = jnp.arange(length, dtype=jnp.int32), jnp.array(turned, jnp.int32)
    return me ^ jnp.where(group == 0, up, down)


def gather_dp(value):
    length = lax.axis_size("dp")
    return [value] + [
        lax.ppermute(value, "dp", [(i, i ^ mask) for i in range(length)]) for mask in range(1, length)
    ]


def block_of(value, index, rows):
    return lax.dynamic_slice_in_dim(value, index * rows, rows, 0)


def split_three(value):
    high = value.astype(BF16)
    rest = value - high.astype(F32)
    mid = rest.astype(BF16)
    return high, mid, (rest - mid.astype(F32)).astype(BF16)


def pack_sums(plain, along):
    tail = [part.astype(F32) for part in split_three(plain) + split_three(along)]
    return jnp.concatenate(tail + [jnp.zeros((10, plain.shape[1]), F32)], 0).astype(BF16)


def unpack_sums(tail):
    tail = tail.astype(F32)
    return tail[0:1] + tail[1:2] + tail[2:3], tail[3:4] + tail[4:5] + tail[5:6]


def gelu_and_slope(v):
    square = v * v
    t = jnp.tanh(SQRT_2_OVER_PI * (v + 0.044715 * (square * v)))
    rise = 0.5 * (1.0 + t)
    slope = rise + 0.5 * v * (1.0 - t * t) * (SQRT_2_OVER_PI * (1.0 + (3 * 0.044715) * square))
    return v * rise, slope


class Stream:
    def __init__(self, pairs, sems):
        self.copies = [pltpu.make_async_copy(a, b, sems.at[k]) for k, (a, b) in enumerate(pairs)]
        self.next = 0
        for copy in self.copies[:AHEAD]:
            copy.start()

    def take(self):
        for k in range(self.next, min(self.next + WIDE, len(self.copies))):
            self.copies[k].wait()
            if k + AHEAD < len(self.copies):
                self.copies[k + AHEAD].start()
            self.next = k + 1


def row_stream(weight, buf, start, stop, sems):
    return Stream(
        [(weight.at[0, pl.ds(a, n), :], buf.at[pl.ds(a - start, n), :]) for a, n in pieces(start, stop)], sems
    )


def column_stream(weight, buf, start, stop, sems):
    return Stream(
        [(weight.at[0, :, pl.ds(a, n)], buf.at[:, pl.ds(a - start, n)]) for a, n in pieces(start, stop)], sems
    )


def pipelined(extent, product, finish):
    held = None
    for part in pieces(0, extent, CHUNK * WIDE):
        value = product(*part)
        if held is not None:
            finish(*held)
        held = part + (value,)
    finish(*held)


def params(flops, moved, transcendentals=0, grant=50):
    return dict(
        compiler_params=pltpu.CompilerParams(vmem_limit_bytes=grant * MIB),
        cost_estimate=pl.CostEstimate(flops=flops, bytes_accessed=moved, transcendentals=transcendentals),
    )


def struct(shape, dtype):
    return jax.ShapeDtypeStruct(shape, dtype)


def staging(rows, features, lanes):
    return pltpu.VMEM((features, lanes) if rows % 16 else (8, 128), F32)


def place_blocks(target, lanes, stage, order, blocks, rows, first=0):
    for place, value in enumerate(blocks):
        if rows % 16:
            stage[pl.ds(pl.multiple_of(order[first + place] * rows, 8), rows), :] = value().astype(F32)
        else:
            target[pl.ds(pl.multiple_of(order[first + place] * rows, 16), rows), lanes] = value()
    if rows % 16:
        target[:, lanes] = stage[...].astype(target.dtype)


def normalize(acts, mod, normed, stats):
    features, tokens = acts.shape[1:]
    parts = pieces(0, features, 128)
    total = jnp.zeros((1, tokens), F32)
    for start, size in parts:
        total += jnp.sum(acts[0, pl.ds(start, size), :].astype(F32), 0, keepdims=True)
    mean = total / features
    total = jnp.zeros((1, tokens), F32)
    for start, size in parts:
        centred = acts[0, pl.ds(start, size), :].astype(F32) - mean
        total += jnp.sum(centred * centred, 0, keepdims=True)
    inv = lax.rsqrt(total / features + EPSILON)
    stats[0:1, :] = mean
    stats[1:2, :] = inv
    for start, size in parts:
        rows = pl.ds(start, size)
        xhat = (acts[0, rows, :].astype(F32) - mean) * inv
        normed[rows, :] = (xhat * (1.0 + mod[rows, 1:2]) + mod[rows, 0:1]).astype(BF16)


def expand_products(stream, buf, normed, turned, slope_out):
    def product(at, size):
        stream.take()
        return jnp.dot(buf[pl.ds(at, size), :], normed[...], preferred_element_type=F32)

    def finish(at, size, pre):
        hidden, slope = gelu_and_slope(pre)
        slope_out[pl.ds(at, size), :] = slope
        turned[:, pl.ds(at, size)] = hidden.T.astype(BF16)

    pipelined(slope_out.shape[0], product, finish)


def expand_first_kernel(acts, mod, w_in, normed, stats, turned, slope_out, buf, sems):
    stream = row_stream(w_in, buf, 0, slope_out.shape[0], sems)
    normalize(acts, mod, normed, stats)
    expand_products(stream, buf, normed, turned, slope_out)


def expand_first(acts, mod, w_in, part, name):
    features, tokens = acts.shape[1:]
    return pl.pallas_call(
        expand_first_kernel,
        out_shape=(
            struct((features, tokens), BF16),
            struct((2, tokens), F32),
            struct((tokens, part), BF16),
            struct((part, tokens), F32),
        ),
        in_specs=[WHOLE, WHOLE, HELD],
        out_specs=[WHOLE] * 4,
        scratch_shapes=[pltpu.VMEM((part, features), BF16), pltpu.SemaphoreType.DMA((len(pieces(0, part)),))],
        name=name,
        **params(2 * part * features * tokens, 2 * part * features + 8 * part * tokens, part * tokens),
    )(acts, mod, w_in)


def expand_rest_kernel(start, normed, w_in, turned, slope_out, buf, sems):
    stream = row_stream(w_in, buf, start, start + slope_out.shape[0], sems)
    expand_products(stream, buf, normed, turned, slope_out)


def expand_rest(normed, w_in, start, name):
    features, tokens = normed.shape
    part = w_in.shape[1] - start
    return pl.pallas_call(
        functools.partial(expand_rest_kernel, start),
        out_shape=(struct((tokens, part), BF16), struct((part, tokens), F32)),
        in_specs=[WHOLE, HELD],
        out_specs=(WHOLE, WHOLE),
        scratch_shapes=[
            pltpu.VMEM((part, features), BF16),
            pltpu.SemaphoreType.DMA((len(pieces(start, start + part)),)),
        ],
        name=name,
        **params(2 * part * features * tokens, 2 * part * features + 8 * part * tokens, part * tokens),
    )(normed, w_in)


def write_blocks(order, full, sent, kept):
    for targets, shift in ((kept, 0), (sent, 1)):
        for place, target in enumerate(targets):
            rows = target.shape[0]
            offset = pl.multiple_of(order[2 * place + shift] * rows, 8)
            target[...] = full[pl.ds(offset, rows), :].astype(target.dtype)


def weight_rows_product(left, right, buf):
    split = left.shape[1]

    def product(at, size):
        columns = pl.ds(at, size)
        return jnp.dot(left[...], buf[:split, columns], preferred_element_type=F32) + jnp.dot(
            right[...], buf[split:, columns], preferred_element_type=F32
        )

    return product


def contract_first_kernel(stop, left, right, weight, full, buf, sems):
    stream = column_stream(weight, buf, 0, stop, sems)
    multiply = weight_rows_product(left, right, buf)

    def product(at, size):
        stream.take()
        return multiply(at, size)

    def finish(at, size, value):
        full[pl.ds(at, size), :] = value.T

    pipelined(stop, product, finish)


def contract_first(left, right, weight, stop, name):
    hidden, features = weight.shape[1:]
    tokens = left.shape[0]
    return pl.pallas_call(
        functools.partial(contract_first_kernel, stop),
        out_shape=struct((stop, tokens), F32),
        in_specs=[WHOLE, WHOLE, HELD],
        out_specs=WHOLE,
        scratch_shapes=[pltpu.VMEM((hidden, stop), BF16), pltpu.SemaphoreType.DMA((len(pieces(0, stop)),))],
        name=name,
        **params(2 * hidden * stop * tokens, 2 * hidden * stop + 2 * hidden * tokens + 4 * stop * tokens),
    )(left, right, weight)


def contract_last_kernel(order, left, right, weight, before, *refs):
    outs, (buf, full, sems) = refs[:-3], refs[-3:]
    start, features = before.shape[0], full.shape[0]
    stream = column_stream(weight, buf, start, features, sems)
    multiply = weight_rows_product(left, right, buf)

    def product(at, size):
        stream.take()
        return multiply(at, size)

    def finish(at, size, value):
        full[pl.ds(start + at, size), :] = value.T

    full[:start, :] = before[...]
    pipelined(features - start, product, finish)
    count = len(outs) // 2
    write_blocks(order, full, outs[:count], outs[count:])


def contract_last(order, left, right, weight, before, blocks, name):
    hidden, features = weight.shape[1:]
    tokens, start = left.shape[0], before.shape[0]
    rows, part, count = features // blocks, features - before.shape[0], blocks // 2
    outs = pl.pallas_call(
        contract_last_kernel,
        out_shape=[struct((rows, tokens), BF16)] * count + [struct((rows, tokens), F32)] * count,
        in_specs=[SCALARS, WHOLE, WHOLE, HELD, WHOLE],
        out_specs=[WHOLE] * blocks,
        scratch_shapes=[
            pltpu.VMEM((hidden, part), BF16),
            pltpu.VMEM((features, tokens), F32),
            pltpu.SemaphoreType.DMA((len(pieces(start, features)),)),
        ],
        name=name,
        **params(2 * hidden * part * tokens, 2 * hidden * part + 2 * hidden * tokens + 8 * features * tokens),
    )(order, left, right, weight, before)
    return outs[:count], outs[count:]


def spread_first_kernel(blocks, order, *refs):
    own, other, far, (mod, slope, weight, grad, turned, buf, stage, sems) = (
        refs[:blocks], refs[blocks : 2 * blocks], refs[2 * blocks : 3 * blocks], refs[3 * blocks :]
    )
    part = slope.shape[0]
    stream = row_stream(weight, buf, 0, part, sems)
    rows, half = own[0].shape
    group = order[blocks]
    control = group == 0

    def scaled(value, place, first):
        at = pl.ds(pl.multiple_of(order[first + place] * rows, 8), rows)
        return (value.astype(F32) * jnp.where(control, 1.0, mod[at, 2:3])).astype(BF16)

    def mine(place):
        return scaled(jnp.where(control, own[place][...], other[place][...]), place, 0)

    def theirs(place):
        return scaled(far[place][...], place, blocks + 1)

    for owner, make, first in ((group, mine, 0), (1 - group, theirs, blocks + 1)):
        lanes = pl.ds(pl.multiple_of(owner * half, half), half)
        values = [functools.partial(make, place) for place in range(blocks)]
        place_blocks(grad, lanes, stage, order, values, rows, first)
    spread_products(stream, buf, grad, slope, turned)


def spread_products(stream, buf, grad, slope, turned):
    def product(at, size):
        stream.take()
        return jnp.dot(buf[pl.ds(at, size), :], grad[...], preferred_element_type=F32)

    def finish(at, size, value):
        turned[:, pl.ds(at, size)] = (value * slope[pl.ds(at, size), :]).T.astype(BF16)

    pipelined(slope.shape[0], product, finish)


def spread_first(order, own, other, far, mod, slope, weight, name):
    hidden, features = weight.shape[1:]
    part, tokens = slope.shape
    blocks = len(own)
    return pl.pallas_call(
        functools.partial(spread_first_kernel, blocks),
        out_shape=(struct((features, tokens), BF16), struct((tokens, part), BF16)),
        in_specs=[SCALARS] + [WHOLE] * (3 * blocks + 2) + [HELD],
        out_specs=(WHOLE, WHOLE),
        scratch_shapes=[
            pltpu.VMEM((part, features), BF16),
            staging(own[0].shape[0], features, own[0].shape[1]),
            pltpu.SemaphoreType.DMA((len(pieces(0, part)),)),
        ],
        name=name,
        **params(2 * part * features * tokens, 2 * part * features + 6 * part * tokens + 4 * features * tokens),
    )(order, *own, *other, *far, mod, slope, weight)


def spread_rest_kernel(start, grad, slope, weight, turned, buf, sems):
    stream = row_stream(weight, buf, start, start + slope.shape[0], sems)
    spread_products(stream, buf, grad, slope, turned)


def spread_rest(grad, slope, weight, start, name):
    hidden, features = weight.shape[1:]
    part, tokens = slope.shape
    return pl.pallas_call(
        functools.partial(spread_rest_kernel, start),
        out_shape=struct((tokens, part), BF16),
        in_specs=[WHOLE, WHOLE, HELD],
        out_specs=WHOLE,
        scratch_shapes=[pltpu.VMEM((part, features), BF16), pltpu.SemaphoreType.DMA((len(pieces(start, hidden)),))],
        name=name,
        **params(2 * part * features * tokens, 2 * part * features + 6 * part * tokens + 2 * features * tokens),
    )(grad, slope, weight)


def norm_products(stream, start, stop, left, right, acts, stats, mod, buf, full, base, sums):
    mean, inv = stats[0:1, :], stats[1:2, :]
    multiply = weight_rows_product(left, right, buf)

    def product(at, size):
        stream.take()
        return multiply(at, size)

    def finish(at, size, value):
        rows = pl.ds(start + at, size)
        value = value.T
        full[pl.ds(base + at, size), :] = value
        scaled = value * (1.0 + mod[rows, 1:2])
        xhat = (acts[0, rows, :].astype(F32) - mean) * inv
        sums[0] += jnp.sum(scaled, 0, keepdims=True)
        sums[1] += jnp.sum(scaled * xhat, 0, keepdims=True)

    pipelined(stop - start, product, finish)


def norm_first_kernel(left, right, acts, stats, mod, weight, full, sums_out, buf, sems):
    stop, tokens = full.shape
    stream = column_stream(weight, buf, 0, stop, sems)
    sums = [jnp.zeros((1, tokens), F32), jnp.zeros((1, tokens), F32)]
    norm_products(stream, 0, stop, left, right, acts, stats, mod, buf, full, 0, sums)
    sums_out[0:1, :] = sums[0]
    sums_out[1:2, :] = sums[1]


def norm_first(left, right, acts, stats, mod, weight, stop, name):
    hidden, features = weight.shape[1:]
    tokens = left.shape[0]
    return pl.pallas_call(
        norm_first_kernel,
        out_shape=(struct((stop, tokens), F32), struct((2, tokens), F32)),
        in_specs=[WHOLE] * 5 + [HELD],
        out_specs=(WHOLE, WHOLE),
        scratch_shapes=[pltpu.VMEM((hidden, stop), BF16), pltpu.SemaphoreType.DMA((len(pieces(0, stop)),))],
        name=name,
        **params(2 * hidden * stop * tokens, 2 * hidden * stop + 2 * hidden * tokens + 6 * stop * tokens),
    )(left, right, acts, stats, mod, weight)


def norm_last_kernel(rows, order, left, right, acts, stats, mod, weight, before, sums_before, *refs):
    outs, (sums_out, buf, full, sems) = refs[:-4], refs[-4:]
    start, (features, tokens) = before.shape[0], full.shape
    stream = column_stream(weight, buf, start, features, sems)
    sums = [sums_before[0:1, :], sums_before[1:2, :]]
    full[:start, :] = before[...]
    norm_products(stream, start, features, left, right, acts, stats, mod, buf, full, start, sums)
    count = len(outs) // 2
    padded = outs[0].shape[0] - 16
    tail = pack_sums(*sums)
    for place in range(count):
        offset = pl.multiple_of(order[2 * place] * rows, 8)
        outs[count + place][...] = full[pl.ds(offset, rows), :]
        offset = pl.multiple_of(order[2 * place + 1] * rows, 8)
        block = full[pl.ds(offset, rows), :]
        if padded > rows:
            block = jnp.concatenate([block, jnp.zeros((padded - rows, tokens), F32)], 0)
        outs[place][:padded, :] = block.astype(BF16)
        outs[place][padded:, :] = tail
    sums_out[0:1, :] = sums[0]
    sums_out[1:2, :] = sums[1]


def norm_last(order, left, right, acts, stats, mod, weight, before, sums, blocks, name):
    hidden, features = weight.shape[1:]
    tokens, start = left.shape[0], before.shape[0]
    rows, part, count = features // blocks, features - before.shape[0], blocks // 2
    outs = pl.pallas_call(
        functools.partial(norm_last_kernel, rows),
        out_shape=[struct((-(-rows // 16) * 16 + 16, tokens), BF16)] * count
        + [struct((rows, tokens), F32)] * count
        + [struct((2, tokens), F32)],
        in_specs=[SCALARS] + [WHOLE] * 5 + [HELD] + [WHOLE] * 2,
        out_specs=[WHOLE] * (blocks + 1),
        scratch_shapes=[
            pltpu.VMEM((hidden, part), BF16),
            pltpu.VMEM((features, tokens), F32),
            pltpu.SemaphoreType.DMA((len(pieces(start, features)),)),
        ],
        name=name,
        **params(2 * hidden * part * tokens, 2 * hidden * part + 2 * hidden * tokens + 8 * features * tokens),
    )(order, left, right, acts, stats, mod, weight, before, sums)
    return outs[:count], outs[count:-1], outs[-1]


def fold_kernel(rows, count, *refs):
    got, kept, (sums, *outs) = refs[:count], refs[count : 2 * count], refs[2 * count :]
    more = unpack_sums(got[0][-16:, :])
    plain, along = sums[0:1, :] + more[0], sums[1:2, :] + more[1]
    tail = pack_sums(plain, along)
    padded = got[0].shape[0] - 16
    for place in range(count // 2):
        even, odd = 2 * place, 2 * place + 1
        outs[count // 2 + place][...] = kept[even][...] + got[even][:rows, :].astype(F32)
        block = kept[odd][...] + got[odd][:rows, :].astype(F32)
        if padded > rows:
            block = jnp.concatenate([block, jnp.zeros((padded - rows, block.shape[1]), F32)], 0)
        outs[place][:padded, :] = block.astype(BF16)
        outs[place][padded:, :] = tail
    outs[-1][0:1, :] = plain
    outs[-1][1:2, :] = along


def fold(got, kept, sums):
    count, (rows, tokens) = len(kept), kept[0].shape
    outs = pl.pallas_call(
        functools.partial(fold_kernel, rows, count),
        out_shape=[struct(got[0].shape, BF16)] * (count // 2)
        + [struct((rows, tokens), F32)] * (count // 2)
        + [struct((2, tokens), F32)],
        in_specs=[WHOLE] * (2 * count + 1),
        out_specs=[WHOLE] * (count + 1),
        name="fold",
        **params(2 * count * rows * tokens, 8 * count * rows * tokens, grant=12),
    )(*got, *kept, sums)
    return outs[: count // 2], outs[count // 2 : -1], outs[-1]


def upstream_kernel(blocks, order, weight, own, arrived, *refs):
    outs, (cot0, cot1, cot1_rows, full) = refs[:-4], refs[-4:]
    group = order[blocks]
    control = group == 0
    half = cot0.shape[1]
    lanes = pl.ds(pl.multiple_of(group * half, half), half)
    cot0[...] = jnp.where(control, own[:, lanes], arrived[:, lanes])
    mine = jnp.where(control, arrived[:, lanes], own[:, lanes])
    cot1[...] = mine
    cot1_rows[...] = jnp.where(control, arrived[...], own[...])
    full[...] = lax.dot_general(mine, weight[...], (((0,), (0,)), ((), ())), preferred_element_type=F32).T
    count = blocks // 2
    write_blocks(order, full, outs[:count], outs[count:])


def upstream_terms(order, weight, own, arrived, blocks):
    rows, tokens = own.shape
    half, count = tokens // 2, blocks // 2
    outs = pl.pallas_call(
        functools.partial(upstream_kernel, blocks),
        out_shape=[struct((rows, half), BF16)] * count
        + [struct((rows, half), F32)] * count
        + [struct((rows, half), BF16)] * 2
        + [struct((rows, tokens), BF16)],
        in_specs=[SCALARS] + [WHOLE] * 3,
        out_specs=[WHOLE] * (blocks + 3),
        scratch_shapes=[pltpu.VMEM((weight.shape[1], half), F32)],
        name="upstream_terms",
        **params(2 * weight.size * half, 2 * weight.size + 4 * blocks * rows * half, grant=12),
    )(order, weight, own, arrived)
    return outs[:count], outs[count:blocks], *outs[blocks:]


def residual_kernel(order, weight, *refs):
    stack, (result, full, stage) = refs[:-3], refs[-3:]
    values = [lambda value=value: value[...] for value in stack]
    place_blocks(full, slice(None), stage, order, values, stack[0].shape[0])
    result[...] = jnp.dot(weight[...], full[...], preferred_element_type=F32)


def residual_rows(order, weight, stack):
    blocks, (rows, half) = len(stack), stack[0].shape
    return pl.pallas_call(
        residual_kernel,
        out_shape=struct((rows, half), F32),
        in_specs=[SCALARS] + [WHOLE] * (blocks + 1),
        out_specs=WHOLE,
        scratch_shapes=[pltpu.VMEM((blocks * rows, half), BF16), staging(rows, blocks * rows, half)],
        name="residual_rows",
        **params(2 * weight.size * half, 2 * weight.size + 4 * blocks * rows * half, grant=12),
    )(order, weight, *stack)


def zero_grad_kernel(blocks, parts, order, dp_order, *refs):
    cots, stacks, (out, lhs, rhs, stage, buf, sems) = refs[:parts], refs[parts:-6], refs[-6:]
    near, near_other, far, far_other = (stacks[k * blocks : (k + 1) * blocks] for k in range(4))
    rows, half = near[0].shape
    group = order[blocks]
    for part in range(parts):
        lhs[:, pl.ds(pl.multiple_of(dp_order[part] * 2 * half, 2 * half), 2 * half)] = cots[part][...]
        for side, sources in enumerate((near, near_other) if part == 0 else (far, far_other)):
            at = Ellipsis if part == 0 else part - 1
            values = [lambda source=source, at=at: source[at] for source in sources]
            owner = group if side == 0 else 1 - group
            lanes = pl.ds(pl.multiple_of((dp_order[part] * 2 + owner) * half, half), half)
            place_blocks(rhs, lanes, stage, order, values, rows, side * (blocks + 1))
    copies = []
    for k, (start, size) in enumerate(pieces(0, blocks * rows, CHUNK * WIDE)):
        columns = pl.ds(start, size)
        buf[:, columns] = lax.dot_general(
            lhs[...], rhs[columns, :], (((1,), (1,)), ((), ())), preferred_element_type=F32
        )
        copies.append(pltpu.make_async_copy(buf.at[:, columns], out.at[:, columns], sems.at[k]))
        copies[-1].start()
    for copy in copies:
        copy.wait()


def zero_projection_grad(order, dp_order, cots, near, near_other, far, far_other):
    blocks, (rows, half) = len(near), near[0].shape
    parts = len(cots)
    features, tokens = blocks * rows, parts * 2 * half

    return pl.pallas_call(
        functools.partial(zero_grad_kernel, blocks, parts),
        out_shape=struct((rows, features), F32),
        in_specs=[SCALARS] * 2 + [WHOLE] * (parts + 4 * blocks),
        out_specs=HELD,
        scratch_shapes=[
            pltpu.VMEM((rows, tokens), BF16),
            pltpu.VMEM((features, tokens), BF16),
            staging(rows, features, half),
            pltpu.VMEM((rows, features), F32),
            pltpu.SemaphoreType.DMA((len(pieces(0, features, CHUNK * WIDE)),)),
        ],
        name="zero_projection_grad",
        **params(2 * tokens * rows * features, 4 * rows * features + 2 * tokens * (rows + features), grant=28),
    )(order, dp_order, *cots, *near, *near_other, *far, *far_other)


def steps(values, level, *during):
    got = [step(value, level) for value in values]
    return list(lax.optimization_barrier((tuple(got),) + during)[0]) if during else got


def local(acts, modulation, w_in, w_out, zero_weight, cotangent):
    own_cot = cotangent[0]
    features, tokens = acts.shape[1:]
    hidden = w_in.shape[1]
    rows = own_cot.shape[0]
    half = tokens // 2
    blocks, levels = lax.axis_size("fsdp"), stages()
    parts = lax.axis_size("dp")
    group = lax.axis_index("grp").astype(jnp.int32)
    me = lax.axis_index("fsdp").astype(jnp.int32)
    is_control = group == 0
    places = block_order(group, me)
    order = jnp.concatenate([places, group[None], block_order(1 - group, me)])
    dp_order = lax.axis_index("dp").astype(jnp.int32) ^ jnp.arange(parts, dtype=jnp.int32)
    mod = modulation[0].T
    own_mod = block_of(mod, me, rows)
    own_gate = own_mod[:, 2:3]

    arrived = swap_grp(own_cot)
    gate0 = jnp.where(is_control, modulation[0, 2], swap_grp(modulation[0, 2]))
    own_gate0 = lax.dynamic_slice_in_dim(gate0, me * rows, rows, 0)[:, None]
    split, cut = middle(hidden), middle(features)
    normed, stats, turned_a, slope_a = expand_first(acts, mod, w_in, split, "expand_first")
    arrived = after(arrived, turned_a)

    sent, kept, cot0, cot1, cot1_rows = upstream_terms(order, zero_weight, own_cot, arrived, blocks)
    cots = gather_dp(cot1_rows)
    cot_stack, done = [cot1], ()
    for level in range(levels):
        if level == 0:
            turned_b, slope_b = expand_rest(after(normed, *sent), w_in, split, "expand_rest")
            done = (turned_b,)
        elif level == 1:
            branch = contract_first(after(turned_a, *sent), turned_b, w_out, cut, "contract_first")
            done = (branch,)
        count = len(kept)
        got = steps(list(sent) + cot_stack, level, *done)
        kept = [a + b.astype(F32) for a, b in zip(kept, got)]
        cot_stack = cot_stack + got[count:]
        if level + 1 < levels:
            sent, kept = [value.astype(BF16) for value in kept[1::2]], kept[0::2]
    up_half = kept[0] + cot0.astype(F32)
    gated = [(own_gate0 * up_half).astype(BF16)]

    sent, kept = contract_last(order, after(turned_a, *gated), turned_b, w_out, branch, blocks, "contract_last")
    for level in range(levels):
        gated = gated + (steps(gated, level, sent[0]) if level == 0 else steps(gated, level))
    crossed = [swap_grp(jnp.where(is_control, a, b)) for a, b in zip(cot_stack, gated)]
    up_rows = jnp.where(is_control, jnp.concatenate([up_half, swap_grp(up_half)], 1), own_cot.astype(F32))

    pre_grads = []
    for level in range(levels):
        if level == 0:
            grad, turned = spread_first(
                order, gated, cot_stack, crossed, mod, after(slope_a, *sent, *cots), w_out, "spread_first"
            )
            pre_grads.append(turned)
        elif level == 1:
            pre_grads.append(spread_rest(grad, after(slope_b, *sent), w_out, split, "spread_rest"))
        got = steps(sent, level, pre_grads[-1])
        kept = [a + b.astype(F32) for a, b in zip(kept, got)]
        if level + 1 < levels:
            sent, kept = [value.astype(BF16) for value in kept[1::2]], kept[0::2]
    own_values = block_of(acts[0], me, rows).astype(F32)
    sums = own_values + own_gate * kept[0]
    out_rows = sums.astype(BF16)

    out_half = jnp.where(is_control, out_rows[:, :half], swap_grp(out_rows[:, half:]))
    far = gather_dp(out_half)[1:]
    near = [out_half]
    for level in range(levels):
        tied = after(pre_grads[0], *near)
        if level == 0:
            norm, token_sums = norm_first(tied, pre_grads[1], acts, stats, mod, w_in, cut, "norm_first")
            done = norm
        elif level == 1:
            sent, kept, token_sums = norm_last(
                order, tied, pre_grads[1], acts, stats, mod, w_in, norm, token_sums, blocks, "norm_last"
            )
            done = sent[0]
        near = near + steps(near, level, done)
    near_other = [swap_grp(value) for value in near]
    residual = residual_rows(order, zero_weight, after(near, sent[0]))
    far = [jnp.stack(after(far, residual))]

    for level in range(levels):
        got = steps(sent, level)
        far = far + steps(far, level)
        if level + 1 < levels:
            sent, kept, token_sums = fold(got, kept, token_sums)
    more = unpack_sums(got[0][-16:])
    plain, along = token_sums[0:1] + more[0], token_sums[1:2] + more[1]
    kept = [kept[0] + got[0][:rows].astype(F32)]
    mean, inv = stats[0:1], stats[1:2]
    back = inv * (
        kept[0] * (1.0 + own_mod[:, 1:2]) - plain / features - (own_values - mean) * inv * (along / features)
    )
    residual = jnp.concatenate([swap_grp(residual), residual], 1)
    block_rows = jnp.where(is_control, out_rows, (sums + residual).astype(BF16))

    far_other = [swap_grp(value) for value in far]
    zero_grad = zero_projection_grad(order, dp_order, cots, near, near_other, far, far_other)
    return (block_rows[None], (up_rows + back)[None], zero_grad)


def solution(mesh):
    placed = (
        P("grp", None, "dp"),
        P("grp", None, None),
        P("grp", "fsdp", None),
        P("grp", "fsdp", None),
        P("fsdp", None),
        P("grp", "fsdp", "dp"),
    )
    return jax.shard_map(
        local,
        mesh=mesh,
        in_specs=placed,
        out_specs=(P("grp", "fsdp", "dp"), P("grp", "fsdp", "dp"), P("fsdp", None)),
        check_vma=False,
    )
```

```python
import functools

import jax
import jax.numpy as jnp
from jax import lax
from jax.experimental import pallas as pl
from jax.experimental.pallas import tpu as pltpu
from jax.sharding import PartitionSpec as P

EPSILON = 1e-06
SQRT_2_OVER_PI = 0.7978845608028654
CHUNK = 512
AHEAD = 3
MIB = 1024 * 1024
F32, BF16 = jnp.float32, jnp.bfloat16
WHOLE = pl.BlockSpec(memory_space=pltpu.VMEM)
HELD = pl.BlockSpec(memory_space=pltpu.HBM)
SCALARS = pl.BlockSpec(memory_space=pltpu.SMEM)


def pieces(start, stop, size=CHUNK):
    return [(at, min(size, stop - at)) for at in range(start, stop, size)]


def split_rows(hidden):
    units = hidden // CHUNK
    return CHUNK * max(units // 2, 1), CHUNK * max(units - 1, 1)


def after(value, *others):
    return lax.optimization_barrier((value,) + others)[0]


def swap_grp(value):
    return lax.ppermute(value, "grp", [(0, 1), (1, 0)])


def stages():
    return (lax.axis_size("fsdp") - 1).bit_length()


def step(value, stage):
    length, bits = lax.axis_size("fsdp"), stages()
    pairs = []
    for group, bit in ((0, stage), (1, bits - 1 - stage)):
        pairs += [(group * length + i, group * length + (i ^ (1 << bit))) for i in range(length)]
    return lax.ppermute(value, ("grp", "fsdp"), pairs)


def block_order(group, me):
    length, bits = lax.axis_size("fsdp"), stages()
    turned = [sum(((v >> b) & 1) << (bits - 1 - b) for b in range(bits)) for v in range(length)]
    up, down = jnp.arange(length, dtype=jnp.int32), jnp.array(turned, jnp.int32)
    return me ^ jnp.where(group == 0, up, down)


def send(value, place):
    length, bits = lax.axis_size("fsdp"), stages()
    turned = sum(((place >> b) & 1) << (bits - 1 - b) for b in range(bits))
    pairs = []
    for group, mask in ((0, place), (1, turned)):
        pairs += [(group * length + i, group * length + (i ^ mask)) for i in range(length)]
    return lax.ppermute(value, ("grp", "fsdp"), pairs)


def gather_dp(value):
    length = lax.axis_size("dp")
    return [value] + [
        lax.ppermute(value, "dp", [(i, i ^ mask) for i in range(length)]) for mask in range(1, length)
    ]


def block_of(value, index, rows):
    return lax.dynamic_slice_in_dim(value, index * rows, rows, 0)


def split_three(value):
    high = value.astype(BF16)
    rest = value - high.astype(F32)
    mid = rest.astype(BF16)
    return high, mid, (rest - mid.astype(F32)).astype(BF16)


def pack_sums(plain, along):
    tail = [part.astype(F32) for part in split_three(plain) + split_three(along)]
    return jnp.concatenate(tail + [jnp.zeros((10, plain.shape[1]), F32)], 0).astype(BF16)


def unpack_sums(tail):
    tail = tail.astype(F32)
    return tail[0:1] + tail[1:2] + tail[2:3], tail[3:4] + tail[4:5] + tail[5:6]


def gelu_and_slope(v):
    square = v * v
    t = jnp.tanh(SQRT_2_OVER_PI * (v + 0.044715 * (square * v)))
    rise = 0.5 * (1.0 + t)
    slope = rise + 0.5 * v * (1.0 - t * t) * (SQRT_2_OVER_PI * (1.0 + (3 * 0.044715) * square))
    return v * rise, slope


class Stream:
    def __init__(self, first, first_buf, second, second_buf, parts, base, sems):
        def copy(weight, buf, part):
            return weight.at[0, pl.ds(part[0], part[1]), :], buf.at[pl.ds(part[0] - base, part[1]), :]

        pairs = [copy(first, first_buf, parts[0])]
        for k, part in enumerate(parts):
            if k + 1 < len(parts):
                pairs.append(copy(first, first_buf, parts[k + 1]))
            pairs.append(copy(second, second_buf, part))
        self.copies = [pltpu.make_async_copy(a, b, sems.at[k]) for k, (a, b) in enumerate(pairs)]
        self.next = 0
        for item in self.copies[:AHEAD]:
            item.start()

    def take(self):
        k = self.next
        self.copies[k].wait()
        if k + AHEAD < len(self.copies):
            self.copies[k + AHEAD].start()
        self.next = k + 1


def pipelined(parts, product, finish):
    held = None
    for part in parts:
        value = product(*part)
        if held is not None:
            finish(*held, False)
        held = part + (value,)
    finish(*held, True)


def params(flops, moved, transcendentals=0, grant=50):
    return dict(
        compiler_params=pltpu.CompilerParams(vmem_limit_bytes=grant * MIB),
        cost_estimate=pl.CostEstimate(flops=flops, bytes_accessed=moved, transcendentals=transcendentals),
    )


def struct(shape, dtype):
    return jax.ShapeDtypeStruct(shape, dtype)


def staging(rows, features, lanes):
    return pltpu.VMEM((features, lanes) if rows % 16 else (8, 128), F32)


def place_blocks(target, lanes, stage, order, blocks, rows, first=0):
    for place, value in enumerate(blocks):
        if rows % 16:
            stage[pl.ds(pl.multiple_of(order[first + place] * rows, 8), rows), :] = value().astype(F32)
        else:
            target[pl.ds(pl.multiple_of(order[first + place] * rows, 16), rows), lanes] = value()
    if rows % 16:
        target[:, lanes] = stage[...].astype(target.dtype)


def turn_modulation(modulation, columns):
    for start, size in pieces(0, modulation.shape[2], 128):
        rows = modulation[0, :, pl.ds(start, size)]
        columns[pl.ds(start, size), :] = jnp.concatenate([rows, jnp.zeros((5, size), F32)], 0).T


def normalize(acts, mod, normed, stats):
    features, tokens = acts.shape[1:]
    parts = pieces(0, features, 128)
    total = jnp.zeros((1, tokens), F32)
    for start, size in parts:
        total += jnp.sum(acts[0, pl.ds(start, size), :].astype(F32), 0, keepdims=True)
    mean = total / features
    total = jnp.zeros((1, tokens), F32)
    for start, size in parts:
        centred = acts[0, pl.ds(start, size), :].astype(F32) - mean
        total += jnp.sum(centred * centred, 0, keepdims=True)
    inv = lax.rsqrt(total / features + EPSILON)
    stats[0:1, :] = mean
    stats[1:2, :] = inv
    for start, size in parts:
        rows = pl.ds(start, size)
        xhat = (acts[0, rows, :].astype(F32) - mean) * inv
        normed[rows, :] = (xhat * (1.0 + mod[rows, 1:2]) + mod[rows, 0:1]).astype(BF16)


def accumulate(total, part, weight, before, finish):
    for at, size in pieces(0, weight.shape[1]):
        columns = pl.ds(at, size)
        value = jnp.dot(part, weight[:, columns], preferred_element_type=F32)
        if before is not None:
            value = value + before[:, columns]
        if finish is None:
            total[:, columns] = value
        else:
            finish(at, size, value)


def forward_products(stream, parts, base, normed, in_buf, out_buf, slope_out, total, before, last):
    state = [before]

    def product(at, size):
        stream.take()
        return jnp.dot(in_buf[pl.ds(at - base, size), :], normed[...], preferred_element_type=F32)

    def finish(at, size, pre, final):
        rows = pl.ds(at - base, size)
        hidden, slope = gelu_and_slope(pre)
        slope_out[rows, :] = slope
        stream.take()
        accumulate(total, hidden.T.astype(BF16), out_buf.at[rows, :], state[0], last if final else None)
        state[0] = total

    pipelined(parts, product, finish)


def forward_first_kernel(acts, modulation, w_in, w_out, mod, normed, stats, slope_out, total, in_buf, out_buf, sems):
    parts = pieces(0, slope_out.shape[0])
    stream = Stream(w_in, in_buf, w_out, out_buf, parts, 0, sems)
    turn_modulation(modulation, mod)
    normalize(acts, mod, normed, stats)
    forward_products(stream, parts, 0, normed, in_buf, out_buf, slope_out, total, None, None)


def forward_last_kernel(start, order, normed, before, w_in, w_out, slope_out, *refs):
    outs, (in_buf, out_buf, total, full, sems) = refs[:-5], refs[-5:]
    parts = pieces(start, start + slope_out.shape[0])
    stream = Stream(w_in, in_buf, w_out, out_buf, parts, start, sems)

    def last(at, size, value):
        full[pl.ds(at, size), :] = value.T

    forward_products(stream, parts, start, normed, in_buf, out_buf, slope_out, total, before, last)
    write_blocks(order, full, outs)


def layer_scratch(part, features):
    return [
        pltpu.VMEM((part, features), BF16),
        pltpu.VMEM((part, features), BF16),
    ]


def layer_params(part, features, tokens, transcendentals):
    return params(4 * part * features * tokens, 4 * part * features + 4 * features * tokens, transcendentals)


def forward_first(acts, modulation, w_in, w_out, part, name):
    features, tokens = acts.shape[1:]
    return pl.pallas_call(
        forward_first_kernel,
        out_shape=(
            struct((features, 8), F32),
            struct((features, tokens), BF16),
            struct((2, tokens), F32),
            struct((part, tokens), F32),
            struct((tokens, features), F32),
        ),
        in_specs=[WHOLE, WHOLE, HELD, HELD],
        out_specs=[WHOLE] * 5,
        scratch_shapes=layer_scratch(part, features) + [pltpu.SemaphoreType.DMA((2 * len(pieces(0, part)),))],
        name=name,
        **layer_params(part, features, tokens, part * tokens),
    )(acts, modulation, w_in, w_out)


def forward_last(order, normed, before, w_in, w_out, start, blocks, name):
    hidden, features = w_in.shape[1:]
    tokens, part, rows = before.shape[0], hidden - start, features // blocks
    slope, *outs = pl.pallas_call(
        functools.partial(forward_last_kernel, start),
        out_shape=[struct((part, tokens), F32), struct((rows, tokens), F32)]
        + [struct((rows, tokens), BF16)] * (blocks - 1),
        in_specs=[SCALARS, WHOLE, WHOLE, HELD, HELD],
        out_specs=[WHOLE] * (blocks + 1),
        scratch_shapes=layer_scratch(part, features)
        + [
            pltpu.VMEM((tokens, features), F32),
            pltpu.VMEM((features, tokens), F32),
            pltpu.SemaphoreType.DMA((2 * len(pieces(start, hidden)),)),
        ],
        name=name,
        **layer_params(part, features, tokens, part * tokens),
    )(order, normed, before, w_in, w_out)
    return slope, outs[0], outs[1:]


def write_blocks(order, full, outs):
    for place, target in enumerate(outs):
        rows = target.shape[0]
        offset = pl.multiple_of(order[place] * rows, 8)
        target[...] = full[pl.ds(offset, rows), :].astype(target.dtype)


def backward_products(stream, parts, base, grad, slopes, in_buf, out_buf, total, before, last):
    state = [before]

    def product(at, size):
        stream.take()
        return jnp.dot(out_buf[pl.ds(at - base, size), :], grad[...], preferred_element_type=F32)

    def finish(at, size, value, final):
        rows = pl.ds(at - base, size)
        seen = slopes[0].shape[0]
        slope = slopes[0][pl.ds(at, size), :] if at < seen else slopes[1][pl.ds(at - seen, size), :]
        stream.take()
        accumulate(total, (value * slope).T.astype(BF16), in_buf.at[rows, :], state[0], last if final else None)
        state[0] = total

    pipelined(parts, product, finish)


def backward_first_kernel(blocks, part, order, *refs):
    pieces_in, (slope_a, slope_b, w_in, w_out, grad, total, in_buf, out_buf, stage, sems) = refs[:blocks], refs[blocks:]
    parts = pieces(0, part)
    stream = Stream(w_out, out_buf, w_in, in_buf, parts, 0, sems)
    values = [lambda ref=ref: ref[...] for ref in pieces_in]
    place_blocks(grad, slice(None), stage, order, values, pieces_in[0].shape[0])
    backward_products(stream, parts, 0, grad, (slope_a, slope_b), in_buf, out_buf, total, None, None)


def backward_first(order, gathered, slope_a, slope_b, w_in, w_out, part, name):
    hidden, features = w_in.shape[1:]
    blocks, (rows, tokens) = len(gathered), gathered[0].shape
    return pl.pallas_call(
        functools.partial(backward_first_kernel, blocks, part),
        out_shape=(struct((features, tokens), BF16), struct((tokens, features), F32)),
        in_specs=[SCALARS] + [WHOLE] * (blocks + 2) + [HELD, HELD],
        out_specs=[WHOLE] * 2,
        scratch_shapes=layer_scratch(part, features)
        + [staging(rows, features, tokens), pltpu.SemaphoreType.DMA((2 * len(pieces(0, part)),))],
        name=name,
        **layer_params(part, features, tokens, 0),
    )(order, *gathered, slope_a, slope_b, w_in, w_out)


def backward_last_kernel(start, rows, order, grad, before, slope_a, slope_b, acts, stats, mod, w_in, w_out, *refs):
    outs, (sums_out, in_buf, out_buf, total, full, sems) = refs[:-6], refs[-6:]
    hidden, (features, tokens) = w_in.shape[1], full.shape
    parts = pieces(start, hidden)
    stream = Stream(w_out, out_buf, w_in, in_buf, parts, start, sems)
    mean, inv = stats[0:1, :], stats[1:2, :]
    sums = [jnp.zeros((1, tokens), F32), jnp.zeros((1, tokens), F32)]

    def last(at, size, value):
        at = pl.ds(at, size)
        value = value.T
        full[at, :] = value
        scaled = value * (1.0 + mod[at, 1:2])
        xhat = (acts[0, at, :].astype(F32) - mean) * inv
        sums[0] += jnp.sum(scaled, 0, keepdims=True)
        sums[1] += jnp.sum(scaled * xhat, 0, keepdims=True)

    backward_products(stream, parts, start, grad, (slope_a, slope_b), in_buf, out_buf, total, before, last)
    count = len(outs) // 2
    padded = outs[0].shape[0] - 16
    tail = pack_sums(*sums)
    for place in range(count):
        offset = pl.multiple_of(order[2 * place] * rows, 8)
        outs[count + place][...] = full[pl.ds(offset, rows), :]
        offset = pl.multiple_of(order[2 * place + 1] * rows, 8)
        block = full[pl.ds(offset, rows), :]
        if padded > rows:
            block = jnp.concatenate([block, jnp.zeros((padded - rows, tokens), F32)], 0)
        outs[place][:padded, :] = block.astype(BF16)
        outs[place][padded:, :] = tail
    sums_out[0:1, :] = sums[0]
    sums_out[1:2, :] = sums[1]


def backward_last(order, grad, before, slope_a, slope_b, acts, stats, mod, w_in, w_out, start, blocks, name):
    hidden, features = w_in.shape[1:]
    tokens, part, rows, count = before.shape[0], hidden - start, features // blocks, blocks // 2
    outs = pl.pallas_call(
        functools.partial(backward_last_kernel, start, rows),
        out_shape=[struct((-(-rows // 16) * 16 + 16, tokens), BF16)] * count
        + [struct((rows, tokens), F32)] * count
        + [struct((2, tokens), F32)],
        in_specs=[SCALARS] + [WHOLE] * 7 + [HELD, HELD],
        out_specs=[WHOLE] * (blocks + 1),
        scratch_shapes=layer_scratch(part, features)
        + [
            pltpu.VMEM((tokens, features), F32),
            pltpu.VMEM((features, tokens), F32),
            pltpu.SemaphoreType.DMA((2 * len(pieces(start, hidden)),)),
        ],
        name=name,
        **layer_params(part, features, tokens, 0),
    )(order, grad, before, slope_a, slope_b, acts, stats, mod, w_in, w_out)
    return outs[:count], outs[count:-1], outs[-1]


def fold_kernel(rows, count, *refs):
    got, kept, (sums, *outs) = refs[:count], refs[count : 2 * count], refs[2 * count :]
    more = unpack_sums(got[0][-16:, :])
    plain, along = sums[0:1, :] + more[0], sums[1:2, :] + more[1]
    tail = pack_sums(plain, along)
    padded = got[0].shape[0] - 16
    for place in range(count // 2):
        even, odd = 2 * place, 2 * place + 1
        outs[count // 2 + place][...] = kept[even][...] + got[even][:rows, :].astype(F32)
        block = kept[odd][...] + got[odd][:rows, :].astype(F32)
        if padded > rows:
            block = jnp.concatenate([block, jnp.zeros((padded - rows, block.shape[1]), F32)], 0)
        outs[place][:padded, :] = block.astype(BF16)
        outs[place][padded:, :] = tail
    outs[-1][0:1, :] = plain
    outs[-1][1:2, :] = along


def fold(got, kept, sums):
    count, (rows, tokens) = len(kept), kept[0].shape
    outs = pl.pallas_call(
        functools.partial(fold_kernel, rows, count),
        out_shape=[struct(got[0].shape, BF16)] * (count // 2)
        + [struct((rows, tokens), F32)] * (count // 2)
        + [struct((2, tokens), F32)],
        in_specs=[WHOLE] * (2 * count + 1),
        out_specs=[WHOLE] * (count + 1),
        name="fold",
        **params(2 * count * rows * tokens, 8 * count * rows * tokens, grant=12),
    )(*got, *kept, sums)
    return outs[: count // 2], outs[count // 2 : -1], outs[-1]


def upstream_kernel(blocks, order, weight, own, arrived, *refs):
    outs, (cot0, cot1_rows, full) = refs[:-3], refs[-3:]
    group = order[blocks]
    control = group == 0
    half = cot0.shape[1]
    lanes = pl.ds(pl.multiple_of(group * half, half), half)
    cot0[...] = jnp.where(control, own[:, lanes], arrived[:, lanes])
    mine = jnp.where(control, arrived[:, lanes], own[:, lanes])
    cot1_rows[...] = jnp.where(control, arrived[...], own[...])
    full[...] = lax.dot_general(mine, weight[...], (((0,), (0,)), ((), ())), preferred_element_type=F32).T
    write_blocks(order, full, outs)


def upstream_terms(order, weight, own, arrived, blocks):
    rows, tokens = own.shape
    half = tokens // 2
    outs = pl.pallas_call(
        functools.partial(upstream_kernel, blocks),
        out_shape=[struct((rows, half), F32)]
        + [struct((rows, half), BF16)] * blocks
        + [struct((rows, tokens), BF16)],
        in_specs=[SCALARS] + [WHOLE] * 3,
        out_specs=[WHOLE] * (blocks + 2),
        scratch_shapes=[pltpu.VMEM((weight.shape[1], half), F32)],
        name="upstream_terms",
        **params(2 * weight.size * half, 2 * weight.size + 4 * blocks * rows * half, grant=12),
    )(order, weight, own, arrived)
    return outs[0], outs[1:blocks], *outs[blocks:]


def residual_kernel(order, weight, *refs):
    stack, (result, full, stage) = refs[:-3], refs[-3:]
    values = [lambda value=value: value[...] for value in stack]
    place_blocks(full, slice(None), stage, order, values, stack[0].shape[0])
    result[...] = jnp.dot(weight[...], full[...], preferred_element_type=F32)


def residual_rows(order, weight, stack):
    blocks, (rows, half) = len(stack), stack[0].shape
    return pl.pallas_call(
        residual_kernel,
        out_shape=struct((rows, half), F32),
        in_specs=[SCALARS] + [WHOLE] * (blocks + 1),
        out_specs=WHOLE,
        scratch_shapes=[pltpu.VMEM((blocks * rows, half), BF16), staging(rows, blocks * rows, half)],
        name="residual_rows",
        **params(2 * weight.size * half, 2 * weight.size + 4 * blocks * rows * half, grant=12),
    )(order, weight, *stack)


def zero_grad_kernel(blocks, parts, order, dp_order, *refs):
    cots, stacks, (out, lhs, rhs, stage, buf, sems) = refs[:parts], refs[parts:-6], refs[-6:]
    near, near_other, far, far_other = (stacks[k * blocks : (k + 1) * blocks] for k in range(4))
    rows, half = near[0].shape
    group = order[blocks]
    for part in range(parts):
        lhs[:, pl.ds(pl.multiple_of(dp_order[part] * 2 * half, 2 * half), 2 * half)] = cots[part][...]
        for side, sources in enumerate((near, near_other) if part == 0 else (far, far_other)):
            at = Ellipsis if part == 0 else part - 1
            values = [lambda source=source, at=at: source[at] for source in sources]
            owner = group if side == 0 else 1 - group
            lanes = pl.ds(pl.multiple_of((dp_order[part] * 2 + owner) * half, half), half)
            place_blocks(rhs, lanes, stage, order, values, rows, side * (blocks + 1))
    copies = []
    for k, (start, size) in enumerate(pieces(0, blocks * rows, CHUNK)):
        columns = pl.ds(start, size)
        buf[:, columns] = lax.dot_general(
            lhs[...], rhs[columns, :], (((1,), (1,)), ((), ())), preferred_element_type=F32
        )
        copies.append(pltpu.make_async_copy(buf.at[:, columns], out.at[:, columns], sems.at[k]))
        copies[-1].start()
    for copy in copies:
        copy.wait()


def zero_projection_grad(order, dp_order, cots, near, near_other, far, far_other):
    blocks, (rows, half) = len(near), near[0].shape
    parts = len(cots)
    features, tokens = blocks * rows, parts * 2 * half

    return pl.pallas_call(
        functools.partial(zero_grad_kernel, blocks, parts),
        out_shape=struct((rows, features), F32),
        in_specs=[SCALARS] * 2 + [WHOLE] * (parts + 4 * blocks),
        out_specs=HELD,
        scratch_shapes=[
            pltpu.VMEM((rows, tokens), BF16),
            pltpu.VMEM((features, tokens), BF16),
            staging(rows, features, half),
            pltpu.VMEM((rows, features), F32),
            pltpu.SemaphoreType.DMA((len(pieces(0, features, CHUNK)),)),
        ],
        name="zero_projection_grad",
        **params(2 * tokens * rows * features, 4 * rows * features + 2 * tokens * (rows + features), grant=28),
    )(order, dp_order, *cots, *near, *near_other, *far, *far_other)


def steps(values, level, *during):
    got = [step(value, level) for value in values]
    return list(lax.optimization_barrier((tuple(got),) + during)[0]) if during else got


def direct(values, *during):
    got = [send(value, place + 1) for place, value in enumerate(values)]
    return list(lax.optimization_barrier((tuple(got),) + during)[0])


def local(acts, modulation, w_in, w_out, zero_weight, cotangent):
    own_cot = cotangent[0]
    features, tokens = acts.shape[1:]
    hidden = w_in.shape[1]
    rows = own_cot.shape[0]
    half = tokens // 2
    blocks, levels = lax.axis_size("fsdp"), stages()
    parts = lax.axis_size("dp")
    group = lax.axis_index("grp").astype(jnp.int32)
    me = lax.axis_index("fsdp").astype(jnp.int32)
    is_control = group == 0
    places = block_order(group, me)
    order = jnp.concatenate([places, group[None], block_order(1 - group, me)])
    dp_order = lax.axis_index("dp").astype(jnp.int32) ^ jnp.arange(parts, dtype=jnp.int32)

    arrived = swap_grp(own_cot)
    own_term, sent, cot0, cot1_rows = upstream_terms(order, zero_weight, own_cot, arrived, blocks)
    split, cut = split_rows(hidden)
    mod, normed, stats, slope_a, total = forward_first(
        after(acts, *sent), modulation, w_in, w_out, split, "forward_first"
    )
    own_mod = block_of(mod, me, rows)
    own_gate = own_mod[:, 2:3]
    got = direct(sent, total)
    up_half = own_term + cot0.astype(F32) + sum(value.astype(F32) for value in got)
    up_rows = jnp.where(is_control, jnp.concatenate([up_half, swap_grp(up_half)], 1), own_cot.astype(F32))
    grad_rows = (own_gate * up_rows).astype(BF16)

    slope_b, kept, sent = forward_last(
        order, after(normed, grad_rows), total, w_in, w_out, split, blocks, "forward_last"
    )
    gathered = [grad_rows] + direct([grad_rows] * (blocks - 1), kept)
    cots = gather_dp(cot1_rows)
    grad, total = backward_first(
        order, after(gathered, *sent), slope_a, slope_b, w_in, w_out, cut, "backward_first"
    )
    got = direct(sent, total)
    own_values = block_of(acts[0], me, rows).astype(F32)
    sums = own_values + own_gate * (kept + sum(value.astype(F32) for value in got))
    out_rows = sums.astype(BF16)

    out_half = jnp.where(is_control, out_rows[:, :half], swap_grp(out_rows[:, half:]))
    far = gather_dp(out_half)[1:]
    sent, kept, token_sums = backward_last(
        order, after(grad, out_half, *cots), total, slope_a, slope_b, acts, stats, mod, w_in, w_out, cut, blocks, "backward_last"
    )
    near = [after(out_half, sent[0])]
    for level in range(levels):
        near = near + steps(near, level)
    near_other = [swap_grp(value) for value in near]
    residual = residual_rows(order, zero_weight, near)
    far = [jnp.stack(far)]

    for level in range(levels):
        got = steps(sent, level)
        far = far + steps(far, level)
        if level + 1 < levels:
            sent, kept, token_sums = fold(got, kept, token_sums)
    more = unpack_sums(got[0][-16:])
    plain, along = token_sums[0:1] + more[0], token_sums[1:2] + more[1]
    kept = [kept[0] + got[0][:rows].astype(F32)]
    mean, inv = stats[0:1], stats[1:2]
    back = inv * (
        kept[0] * (1.0 + own_mod[:, 1:2]) - plain / features - (own_values - mean) * inv * (along / features)
    )
    residual = jnp.concatenate([swap_grp(residual), residual], 1)
    block_rows = jnp.where(is_control, out_rows, (sums + residual).astype(BF16))

    far_other = [swap_grp(value) for value in far]
    zero_grad = zero_projection_grad(order, dp_order, cots, near, near_other, far, far_other)
    return (block_rows[None], (up_rows + back)[None], zero_grad)


def solution(mesh):
    placed = (
        P("grp", None, "dp"),
        P("grp", None, None),
        P("grp", "fsdp", None),
        P("grp", "fsdp", None),
        P("fsdp", None),
        P("grp", "fsdp", "dp"),
    )
    return jax.shard_map(
        local,
        mesh=mesh,
        in_specs=placed,
        out_specs=(P("grp", "fsdp", "dp"), P("grp", "fsdp", "dp"), P("fsdp", None)),
        check_vma=False,
    )
```

```python
import functools

import jax
import jax.numpy as jnp
from jax import lax
from jax.experimental import pallas as pl
from jax.experimental.pallas import tpu as pltpu
from jax.sharding import PartitionSpec as P

EPSILON = 1e-06
SQRT_2_OVER_PI = 0.7978845608028654
CHUNK = 512
AHEAD = 3
MIB = 1024 * 1024
F32, BF16 = jnp.float32, jnp.bfloat16
WHOLE = pl.BlockSpec(memory_space=pltpu.VMEM)
HELD = pl.BlockSpec(memory_space=pltpu.HBM)
SCALARS = pl.BlockSpec(memory_space=pltpu.SMEM)


def pieces(start, stop, size=CHUNK):
    return [(at, min(size, stop - at)) for at in range(start, stop, size)]


def split_rows(hidden):
    units = hidden // CHUNK
    return CHUNK * max(units // 2, 1), CHUNK * max(units - 1, 1)


def after(value, *others):
    return lax.optimization_barrier((value,) + others)[0]


def swap_grp(value):
    return lax.ppermute(value, "grp", [(0, 1), (1, 0)])


def stages():
    return (lax.axis_size("fsdp") - 1).bit_length()


def step(value, stage):
    length, bits = lax.axis_size("fsdp"), stages()
    pairs = []
    for group, bit in ((0, stage), (1, bits - 1 - stage)):
        pairs += [(group * length + i, group * length + (i ^ (1 << bit))) for i in range(length)]
    return lax.ppermute(value, ("grp", "fsdp"), pairs)


def block_order(group, me):
    length, bits = lax.axis_size("fsdp"), stages()
    turned = [sum(((v >> b) & 1) << (bits - 1 - b) for b in range(bits)) for v in range(length)]
    up, down = jnp.arange(length, dtype=jnp.int32), jnp.array(turned, jnp.int32)
    return me ^ jnp.where(group == 0, up, down)


def send(value, place):
    length, bits = lax.axis_size("fsdp"), stages()
    turned = sum(((place >> b) & 1) << (bits - 1 - b) for b in range(bits))
    pairs = []
    for group, mask in ((0, place), (1, turned)):
        pairs += [(group * length + i, group * length + (i ^ mask)) for i in range(length)]
    return lax.ppermute(value, ("grp", "fsdp"), pairs)


def gather_dp(value):
    length = lax.axis_size("dp")
    return [value] + [
        lax.ppermute(value, "dp", [(i, i ^ mask) for i in range(length)]) for mask in range(1, length)
    ]


def block_of(value, index, rows):
    return lax.dynamic_slice_in_dim(value, index * rows, rows, 0)


def split_three(value):
    high = value.astype(BF16)
    rest = value - high.astype(F32)
    mid = rest.astype(BF16)
    return high, mid, (rest - mid.astype(F32)).astype(BF16)


def pack_sums(plain, along):
    tail = [part.astype(F32) for part in split_three(plain) + split_three(along)]
    return jnp.concatenate(tail + [jnp.zeros((10, plain.shape[1]), F32)], 0).astype(BF16)


def unpack_sums(tail):
    tail = tail.astype(F32)
    return tail[0:1] + tail[1:2] + tail[2:3], tail[3:4] + tail[4:5] + tail[5:6]


def gelu_and_slope(v):
    square = v * v
    t = jnp.tanh(SQRT_2_OVER_PI * (v + 0.044715 * (square * v)))
    rise = 0.5 * (1.0 + t)
    slope = rise + 0.5 * v * (1.0 - t * t) * (SQRT_2_OVER_PI * (1.0 + (3 * 0.044715) * square))
    return v * rise, slope


class Stream:
    def __init__(self, first, first_buf, second, second_buf, parts, base, sems):
        def copy(weight, buf, part):
            return weight.at[0, pl.ds(part[0], part[1]), :], buf.at[pl.ds(part[0] - base, part[1]), :]

        pairs = [copy(first, first_buf, parts[0])]
        for k, part in enumerate(parts):
            if k + 1 < len(parts):
                pairs.append(copy(first, first_buf, parts[k + 1]))
            pairs.append(copy(second, second_buf, part))
        self.copies = [pltpu.make_async_copy(a, b, sems.at[k]) for k, (a, b) in enumerate(pairs)]
        self.next = 0
        for item in self.copies[:AHEAD]:
            item.start()

    def take(self):
        k = self.next
        self.copies[k].wait()
        if k + AHEAD < len(self.copies):
            self.copies[k + AHEAD].start()
        self.next = k + 1


def pipelined(parts, product, finish):
    held = None
    for part in parts:
        value = product(*part)
        if held is not None:
            finish(*held, False)
        held = part + (value,)
    finish(*held, True)


def params(flops, moved, transcendentals=0, grant=50):
    return dict(
        compiler_params=pltpu.CompilerParams(vmem_limit_bytes=grant * MIB),
        cost_estimate=pl.CostEstimate(flops=flops, bytes_accessed=moved, transcendentals=transcendentals),
    )


def struct(shape, dtype):
    return jax.ShapeDtypeStruct(shape, dtype)


def staging(rows, features, lanes):
    return pltpu.VMEM((features, lanes) if rows % 16 else (8, 128), F32)


def place_blocks(target, lanes, stage, order, blocks, rows, first=0):
    for place, value in enumerate(blocks):
        if rows % 16:
            stage[pl.ds(pl.multiple_of(order[first + place] * rows, 8), rows), :] = value().astype(F32)
        else:
            target[pl.ds(pl.multiple_of(order[first + place] * rows, 16), rows), lanes] = value()
    if rows % 16:
        target[:, lanes] = stage[...].astype(target.dtype)


def turn_modulation(modulation, columns):
    for start, size in pieces(0, modulation.shape[2], 128):
        rows = modulation[0, :, pl.ds(start, size)]
        columns[pl.ds(start, size), :] = jnp.concatenate([rows, jnp.zeros((5, size), F32)], 0).T


def normalize(acts, mod, normed, stats):
    features, tokens = acts.shape[1:]
    parts = pieces(0, features, 128)
    total = jnp.zeros((1, tokens), F32)
    for start, size in parts:
        total += jnp.sum(acts[0, pl.ds(start, size), :].astype(F32), 0, keepdims=True)
    mean = total / features
    total = jnp.zeros((1, tokens), F32)
    for start, size in parts:
        centred = acts[0, pl.ds(start, size), :].astype(F32) - mean
        total += jnp.sum(centred * centred, 0, keepdims=True)
    inv = lax.rsqrt(total / features + EPSILON)
    stats[0:1, :] = mean
    stats[1:2, :] = inv
    for start, size in parts:
        rows = pl.ds(start, size)
        xhat = (acts[0, rows, :].astype(F32) - mean) * inv
        normed[:, rows] = (xhat * (1.0 + mod[rows, 1:2]) + mod[rows, 0:1]).T.astype(BF16)


def against_rows(columns, weight):
    return lax.dot_general(columns, weight, (((1,), (1,)), ((), ())), preferred_element_type=F32)


def accumulate(total, part, weight, before, finish):
    for at, size in pieces(0, weight.shape[1]):
        columns = pl.ds(at, size)
        value = jnp.dot(part, weight[:, columns], preferred_element_type=F32)
        if before is not None:
            value = value + before[:, columns]
        if finish is None:
            total[:, columns] = value
        else:
            finish(at, size, value)


def forward_products(stream, parts, base, normed, in_buf, out_buf, slope_out, total, before, last):
    state = [before]

    def product(at, size):
        stream.take()
        return against_rows(normed[...], in_buf[pl.ds(at - base, size), :])

    def finish(at, size, pre, final):
        rows = pl.ds(at - base, size)
        hidden, slope = gelu_and_slope(pre)
        slope_out[:, rows] = slope
        stream.take()
        accumulate(total, hidden.astype(BF16), out_buf.at[rows, :], state[0], last if final else None)
        state[0] = total

    pipelined(parts, product, finish)


def forward_first_kernel(acts, modulation, w_in, w_out, mod, normed, stats, slope_out, total, in_buf, out_buf, sems):
    parts = pieces(0, slope_out.shape[1])
    stream = Stream(w_in, in_buf, w_out, out_buf, parts, 0, sems)
    turn_modulation(modulation, mod)
    normalize(acts, mod, normed, stats)
    forward_products(stream, parts, 0, normed, in_buf, out_buf, slope_out, total, None, None)


def forward_last_kernel(start, order, normed, before, w_in, w_out, slope_out, *refs):
    outs, (in_buf, out_buf, total, full, sems) = refs[:-5], refs[-5:]
    parts = pieces(start, start + slope_out.shape[1])
    stream = Stream(w_in, in_buf, w_out, out_buf, parts, start, sems)

    def last(at, size, value):
        full[pl.ds(at, size), :] = value.T

    forward_products(stream, parts, start, normed, in_buf, out_buf, slope_out, total, before, last)
    write_blocks(order, full, outs)


def layer_scratch(part, features):
    return [
        pltpu.VMEM((part, features), BF16),
        pltpu.VMEM((part, features), BF16),
    ]


def layer_params(part, features, tokens, transcendentals):
    return params(4 * part * features * tokens, 4 * part * features + 4 * features * tokens, transcendentals)


def forward_first(acts, modulation, w_in, w_out, part, name):
    features, tokens = acts.shape[1:]
    return pl.pallas_call(
        forward_first_kernel,
        out_shape=(
            struct((features, 8), F32),
            struct((tokens, features), BF16),
            struct((2, tokens), F32),
            struct((tokens, part), F32),
            struct((tokens, features), F32),
        ),
        in_specs=[WHOLE, WHOLE, HELD, HELD],
        out_specs=[WHOLE] * 5,
        scratch_shapes=layer_scratch(part, features) + [pltpu.SemaphoreType.DMA((2 * len(pieces(0, part)),))],
        name=name,
        **layer_params(part, features, tokens, part * tokens),
    )(acts, modulation, w_in, w_out)


def forward_last(order, normed, before, w_in, w_out, start, blocks, name):
    hidden, features = w_in.shape[1:]
    tokens, part, rows = before.shape[0], hidden - start, features // blocks
    slope, *outs = pl.pallas_call(
        functools.partial(forward_last_kernel, start),
        out_shape=[struct((tokens, part), F32), struct((rows, tokens), F32)]
        + [struct((rows, tokens), BF16)] * (blocks - 1),
        in_specs=[SCALARS, WHOLE, WHOLE, HELD, HELD],
        out_specs=[WHOLE] * (blocks + 1),
        scratch_shapes=layer_scratch(part, features)
        + [
            pltpu.VMEM((tokens, features), F32),
            pltpu.VMEM((features, tokens), F32),
            pltpu.SemaphoreType.DMA((2 * len(pieces(start, hidden)),)),
        ],
        name=name,
        **layer_params(part, features, tokens, part * tokens),
    )(order, normed, before, w_in, w_out)
    return slope, outs[0], outs[1:]


def write_blocks(order, full, outs):
    for place, target in enumerate(outs):
        rows = target.shape[0]
        offset = pl.multiple_of(order[place] * rows, 8)
        target[...] = full[pl.ds(offset, rows), :].astype(target.dtype)


def backward_products(stream, parts, base, grad, slopes, in_buf, out_buf, total, before, last):
    state = [before]

    def product(at, size):
        stream.take()
        return against_rows(grad[...], out_buf[pl.ds(at - base, size), :])

    def finish(at, size, value, final):
        rows = pl.ds(at - base, size)
        seen = slopes[0].shape[1]
        slope = slopes[0][:, pl.ds(at, size)] if at < seen else slopes[1][:, pl.ds(at - seen, size)]
        stream.take()
        accumulate(total, (value * slope).astype(BF16), in_buf.at[rows, :], state[0], last if final else None)
        state[0] = total

    pipelined(parts, product, finish)


def backward_first_kernel(blocks, part, order, *refs):
    pieces_in, (slope_a, slope_b, w_in, w_out, grad, total, in_buf, out_buf, full, stage, sems) = refs[:blocks], refs[blocks:]
    parts = pieces(0, part)
    stream = Stream(w_out, out_buf, w_in, in_buf, parts, 0, sems)
    values = [lambda ref=ref: ref[...] for ref in pieces_in]
    place_blocks(full, slice(None), stage, order, values, pieces_in[0].shape[0])
    for start, size in pieces(0, full.shape[0], 128):
        rows = pl.ds(start, size)
        grad[:, rows] = full[rows, :].astype(F32).T.astype(BF16)
    backward_products(stream, parts, 0, grad, (slope_a, slope_b), in_buf, out_buf, total, None, None)


def backward_first(order, gathered, slope_a, slope_b, w_in, w_out, part, name):
    hidden, features = w_in.shape[1:]
    blocks, (rows, tokens) = len(gathered), gathered[0].shape
    return pl.pallas_call(
        functools.partial(backward_first_kernel, blocks, part),
        out_shape=(struct((tokens, features), BF16), struct((tokens, features), F32)),
        in_specs=[SCALARS] + [WHOLE] * (blocks + 2) + [HELD, HELD],
        out_specs=[WHOLE] * 2,
        scratch_shapes=layer_scratch(part, features)
        + [
            pltpu.VMEM((features, tokens), BF16),
            staging(rows, features, tokens),
            pltpu.SemaphoreType.DMA((2 * len(pieces(0, part)),)),
        ],
        name=name,
        **layer_params(part, features, tokens, 0),
    )(order, *gathered, slope_a, slope_b, w_in, w_out)


def backward_last_kernel(start, rows, order, grad, before, slope_a, slope_b, acts, stats, mod, w_in, w_out, *refs):
    outs, (sums_out, in_buf, out_buf, total, full, sems) = refs[:-6], refs[-6:]
    hidden, (features, tokens) = w_in.shape[1], full.shape
    parts = pieces(start, hidden)
    stream = Stream(w_out, out_buf, w_in, in_buf, parts, start, sems)
    mean, inv = stats[0:1, :], stats[1:2, :]
    sums = [jnp.zeros((1, tokens), F32), jnp.zeros((1, tokens), F32)]

    def last(at, size, value):
        at = pl.ds(at, size)
        value = value.T
        full[at, :] = value
        scaled = value * (1.0 + mod[at, 1:2])
        xhat = (acts[0, at, :].astype(F32) - mean) * inv
        sums[0] += jnp.sum(scaled, 0, keepdims=True)
        sums[1] += jnp.sum(scaled * xhat, 0, keepdims=True)

    backward_products(stream, parts, start, grad, (slope_a, slope_b), in_buf, out_buf, total, before, last)
    count = len(outs) // 2
    padded = outs[0].shape[0] - 16
    tail = pack_sums(*sums)
    for place in range(count):
        offset = pl.multiple_of(order[2 * place] * rows, 8)
        outs[count + place][...] = full[pl.ds(offset, rows), :]
        offset = pl.multiple_of(order[2 * place + 1] * rows, 8)
        block = full[pl.ds(offset, rows), :]
        if padded > rows:
            block = jnp.concatenate([block, jnp.zeros((padded - rows, tokens), F32)], 0)
        outs[place][:padded, :] = block.astype(BF16)
        outs[place][padded:, :] = tail
    sums_out[0:1, :] = sums[0]
    sums_out[1:2, :] = sums[1]


def backward_last(order, grad, before, slope_a, slope_b, acts, stats, mod, w_in, w_out, start, blocks, name):
    hidden, features = w_in.shape[1:]
    tokens, part, rows, count = before.shape[0], hidden - start, features // blocks, blocks // 2
    outs = pl.pallas_call(
        functools.partial(backward_last_kernel, start, rows),
        out_shape=[struct((-(-rows // 16) * 16 + 16, tokens), BF16)] * count
        + [struct((rows, tokens), F32)] * count
        + [struct((2, tokens), F32)],
        in_specs=[SCALARS] + [WHOLE] * 7 + [HELD, HELD],
        out_specs=[WHOLE] * (blocks + 1),
        scratch_shapes=layer_scratch(part, features)
        + [
            pltpu.VMEM((tokens, features), F32),
            pltpu.VMEM((features, tokens), F32),
            pltpu.SemaphoreType.DMA((2 * len(pieces(start, hidden)),)),
        ],
        name=name,
        **layer_params(part, features, tokens, 0),
    )(order, grad, before, slope_a, slope_b, acts, stats, mod, w_in, w_out)
    return outs[:count], outs[count:-1], outs[-1]


def fold_kernel(rows, count, *refs):
    got, kept, (sums, *outs) = refs[:count], refs[count : 2 * count], refs[2 * count :]
    more = unpack_sums(got[0][-16:, :])
    plain, along = sums[0:1, :] + more[0], sums[1:2, :] + more[1]
    tail = pack_sums(plain, along)
    padded = got[0].shape[0] - 16
    for place in range(count // 2):
        even, odd = 2 * place, 2 * place + 1
        outs[count // 2 + place][...] = kept[even][...] + got[even][:rows, :].astype(F32)
        block = kept[odd][...] + got[odd][:rows, :].astype(F32)
        if padded > rows:
            block = jnp.concatenate([block, jnp.zeros((padded - rows, block.shape[1]), F32)], 0)
        outs[place][:padded, :] = block.astype(BF16)
        outs[place][padded:, :] = tail
    outs[-1][0:1, :] = plain
    outs[-1][1:2, :] = along


def fold(got, kept, sums):
    count, (rows, tokens) = len(kept), kept[0].shape
    outs = pl.pallas_call(
        functools.partial(fold_kernel, rows, count),
        out_shape=[struct(got[0].shape, BF16)] * (count // 2)
        + [struct((rows, tokens), F32)] * (count // 2)
        + [struct((2, tokens), F32)],
        in_specs=[WHOLE] * (2 * count + 1),
        out_specs=[WHOLE] * (count + 1),
        name="fold",
        **params(2 * count * rows * tokens, 8 * count * rows * tokens, grant=12),
    )(*got, *kept, sums)
    return outs[: count // 2], outs[count // 2 : -1], outs[-1]


def upstream_kernel(blocks, order, weight, own, arrived, *refs):
    outs, (cot0, cot1_rows, full) = refs[:-3], refs[-3:]
    group = order[blocks]
    control = group == 0
    half = cot0.shape[1]
    lanes = pl.ds(pl.multiple_of(group * half, half), half)
    cot0[...] = jnp.where(control, own[:, lanes], arrived[:, lanes])
    mine = jnp.where(control, arrived[:, lanes], own[:, lanes])
    cot1_rows[...] = jnp.where(control, arrived[...], own[...])
    full[...] = lax.dot_general(mine, weight[...], (((0,), (0,)), ((), ())), preferred_element_type=F32).T
    write_blocks(order, full, outs)


def upstream_terms(order, weight, own, arrived, blocks):
    rows, tokens = own.shape
    half = tokens // 2
    outs = pl.pallas_call(
        functools.partial(upstream_kernel, blocks),
        out_shape=[struct((rows, half), F32)]
        + [struct((rows, half), BF16)] * blocks
        + [struct((rows, tokens), BF16)],
        in_specs=[SCALARS] + [WHOLE] * 3,
        out_specs=[WHOLE] * (blocks + 2),
        scratch_shapes=[pltpu.VMEM((weight.shape[1], half), F32)],
        name="upstream_terms",
        **params(2 * weight.size * half, 2 * weight.size + 4 * blocks * rows * half, grant=12),
    )(order, weight, own, arrived)
    return outs[0], outs[1:blocks], *outs[blocks:]


def residual_kernel(order, weight, *refs):
    stack, (result, full, stage) = refs[:-3], refs[-3:]
    values = [lambda value=value: value[...] for value in stack]
    place_blocks(full, slice(None), stage, order, values, stack[0].shape[0])
    result[...] = jnp.dot(weight[...], full[...], preferred_element_type=F32)


def residual_rows(order, weight, stack):
    blocks, (rows, half) = len(stack), stack[0].shape
    return pl.pallas_call(
        residual_kernel,
        out_shape=struct((rows, half), F32),
        in_specs=[SCALARS] + [WHOLE] * (blocks + 1),
        out_specs=WHOLE,
        scratch_shapes=[pltpu.VMEM((blocks * rows, half), BF16), staging(rows, blocks * rows, half)],
        name="residual_rows",
        **params(2 * weight.size * half, 2 * weight.size + 4 * blocks * rows * half, grant=12),
    )(order, weight, *stack)


def zero_grad_kernel(blocks, parts, order, dp_order, *refs):
    cots, stacks, (out, lhs, rhs, stage, buf, sems) = refs[:parts], refs[parts:-6], refs[-6:]
    near, near_other, far, far_other = (stacks[k * blocks : (k + 1) * blocks] for k in range(4))
    rows, half = near[0].shape
    group = order[blocks]
    for part in range(parts):
        lhs[:, pl.ds(pl.multiple_of(dp_order[part] * 2 * half, 2 * half), 2 * half)] = cots[part][...]
        for side, sources in enumerate((near, near_other) if part == 0 else (far, far_other)):
            at = Ellipsis if part == 0 else part - 1
            values = [lambda source=source, at=at: source[at] for source in sources]
            owner = group if side == 0 else 1 - group
            lanes = pl.ds(pl.multiple_of((dp_order[part] * 2 + owner) * half, half), half)
            place_blocks(rhs, lanes, stage, order, values, rows, side * (blocks + 1))
    copies = []
    for k, (start, size) in enumerate(pieces(0, blocks * rows, CHUNK)):
        columns = pl.ds(start, size)
        buf[:, columns] = lax.dot_general(
            lhs[...], rhs[columns, :], (((1,), (1,)), ((), ())), preferred_element_type=F32
        )
        copies.append(pltpu.make_async_copy(buf.at[:, columns], out.at[:, columns], sems.at[k]))
        copies[-1].start()
    for copy in copies:
        copy.wait()


def zero_projection_grad(order, dp_order, cots, near, near_other, far, far_other):
    blocks, (rows, half) = len(near), near[0].shape
    parts = len(cots)
    features, tokens = blocks * rows, parts * 2 * half

    return pl.pallas_call(
        functools.partial(zero_grad_kernel, blocks, parts),
        out_shape=struct((rows, features), F32),
        in_specs=[SCALARS] * 2 + [WHOLE] * (parts + 4 * blocks),
        out_specs=HELD,
        scratch_shapes=[
            pltpu.VMEM((rows, tokens), BF16),
            pltpu.VMEM((features, tokens), BF16),
            staging(rows, features, half),
            pltpu.VMEM((rows, features), F32),
            pltpu.SemaphoreType.DMA((len(pieces(0, features, CHUNK)),)),
        ],
        name="zero_projection_grad",
        **params(2 * tokens * rows * features, 4 * rows * features + 2 * tokens * (rows + features), grant=28),
    )(order, dp_order, *cots, *near, *near_other, *far, *far_other)


def steps(values, level, *during):
    got = [step(value, level) for value in values]
    return list(lax.optimization_barrier((tuple(got),) + during)[0]) if during else got


def direct(values, *during):
    got = [send(value, place + 1) for place, value in enumerate(values)]
    return list(lax.optimization_barrier((tuple(got),) + during)[0])


def local(acts, modulation, w_in, w_out, zero_weight, cotangent):
    own_cot = cotangent[0]
    features, tokens = acts.shape[1:]
    hidden = w_in.shape[1]
    rows = own_cot.shape[0]
    half = tokens // 2
    blocks, levels = lax.axis_size("fsdp"), stages()
    parts = lax.axis_size("dp")
    group = lax.axis_index("grp").astype(jnp.int32)
    me = lax.axis_index("fsdp").astype(jnp.int32)
    is_control = group == 0
    places = block_order(group, me)
    order = jnp.concatenate([places, group[None], block_order(1 - group, me)])
    dp_order = lax.axis_index("dp").astype(jnp.int32) ^ jnp.arange(parts, dtype=jnp.int32)

    arrived = swap_grp(own_cot)
    own_term, sent, cot0, cot1_rows = upstream_terms(order, zero_weight, own_cot, arrived, blocks)
    split, cut = split_rows(hidden)
    mod, normed, stats, slope_a, total = forward_first(
        after(acts, *sent), modulation, w_in, w_out, split, "forward_first"
    )
    own_mod = block_of(mod, me, rows)
    own_gate = own_mod[:, 2:3]
    got = direct(sent, total)
    up_half = own_term + cot0.astype(F32) + sum(value.astype(F32) for value in got)
    up_rows = jnp.where(is_control, jnp.concatenate([up_half, swap_grp(up_half)], 1), own_cot.astype(F32))
    grad_rows = (own_gate * up_rows).astype(BF16)

    slope_b, kept, sent = forward_last(
        order, after(normed, grad_rows), total, w_in, w_out, split, blocks, "forward_last"
    )
    gathered = [grad_rows] + direct([grad_rows] * (blocks - 1), kept)
    cots = gather_dp(cot1_rows)
    grad, total = backward_first(
        order, after(gathered, *sent, *cots), slope_a, slope_b, w_in, w_out, cut, "backward_first"
    )
    got = direct(sent, total)
    own_values = block_of(acts[0], me, rows).astype(F32)
    sums = own_values + own_gate * (kept + sum(value.astype(F32) for value in got))
    out_rows = sums.astype(BF16)

    out_half = jnp.where(is_control, out_rows[:, :half], swap_grp(out_rows[:, half:]))
    far = gather_dp(out_half)[1:]
    sent, kept, token_sums = backward_last(
        order, after(grad, out_half), total, slope_a, slope_b, acts, stats, mod, w_in, w_out, cut, blocks, "backward_last"
    )
    near = [out_half, step(out_half, 0)]
    far, near, sent, kept, token_sums = lax.optimization_barrier((far, near, sent, kept, token_sums))
    for level in range(1, levels):
        near = near + steps(near, level)
    near_other = [swap_grp(value) for value in near]
    residual = residual_rows(order, zero_weight, near)
    far = [jnp.stack(far)]

    for level in range(levels):
        got = steps(sent, level)
        far = far + steps(far, level)
        if level + 1 < levels:
            sent, kept, token_sums = fold(got, kept, token_sums)
    more = unpack_sums(got[0][-16:])
    plain, along = token_sums[0:1] + more[0], token_sums[1:2] + more[1]
    kept = [kept[0] + got[0][:rows].astype(F32)]
    mean, inv = stats[0:1], stats[1:2]
    back = inv * (
        kept[0] * (1.0 + own_mod[:, 1:2]) - plain / features - (own_values - mean) * inv * (along / features)
    )
    residual = jnp.concatenate([swap_grp(residual), residual], 1)
    block_rows = jnp.where(is_control, out_rows, (sums + residual).astype(BF16))

    far_other = [swap_grp(value) for value in far]
    zero_grad = zero_projection_grad(order, dp_order, cots, near, near_other, far, far_other)
    return (block_rows[None], (up_rows + back)[None], zero_grad)


def solution(mesh):
    placed = (
        P("grp", None, "dp"),
        P("grp", None, None),
        P("grp", "fsdp", None),
        P("grp", "fsdp", None),
        P("fsdp", None),
        P("grp", "fsdp", "dp"),
    )
    return jax.shard_map(
        local,
        mesh=mesh,
        in_specs=placed,
        out_specs=(P("grp", "fsdp", "dp"), P("grp", "fsdp", "dp"), P("fsdp", None)),
        check_vma=False,
    )
```

```python
import functools

import jax
import jax.numpy as jnp
from jax import lax
from jax.experimental import pallas as pl
from jax.experimental.pallas import tpu as pltpu
from jax.sharding import PartitionSpec as P

EPSILON = 1e-06
SQRT_2_OVER_PI = 0.7978845608028654
CHUNK = 512
AHEAD = 3
MIB = 1024 * 1024
F32, BF16 = jnp.float32, jnp.bfloat16
WHOLE = pl.BlockSpec(memory_space=pltpu.VMEM)
HELD = pl.BlockSpec(memory_space=pltpu.HBM)
SCALARS = pl.BlockSpec(memory_space=pltpu.SMEM)


def pieces(start, stop, size=CHUNK):
    return [(at, min(size, stop - at)) for at in range(start, stop, size)]


def split_rows(hidden):
    units = hidden // CHUNK
    return CHUNK * max(units // 2, 1), (hidden - 1) // CHUNK * CHUNK


def after(value, *others):
    return lax.optimization_barrier((value,) + others)[0]


def swap_grp(value):
    return lax.ppermute(value, "grp", [(0, 1), (1, 0)])


def stages():
    return (lax.axis_size("fsdp") - 1).bit_length()


def step(value, stage):
    length, bits = lax.axis_size("fsdp"), stages()
    pairs = []
    for group, bit in ((0, stage), (1, bits - 1 - stage)):
        pairs += [(group * length + i, group * length + (i ^ (1 << bit))) for i in range(length)]
    return lax.ppermute(value, ("grp", "fsdp"), pairs)


def block_order(group, me):
    length, bits = lax.axis_size("fsdp"), stages()
    turned = [sum(((v >> b) & 1) << (bits - 1 - b) for b in range(bits)) for v in range(length)]
    up, down = jnp.arange(length, dtype=jnp.int32), jnp.array(turned, jnp.int32)
    return me ^ jnp.where(group == 0, up, down)


def send(value, place):
    length, bits = lax.axis_size("fsdp"), stages()
    turned = sum(((place >> b) & 1) << (bits - 1 - b) for b in range(bits))
    pairs = []
    for group, mask in ((0, place), (1, turned)):
        pairs += [(group * length + i, group * length + (i ^ mask)) for i in range(length)]
    return lax.ppermute(value, ("grp", "fsdp"), pairs)


def gather_dp(value):
    length = lax.axis_size("dp")
    return [value] + [
        lax.ppermute(value, "dp", [(i, i ^ mask) for i in range(length)]) for mask in range(1, length)
    ]


def block_of(value, index, rows):
    return lax.dynamic_slice_in_dim(value, index * rows, rows, 0)


def split_three(value):
    high = value.astype(BF16)
    rest = value - high.astype(F32)
    mid = rest.astype(BF16)
    return high, mid, (rest - mid.astype(F32)).astype(BF16)


def pack_sums(plain, along):
    tail = [part.astype(F32) for part in split_three(plain) + split_three(along)]
    return jnp.concatenate(tail + [jnp.zeros((10, plain.shape[1]), F32)], 0).astype(BF16)


def unpack_sums(tail):
    tail = tail.astype(F32)
    return tail[0:1] + tail[1:2] + tail[2:3], tail[3:4] + tail[4:5] + tail[5:6]


def gelu_and_slope(v):
    square = v * v
    t = jnp.tanh(SQRT_2_OVER_PI * (v + 0.044715 * (square * v)))
    rise = 0.5 * (1.0 + t)
    slope = rise + 0.5 * v * (1.0 - t * t) * (SQRT_2_OVER_PI * (1.0 + (3 * 0.044715) * square))
    return v * rise, slope


class Stream:
    def __init__(self, first, first_buf, second, second_buf, parts, base, sems):
        def copy(weight, buf, part):
            return weight.at[0, pl.ds(part[0], part[1]), :], buf.at[pl.ds(part[0] - base, part[1]), :]

        pairs = [copy(first, first_buf, parts[0])]
        for k, part in enumerate(parts):
            if k + 1 < len(parts):
                pairs.append(copy(first, first_buf, parts[k + 1]))
            pairs.append(copy(second, second_buf, part))
        self.copies = [pltpu.make_async_copy(a, b, sems.at[k]) for k, (a, b) in enumerate(pairs)]
        self.next = 0
        for item in self.copies[:AHEAD]:
            item.start()

    def take(self):
        k = self.next
        self.copies[k].wait()
        if k + AHEAD < len(self.copies):
            self.copies[k + AHEAD].start()
        self.next = k + 1


def pipelined(parts, product, finish):
    held = None
    for part in parts:
        value = product(*part)
        if held is not None:
            finish(*held, False)
        held = part + (value,)
    finish(*held, True)


def params(flops, moved, transcendentals=0, grant=50):
    return dict(
        compiler_params=pltpu.CompilerParams(vmem_limit_bytes=grant * MIB),
        cost_estimate=pl.CostEstimate(flops=flops, bytes_accessed=moved, transcendentals=transcendentals),
    )


def struct(shape, dtype):
    return jax.ShapeDtypeStruct(shape, dtype)


def staging(rows, features, lanes):
    return pltpu.VMEM((features, lanes) if rows % 16 else (8, 128), F32)


def place_blocks(target, lanes, stage, order, blocks, rows, first=0):
    for place, value in enumerate(blocks):
        if rows % 16:
            stage[pl.ds(pl.multiple_of(order[first + place] * rows, 8), rows), :] = value().astype(F32)
        else:
            target[pl.ds(pl.multiple_of(order[first + place] * rows, 16), rows), lanes] = value()
    if rows % 16:
        target[:, lanes] = stage[...].astype(target.dtype)


def turn_modulation(modulation, columns):
    for start, size in pieces(0, modulation.shape[2], 128):
        rows = modulation[0, :, pl.ds(start, size)]
        columns[pl.ds(start, size), :] = jnp.concatenate([rows, jnp.zeros((5, size), F32)], 0).T


def normalize(acts, mod, normed, stats):
    features, tokens = acts.shape[1:]
    parts = pieces(0, features, 128)
    total = jnp.zeros((1, tokens), F32)
    for start, size in parts:
        total += jnp.sum(acts[0, pl.ds(start, size), :].astype(F32), 0, keepdims=True)
    mean = total / features
    total = jnp.zeros((1, tokens), F32)
    for start, size in parts:
        centred = acts[0, pl.ds(start, size), :].astype(F32) - mean
        total += jnp.sum(centred * centred, 0, keepdims=True)
    inv = lax.rsqrt(total / features + EPSILON)
    stats[0:1, :] = mean
    stats[1:2, :] = inv
    for start, size in parts:
        rows = pl.ds(start, size)
        xhat = (acts[0, rows, :].astype(F32) - mean) * inv
        normed[:, rows] = (xhat * (1.0 + mod[rows, 1:2]) + mod[rows, 0:1]).T.astype(BF16)


def against_rows(columns, weight):
    return lax.dot_general(columns, weight, (((1,), (1,)), ((), ())), preferred_element_type=F32)


def accumulate(total, part, weight, before, finish):
    for at, size in pieces(0, weight.shape[1]):
        columns = pl.ds(at, size)
        value = jnp.dot(part, weight[:, columns], preferred_element_type=F32)
        if before is not None:
            value = value + before[:, columns]
        if finish is None:
            total[:, columns] = value
        else:
            finish(at, size, value)


def forward_products(stream, parts, base, normed, in_buf, out_buf, slope_out, total, before, last):
    state = [before]

    def product(at, size):
        stream.take()
        return against_rows(normed[...], in_buf[pl.ds(at - base, size), :])

    def finish(at, size, pre, final):
        rows = pl.ds(at - base, size)
        hidden, slope = gelu_and_slope(pre)
        slope_out[:, rows] = slope
        stream.take()
        accumulate(total, hidden.astype(BF16), out_buf.at[rows, :], state[0], last if final else None)
        state[0] = total

    pipelined(parts, product, finish)


def forward_first_kernel(normed, w_in, w_out, slope_out, total, in_buf, out_buf, sems):
    parts = pieces(0, slope_out.shape[1])
    stream = Stream(w_in, in_buf, w_out, out_buf, parts, 0, sems)
    forward_products(stream, parts, 0, normed, in_buf, out_buf, slope_out, total, None, None)


def forward_last_kernel(start, order, normed, before, w_in, w_out, slope_out, *refs):
    outs, (in_buf, out_buf, total, full, sems) = refs[:-5], refs[-5:]
    parts = pieces(start, start + slope_out.shape[1])
    stream = Stream(w_in, in_buf, w_out, out_buf, parts, start, sems)

    def last(at, size, value):
        full[pl.ds(at, size), :] = value.T

    forward_products(stream, parts, start, normed, in_buf, out_buf, slope_out, total, before, last)
    write_blocks(order, full, outs)


def layer_scratch(part, features):
    return [
        pltpu.VMEM((part, features), BF16),
        pltpu.VMEM((part, features), BF16),
    ]


def layer_params(part, features, tokens, transcendentals):
    return params(4 * part * features * tokens, 4 * part * features + 4 * features * tokens, transcendentals)


def forward_first(normed, w_in, w_out, part, name):
    tokens, features = normed.shape
    return pl.pallas_call(
        forward_first_kernel,
        out_shape=(struct((tokens, part), F32), struct((tokens, features), F32)),
        in_specs=[WHOLE, HELD, HELD],
        out_specs=[WHOLE] * 2,
        scratch_shapes=layer_scratch(part, features) + [pltpu.SemaphoreType.DMA((2 * len(pieces(0, part)),))],
        name=name,
        **layer_params(part, features, tokens, part * tokens),
    )(normed, w_in, w_out)


def forward_last(order, normed, before, w_in, w_out, start, blocks, name):
    hidden, features = w_in.shape[1:]
    tokens, part, rows = before.shape[0], hidden - start, features // blocks
    slope, *outs = pl.pallas_call(
        functools.partial(forward_last_kernel, start),
        out_shape=[struct((tokens, part), F32), struct((rows, tokens), F32)]
        + [struct((rows, tokens), BF16)] * (blocks - 1),
        in_specs=[SCALARS, WHOLE, WHOLE, HELD, HELD],
        out_specs=[WHOLE] * (blocks + 1),
        scratch_shapes=layer_scratch(part, features)
        + [
            pltpu.VMEM((tokens, features), F32),
            pltpu.VMEM((features, tokens), F32),
            pltpu.SemaphoreType.DMA((2 * len(pieces(start, hidden)),)),
        ],
        name=name,
        **layer_params(part, features, tokens, part * tokens),
    )(order, normed, before, w_in, w_out)
    return slope, outs[0], outs[1:]


def write_blocks(order, full, outs):
    for place, target in enumerate(outs):
        rows = target.shape[0]
        offset = pl.multiple_of(order[place] * rows, 8)
        target[...] = full[pl.ds(offset, rows), :].astype(target.dtype)


def backward_products(stream, parts, base, grad, slopes, in_buf, out_buf, total, before, last):
    state = [before]

    def product(at, size):
        stream.take()
        return against_rows(grad[...], out_buf[pl.ds(at - base, size), :])

    def finish(at, size, value, final):
        rows = pl.ds(at - base, size)
        seen = slopes[0].shape[1]
        slope = slopes[0][:, pl.ds(at, size)] if at < seen else slopes[1][:, pl.ds(at - seen, size)]
        stream.take()
        accumulate(total, (value * slope).astype(BF16), in_buf.at[rows, :], state[0], last if final else None)
        state[0] = total

    pipelined(parts, product, finish)


def backward_first_kernel(blocks, part, order, *refs):
    pieces_in, (slope_a, slope_b, w_in, w_out, grad, total, in_buf, out_buf, full, stage, sems) = refs[:blocks], refs[blocks:]
    parts = pieces(0, part)
    stream = Stream(w_out, out_buf, w_in, in_buf, parts, 0, sems)
    values = [lambda ref=ref: ref[...] for ref in pieces_in]
    place_blocks(full, slice(None), stage, order, values, pieces_in[0].shape[0])
    for start, size in pieces(0, full.shape[0], 128):
        rows = pl.ds(start, size)
        grad[:, rows] = full[rows, :].astype(F32).T.astype(BF16)
    backward_products(stream, parts, 0, grad, (slope_a, slope_b), in_buf, out_buf, total, None, None)


def backward_first(order, gathered, slope_a, slope_b, w_in, w_out, part, name):
    hidden, features = w_in.shape[1:]
    blocks, (rows, tokens) = len(gathered), gathered[0].shape
    return pl.pallas_call(
        functools.partial(backward_first_kernel, blocks, part),
        out_shape=(struct((tokens, features), BF16), struct((tokens, features), F32)),
        in_specs=[SCALARS] + [WHOLE] * (blocks + 2) + [HELD, HELD],
        out_specs=[WHOLE] * 2,
        scratch_shapes=layer_scratch(part, features)
        + [
            pltpu.VMEM((features, tokens), BF16),
            staging(rows, features, tokens),
            pltpu.SemaphoreType.DMA((2 * len(pieces(0, part)),)),
        ],
        name=name,
        **layer_params(part, features, tokens, 0),
    )(order, *gathered, slope_a, slope_b, w_in, w_out)


def backward_last_kernel(start, rows, order, grad, before, slope_a, slope_b, acts, stats, mod, w_in, w_out, *refs):
    outs, (sums_out, in_buf, out_buf, total, full, sems) = refs[:-6], refs[-6:]
    hidden, (features, tokens) = w_in.shape[1], full.shape
    parts = pieces(start, hidden)
    stream = Stream(w_out, out_buf, w_in, in_buf, parts, start, sems)
    mean, inv = stats[0:1, :], stats[1:2, :]
    sums = [jnp.zeros((1, tokens), F32), jnp.zeros((1, tokens), F32)]

    def last(at, size, value):
        at = pl.ds(at, size)
        value = value.T
        full[at, :] = value
        scaled = value * (1.0 + mod[at, 1:2])
        xhat = (acts[0, at, :].astype(F32) - mean) * inv
        sums[0] += jnp.sum(scaled, 0, keepdims=True)
        sums[1] += jnp.sum(scaled * xhat, 0, keepdims=True)

    backward_products(stream, parts, start, grad, (slope_a, slope_b), in_buf, out_buf, total, before, last)
    count = len(outs) // 2
    padded = outs[0].shape[0] - 16
    tail = pack_sums(*sums)
    for place in range(count):
        offset = pl.multiple_of(order[2 * place] * rows, 8)
        outs[count + place][...] = full[pl.ds(offset, rows), :]
        offset = pl.multiple_of(order[2 * place + 1] * rows, 8)
        block = full[pl.ds(offset, rows), :]
        if padded > rows:
            block = jnp.concatenate([block, jnp.zeros((padded - rows, tokens), F32)], 0)
        outs[place][:padded, :] = block.astype(BF16)
        outs[place][padded:, :] = tail
    sums_out[0:1, :] = sums[0]
    sums_out[1:2, :] = sums[1]


def backward_last(order, grad, before, slope_a, slope_b, acts, stats, mod, w_in, w_out, start, blocks, name):
    hidden, features = w_in.shape[1:]
    tokens, part, rows, count = before.shape[0], hidden - start, features // blocks, blocks // 2
    outs = pl.pallas_call(
        functools.partial(backward_last_kernel, start, rows),
        out_shape=[struct((-(-rows // 16) * 16 + 16, tokens), BF16)] * count
        + [struct((rows, tokens), F32)] * count
        + [struct((2, tokens), F32)],
        in_specs=[SCALARS] + [WHOLE] * 7 + [HELD, HELD],
        out_specs=[WHOLE] * (blocks + 1),
        scratch_shapes=layer_scratch(part, features)
        + [
            pltpu.VMEM((tokens, features), F32),
            pltpu.VMEM((features, tokens), F32),
            pltpu.SemaphoreType.DMA((2 * len(pieces(start, hidden)),)),
        ],
        name=name,
        **layer_params(part, features, tokens, 0),
    )(order, grad, before, slope_a, slope_b, acts, stats, mod, w_in, w_out)
    return outs[:count], outs[count:-1], outs[-1]


def fold_kernel(rows, count, *refs):
    got, kept, (sums, *outs) = refs[:count], refs[count : 2 * count], refs[2 * count :]
    more = unpack_sums(got[0][-16:, :])
    plain, along = sums[0:1, :] + more[0], sums[1:2, :] + more[1]
    tail = pack_sums(plain, along)
    padded = got[0].shape[0] - 16
    for place in range(count // 2):
        even, odd = 2 * place, 2 * place + 1
        outs[count // 2 + place][...] = kept[even][...] + got[even][:rows, :].astype(F32)
        block = kept[odd][...] + got[odd][:rows, :].astype(F32)
        if padded > rows:
            block = jnp.concatenate([block, jnp.zeros((padded - rows, block.shape[1]), F32)], 0)
        outs[place][:padded, :] = block.astype(BF16)
        outs[place][padded:, :] = tail
    outs[-1][0:1, :] = plain
    outs[-1][1:2, :] = along


def fold(got, kept, sums):
    count, (rows, tokens) = len(kept), kept[0].shape
    outs = pl.pallas_call(
        functools.partial(fold_kernel, rows, count),
        out_shape=[struct(got[0].shape, BF16)] * (count // 2)
        + [struct((rows, tokens), F32)] * (count // 2)
        + [struct((2, tokens), F32)],
        in_specs=[WHOLE] * (2 * count + 1),
        out_specs=[WHOLE] * (count + 1),
        name="fold",
        **params(2 * count * rows * tokens, 8 * count * rows * tokens, grant=12),
    )(*got, *kept, sums)
    return outs[: count // 2], outs[count // 2 : -1], outs[-1]


def prepare_kernel(blocks, order, acts, modulation, own, arrived, weight, *refs):
    outs, (mod, normed, stats, cot0, cot1, cot1_rows, full, buf, sem) = refs[:blocks], refs[blocks:]
    load = pltpu.make_async_copy(weight, buf, sem)
    load.start()
    group = order[blocks]
    control = group == 0
    half = cot0.shape[1]
    lanes = pl.ds(pl.multiple_of(group * half, half), half)
    cot0[...] = jnp.where(control, own[:, lanes], arrived[:, lanes])
    mine = jnp.where(control, arrived[:, lanes], own[:, lanes])
    cot1[...] = mine
    cot1_rows[...] = jnp.where(control, arrived[...], own[...])
    turn_modulation(modulation, mod)
    normalize(acts, mod, normed, stats)
    load.wait()
    full[...] = lax.dot_general(mine, buf[...], (((0,), (0,)), ((), ())), preferred_element_type=F32).T
    write_blocks(order, full, outs)


def prepare(order, acts, modulation, own, arrived, weight, blocks):
    rows, tokens = own.shape
    half, features = tokens // 2, weight.shape[1]
    outs = pl.pallas_call(
        functools.partial(prepare_kernel, blocks),
        out_shape=[struct((rows, half), F32)]
        + [struct((rows, half), BF16)] * (blocks - 1)
        + [
            struct((features, 8), F32),
            struct((tokens, features), BF16),
            struct((2, tokens), F32),
            struct((rows, half), BF16),
            struct((rows, half), BF16),
            struct((rows, tokens), BF16),
        ],
        in_specs=[SCALARS] + [WHOLE] * 4 + [HELD],
        out_specs=[WHOLE] * (blocks + 6),
        scratch_shapes=[
            pltpu.VMEM((features, half), F32),
            pltpu.VMEM(weight.shape, BF16),
            pltpu.SemaphoreType.DMA(()),
        ],
        name="prepare",
        **params(2 * weight.size * half, 2 * weight.size + 4 * blocks * rows * half, grant=50),
    )(order, acts, modulation, own, arrived, weight)
    return outs[0], outs[1:blocks], *outs[blocks:]


def residual_kernel(order, weight, *refs):
    stack, (result, full, stage) = refs[:-3], refs[-3:]
    values = [lambda value=value: value[...] for value in stack]
    place_blocks(full, slice(None), stage, order, values, stack[0].shape[0])
    result[...] = jnp.dot(weight[...], full[...], preferred_element_type=F32)


def residual_rows(order, weight, stack):
    blocks, (rows, half) = len(stack), stack[0].shape
    return pl.pallas_call(
        residual_kernel,
        out_shape=struct((rows, half), F32),
        in_specs=[SCALARS] + [WHOLE] * (blocks + 1),
        out_specs=WHOLE,
        scratch_shapes=[pltpu.VMEM((blocks * rows, half), BF16), staging(rows, blocks * rows, half)],
        name="residual_rows",
        **params(2 * weight.size * half, 2 * weight.size + 4 * blocks * rows * half, grant=12),
    )(order, weight, *stack)


def zero_grad_kernel(blocks, first, count, order, dp_order, *refs):
    cots, refs = (refs[:count], refs[count : 2 * count]), refs[2 * count :]
    stacks = []
    while len(refs) > (7 if first else 4):
        stacks.append((refs[:blocks], refs[blocks : 2 * blocks]))
        refs = refs[2 * blocks :]
    before = None
    if first:
        before, out, lhs, rhs, stage, buf, sems = refs
    else:
        buf, lhs, rhs, stage = refs
    rows, half = cots[0][0].shape
    group = order[blocks]
    for part in range(count):
        slot = part // 2 * 2 + (dp_order[first + part] & 1)
        for side, owner in enumerate((group, 1 - group)):
            lanes = pl.ds(pl.multiple_of((slot * 2 + owner) * half, half), half)
            lhs[:, lanes] = cots[side][part][...]
            if len(stacks) == count:
                values = [lambda source=source: source[...] for source in stacks[part][side]]
            else:
                values = [lambda source=source, part=part: source[part] for source in stacks[0][side]]
            place_blocks(rhs, lanes, stage, order, values, rows, side * (blocks + 1))
    copies = []
    for k, (start, size) in enumerate(pieces(0, blocks * rows)):
        columns = pl.ds(start, size)
        value = against_rows(lhs[...], rhs[columns, :])
        buf[:, columns] = value if before is None else before[:, columns] + value
        if before is not None:
            copies.append(pltpu.make_async_copy(buf.at[:, columns], out.at[:, columns], sems.at[k]))
            copies[-1].start()
    for copy in copies:
        copy.wait()


def zero_projection_grad(order, dp_order, first, cots, cots_other, stacks, before, name):
    blocks, (rows, half) = len(stacks[0][0]), cots[0].shape
    count = len(cots)
    features, tokens = blocks * rows, count * 2 * half
    flat = [block for pair in stacks for side in pair for block in side]
    extra = [] if before is None else [before]
    scratch = [
        pltpu.VMEM((rows, tokens), BF16),
        pltpu.VMEM((features, tokens), BF16),
        staging(rows, features, half),
    ]
    if extra:
        scratch += [
            pltpu.VMEM((rows, features), F32),
            pltpu.SemaphoreType.DMA((len(pieces(0, features)),)),
        ]
    return pl.pallas_call(
        functools.partial(zero_grad_kernel, blocks, first, count),
        out_shape=struct((rows, features), F32),
        in_specs=[SCALARS] * 2 + [WHOLE] * (2 * count + len(flat) + len(extra)),
        out_specs=HELD if extra else WHOLE,
        scratch_shapes=scratch,
        name=name,
        **params(2 * tokens * rows * features, 4 * rows * features + 2 * tokens * (rows + features), grant=28),
    )(order, dp_order, *cots, *cots_other, *flat, *extra)


def steps(values, level, *during):
    got = [step(value, level) for value in values]
    return list(lax.optimization_barrier((tuple(got),) + during)[0]) if during else got


def direct(values, *during):
    got = [send(value, place + 1) for place, value in enumerate(values)]
    return list(lax.optimization_barrier((tuple(got),) + during)[0])


def local(acts, modulation, w_in, w_out, zero_weight, cotangent):
    own_cot = cotangent[0]
    features, tokens = acts.shape[1:]
    hidden = w_in.shape[1]
    rows = own_cot.shape[0]
    half = tokens // 2
    blocks, levels = lax.axis_size("fsdp"), stages()
    parts = lax.axis_size("dp")
    group = lax.axis_index("grp").astype(jnp.int32)
    me = lax.axis_index("fsdp").astype(jnp.int32)
    is_control = group == 0
    places = block_order(group, me)
    order = jnp.concatenate([places, group[None], block_order(1 - group, me)])
    dp_order = lax.axis_index("dp").astype(jnp.int32) ^ jnp.arange(parts, dtype=jnp.int32)

    arrived = swap_grp(own_cot)
    own_term, sent, mod, normed, stats, cot0, cot1, cot1_rows = prepare(
        order, acts, modulation, own_cot, arrived, zero_weight, blocks
    )
    split, cut = split_rows(hidden)
    slope_a, total = forward_first(after(normed, *sent), w_in, w_out, split, "forward_first")
    own_mod = block_of(mod, me, rows)
    own_gate = own_mod[:, 2:3]
    cots = gather_dp(cot1)
    got = direct(sent, total)
    up_half = own_term + cot0.astype(F32) + sum(value.astype(F32) for value in got)
    up_rows = jnp.where(is_control, jnp.concatenate([up_half, swap_grp(up_half)], 1), own_cot.astype(F32))
    grad_rows = (own_gate * up_rows).astype(BF16)

    slope_b, kept, sent = forward_last(
        order, after(normed, grad_rows, *cots), total, w_in, w_out, split, blocks, "forward_last"
    )
    gathered = [grad_rows] + direct([grad_rows] * (blocks - 1), kept)
    grad, total = backward_first(
        order, after(gathered, *sent), slope_a, slope_b, w_in, w_out, cut, "backward_first"
    )
    got = direct(sent, total)
    own_values = block_of(acts[0], me, rows).astype(F32)
    sums = own_values + own_gate * (kept + sum(value.astype(F32) for value in got))
    out_rows = sums.astype(BF16)

    out_half = jnp.where(is_control, out_rows[:, :half], swap_grp(out_rows[:, half:]))
    far = gather_dp(out_half)[1:]
    sent, kept, token_sums = backward_last(
        order, after(grad, out_half), total, slope_a, slope_b, acts, stats, mod, w_in, w_out, cut, blocks, "backward_last"
    )
    near = [out_half, step(out_half, 0)]
    far, near, sent, kept, token_sums = lax.optimization_barrier((far, near, sent, kept, token_sums))
    for level in range(1, levels):
        near = near + steps(near, level)
    near_other = [swap_grp(value) for value in near]
    residual = residual_rows(order, zero_weight, near)
    cots_other = [swap_grp(value) for value in cots]

    gathers = [[far[0]], [jnp.stack(far[1:])]]
    for level in range(levels):
        got = steps(sent, level)
        gathers = [blocks_so_far + steps(blocks_so_far, level) for blocks_so_far in gathers]
        if level + 1 < levels:
            sent, kept, token_sums = fold(got, kept, token_sums)
    more = unpack_sums(got[0][-16:])
    plain, along = token_sums[0:1] + more[0], token_sums[1:2] + more[1]
    kept = [kept[0] + got[0][:rows].astype(F32)]
    mean, inv = stats[0:1], stats[1:2]
    back = inv * (
        kept[0] * (1.0 + own_mod[:, 1:2]) - plain / features - (own_values - mean) * inv * (along / features)
    )
    residual = jnp.concatenate([swap_grp(residual), residual], 1)
    block_rows = jnp.where(is_control, out_rows, (sums + residual).astype(BF16))

    stacks = [(near, near_other)] + [(mine, [swap_grp(value) for value in mine]) for mine in gathers]
    zero_grad = zero_projection_grad(
        order, dp_order, 0, cots[:2], cots_other[:2], stacks[:2], None, "zero_projection_grad_first"
    )
    zero_grad = zero_projection_grad(
        order, dp_order, 2, cots[2:], cots_other[2:], stacks[2:], zero_grad, "zero_projection_grad_last"
    )
    return (block_rows[None], (up_rows + back)[None], zero_grad)


def solution(mesh):
    placed = (
        P("grp", None, "dp"),
        P("grp", None, None),
        P("grp", "fsdp", None),
        P("grp", "fsdp", None),
        P("fsdp", None),
        P("grp", "fsdp", "dp"),
    )
    return jax.shard_map(
        local,
        mesh=mesh,
        in_specs=placed,
        out_specs=(P("grp", "fsdp", "dp"), P("grp", "fsdp", "dp"), P("fsdp", None)),
        check_vma=False,
    )
```

```python
import functools

import jax
import jax.numpy as jnp
from jax import lax
from jax.experimental import pallas as pl
from jax.experimental.pallas import tpu as pltpu
from jax.sharding import PartitionSpec as P

EPSILON = 1e-06
SQRT_2_OVER_PI = 0.7978845608028654
CHUNK = 512
AHEAD = 3
MIB = 1024 * 1024
F32, BF16 = jnp.float32, jnp.bfloat16
WHOLE = pl.BlockSpec(memory_space=pltpu.VMEM)
HELD = pl.BlockSpec(memory_space=pltpu.HBM)
SCALARS = pl.BlockSpec(memory_space=pltpu.SMEM)


def pieces(start, stop, size=CHUNK):
    return [(at, min(size, stop - at)) for at in range(start, stop, size)]


def split_rows(hidden):
    units = hidden // CHUNK
    return CHUNK * max(units // 2, 1), (hidden - 1) // CHUNK * CHUNK


def after(value, *others):
    return lax.optimization_barrier((value,) + others)[0]


def swap_grp(value):
    return lax.ppermute(value, "grp", [(0, 1), (1, 0)])


def stages():
    return (lax.axis_size("fsdp") - 1).bit_length()


def step(value, stage):
    length, bits = lax.axis_size("fsdp"), stages()
    pairs = []
    for group, bit in ((0, stage), (1, bits - 1 - stage)):
        pairs += [(group * length + i, group * length + (i ^ (1 << bit))) for i in range(length)]
    return lax.ppermute(value, ("grp", "fsdp"), pairs)


def block_order(group, me):
    length, bits = lax.axis_size("fsdp"), stages()
    turned = [sum(((v >> b) & 1) << (bits - 1 - b) for b in range(bits)) for v in range(length)]
    up, down = jnp.arange(length, dtype=jnp.int32), jnp.array(turned, jnp.int32)
    return me ^ jnp.where(group == 0, up, down)


def send(value, place):
    length, bits = lax.axis_size("fsdp"), stages()
    turned = sum(((place >> b) & 1) << (bits - 1 - b) for b in range(bits))
    pairs = []
    for group, mask in ((0, place), (1, turned)):
        pairs += [(group * length + i, group * length + (i ^ mask)) for i in range(length)]
    return lax.ppermute(value, ("grp", "fsdp"), pairs)


def gather_dp(value):
    length = lax.axis_size("dp")
    return [value] + [
        lax.ppermute(value, "dp", [(i, i ^ mask) for i in range(length)]) for mask in range(1, length)
    ]


def block_of(value, index, rows):
    return lax.dynamic_slice_in_dim(value, index * rows, rows, 0)


def split_three(value):
    high = value.astype(BF16)
    rest = value - high.astype(F32)
    mid = rest.astype(BF16)
    return high, mid, (rest - mid.astype(F32)).astype(BF16)


def pack_sums(plain, along):
    tail = [part.astype(F32) for part in split_three(plain) + split_three(along)]
    return jnp.concatenate(tail + [jnp.zeros((10, plain.shape[1]), F32)], 0).astype(BF16)


def unpack_sums(tail):
    tail = tail.astype(F32)
    return tail[0:1] + tail[1:2] + tail[2:3], tail[3:4] + tail[4:5] + tail[5:6]


def gelu_and_slope(v):
    square = v * v
    t = jnp.tanh(SQRT_2_OVER_PI * (v + 0.044715 * (square * v)))
    rise = 0.5 * (1.0 + t)
    slope = rise + 0.5 * v * (1.0 - t * t) * (SQRT_2_OVER_PI * (1.0 + (3 * 0.044715) * square))
    return v * rise, slope


class Stream:
    def __init__(self, first, first_buf, second, second_buf, parts, base, sems):
        def copy(weight, buf, part):
            return weight.at[0, pl.ds(part[0], part[1]), :], buf.at[pl.ds(part[0] - base, part[1]), :]

        pairs = [copy(first, first_buf, parts[0])]
        for k, part in enumerate(parts):
            if k + 1 < len(parts):
                pairs.append(copy(first, first_buf, parts[k + 1]))
            pairs.append(copy(second, second_buf, part))
        self.copies = [pltpu.make_async_copy(a, b, sems.at[k]) for k, (a, b) in enumerate(pairs)]
        self.next = 0
        for item in self.copies[:AHEAD]:
            item.start()

    def take(self):
        k = self.next
        self.copies[k].wait()
        if k + AHEAD < len(self.copies):
            self.copies[k + AHEAD].start()
        self.next = k + 1


def pipelined(parts, product, finish):
    held = None
    for part in parts:
        value = product(*part)
        if held is not None:
            finish(*held, False)
        held = part + (value,)
    finish(*held, True)


def params(flops, moved, transcendentals=0, grant=50):
    return dict(
        compiler_params=pltpu.CompilerParams(vmem_limit_bytes=grant * MIB),
        cost_estimate=pl.CostEstimate(flops=flops, bytes_accessed=moved, transcendentals=transcendentals),
    )


def struct(shape, dtype):
    return jax.ShapeDtypeStruct(shape, dtype)


def staging(rows, features, lanes):
    return pltpu.VMEM((features, lanes) if rows % 16 else (8, 128), F32)


def place_blocks(target, lanes, stage, order, blocks, rows, first=0):
    for place, value in enumerate(blocks):
        if rows % 16:
            stage[pl.ds(pl.multiple_of(order[first + place] * rows, 8), rows), :] = value().astype(F32)
        else:
            target[pl.ds(pl.multiple_of(order[first + place] * rows, 16), rows), lanes] = value()
    if rows % 16:
        target[:, lanes] = stage[...].astype(target.dtype)


def turn_modulation(modulation, columns):
    for start, size in pieces(0, modulation.shape[2], 128):
        rows = modulation[0, :, pl.ds(start, size)]
        columns[pl.ds(start, size), :] = jnp.concatenate([rows, jnp.zeros((5, size), F32)], 0).T


def normalize(acts, modulation, normed, stats):
    features, tokens = acts.shape[1:]
    parts = pieces(0, features, 128)
    total = jnp.zeros((1, tokens), F32)
    for start, size in parts:
        total += jnp.sum(acts[0, pl.ds(start, size), :].astype(F32), 0, keepdims=True)
    mean = total / features
    total = jnp.zeros((1, tokens), F32)
    for start, size in parts:
        centred = acts[0, pl.ds(start, size), :].astype(F32) - mean
        total += jnp.sum(centred * centred, 0, keepdims=True)
    inv = lax.rsqrt(total / features + EPSILON)
    stats[0:1, :] = mean
    stats[1:2, :] = inv
    for start, size in parts:
        rows = pl.ds(start, size)
        xhat = (acts[0, rows, :].astype(F32) - mean) * inv
        shift, scale = modulation[0, 0:1, rows], modulation[0, 1:2, rows]
        normed[:, rows] = (xhat.T * (1.0 + scale) + shift).astype(BF16)


def against_rows(columns, weight):
    return lax.dot_general(columns, weight, (((1,), (1,)), ((), ())), preferred_element_type=F32)


def accumulate(total, part, weight, before, finish):
    for at, size in pieces(0, weight.shape[1]):
        columns = pl.ds(at, size)
        value = jnp.dot(part, weight[:, columns], preferred_element_type=F32)
        if before is not None:
            value = value + before[:, columns]
        if finish is None:
            total[:, columns] = value
        else:
            finish(at, size, value)


def forward_products(stream, parts, base, normed, in_buf, out_buf, slope_out, total, before, last):
    state = [before]

    def product(at, size):
        stream.take()
        return against_rows(normed[...], in_buf[pl.ds(at - base, size), :])

    def finish(at, size, pre, final):
        rows = pl.ds(at - base, size)
        hidden, slope = gelu_and_slope(pre)
        slope_out[:, rows] = slope
        stream.take()
        accumulate(total, hidden.astype(BF16), out_buf.at[rows, :], state[0], last if final else None)
        state[0] = total

    pipelined(parts, product, finish)


def forward_first_kernel(normed, modulation, w_in, w_out, slope_out, total, mod, in_buf, out_buf, sems):
    parts = pieces(0, slope_out.shape[1])
    stream = Stream(w_in, in_buf, w_out, out_buf, parts, 0, sems)
    turn_modulation(modulation, mod)
    forward_products(stream, parts, 0, normed, in_buf, out_buf, slope_out, total, None, None)


def forward_last_kernel(start, order, normed, before, w_in, w_out, slope_out, *refs):
    outs, (in_buf, out_buf, total, full, sems) = refs[:-5], refs[-5:]
    parts = pieces(start, start + slope_out.shape[1])
    stream = Stream(w_in, in_buf, w_out, out_buf, parts, start, sems)

    def last(at, size, value):
        full[pl.ds(at, size), :] = value.T

    forward_products(stream, parts, start, normed, in_buf, out_buf, slope_out, total, before, last)
    write_blocks(order, full, outs)


def layer_scratch(part, features):
    return [
        pltpu.VMEM((part, features), BF16),
        pltpu.VMEM((part, features), BF16),
    ]


def layer_params(part, features, tokens, transcendentals):
    return params(4 * part * features * tokens, 4 * part * features + 4 * features * tokens, transcendentals)


def forward_first(normed, modulation, w_in, w_out, part, name):
    tokens, features = normed.shape
    return pl.pallas_call(
        forward_first_kernel,
        out_shape=(struct((tokens, part), F32), struct((tokens, features), F32), struct((features, 8), F32)),
        in_specs=[WHOLE, WHOLE, HELD, HELD],
        out_specs=[WHOLE] * 3,
        scratch_shapes=layer_scratch(part, features) + [pltpu.SemaphoreType.DMA((2 * len(pieces(0, part)),))],
        name=name,
        **layer_params(part, features, tokens, part * tokens),
    )(normed, modulation, w_in, w_out)


def forward_last(order, normed, before, w_in, w_out, start, blocks, name):
    hidden, features = w_in.shape[1:]
    tokens, part, rows = before.shape[0], hidden - start, features // blocks
    slope, *outs = pl.pallas_call(
        functools.partial(forward_last_kernel, start),
        out_shape=[struct((tokens, part), F32), struct((rows, tokens), F32)]
        + [struct((rows, tokens), BF16)] * (blocks - 1),
        in_specs=[SCALARS, WHOLE, WHOLE, HELD, HELD],
        out_specs=[WHOLE] * (blocks + 1),
        scratch_shapes=layer_scratch(part, features)
        + [
            pltpu.VMEM((tokens, features), F32),
            pltpu.VMEM((features, tokens), F32),
            pltpu.SemaphoreType.DMA((2 * len(pieces(start, hidden)),)),
        ],
        name=name,
        **layer_params(part, features, tokens, part * tokens),
    )(order, normed, before, w_in, w_out)
    return slope, outs[0], outs[1:]


def write_blocks(order, full, outs):
    for place, target in enumerate(outs):
        rows = target.shape[0]
        offset = pl.multiple_of(order[place] * rows, 8)
        target[...] = full[pl.ds(offset, rows), :].astype(target.dtype)


def backward_products(stream, parts, base, grad, slopes, in_buf, out_buf, total, before, last):
    state = [before]

    def product(at, size):
        stream.take()
        return against_rows(grad[...], out_buf[pl.ds(at - base, size), :])

    def finish(at, size, value, final):
        rows = pl.ds(at - base, size)
        seen = slopes[0].shape[1]
        slope = slopes[0][:, pl.ds(at, size)] if at < seen else slopes[1][:, pl.ds(at - seen, size)]
        stream.take()
        accumulate(total, (value * slope).astype(BF16), in_buf.at[rows, :], state[0], last if final else None)
        state[0] = total

    pipelined(parts, product, finish)


def backward_first_kernel(blocks, part, order, *refs):
    pieces_in, (slope_a, slope_b, w_in, w_out, grad, total, in_buf, out_buf, full, stage, sems) = refs[:blocks], refs[blocks:]
    parts = pieces(0, part)
    stream = Stream(w_out, out_buf, w_in, in_buf, parts, 0, sems)
    values = [lambda ref=ref: ref[...] for ref in pieces_in]
    place_blocks(full, slice(None), stage, order, values, pieces_in[0].shape[0])
    for start, size in pieces(0, full.shape[0], 128):
        rows = pl.ds(start, size)
        grad[:, rows] = full[rows, :].astype(F32).T.astype(BF16)
    backward_products(stream, parts, 0, grad, (slope_a, slope_b), in_buf, out_buf, total, None, None)


def backward_first(order, gathered, slope_a, slope_b, w_in, w_out, part, name):
    hidden, features = w_in.shape[1:]
    blocks, (rows, tokens) = len(gathered), gathered[0].shape
    return pl.pallas_call(
        functools.partial(backward_first_kernel, blocks, part),
        out_shape=(struct((tokens, features), BF16), struct((tokens, features), F32)),
        in_specs=[SCALARS] + [WHOLE] * (blocks + 2) + [HELD, HELD],
        out_specs=[WHOLE] * 2,
        scratch_shapes=layer_scratch(part, features)
        + [
            pltpu.VMEM((features, tokens), BF16),
            staging(rows, features, tokens),
            pltpu.SemaphoreType.DMA((2 * len(pieces(0, part)),)),
        ],
        name=name,
        **layer_params(part, features, tokens, 0),
    )(order, *gathered, slope_a, slope_b, w_in, w_out)


def backward_last_kernel(start, rows, order, grad, before, slope_a, slope_b, acts, stats, mod, w_in, w_out, *refs):
    outs, (sums_out, in_buf, out_buf, total, full, sems) = refs[:-6], refs[-6:]
    hidden, (features, tokens) = w_in.shape[1], full.shape
    parts = pieces(start, hidden)
    stream = Stream(w_out, out_buf, w_in, in_buf, parts, start, sems)
    mean, inv = stats[0:1, :], stats[1:2, :]
    sums = [jnp.zeros((1, tokens), F32), jnp.zeros((1, tokens), F32)]

    def last(at, size, value):
        at = pl.ds(at, size)
        value = value.T
        full[at, :] = value
        scaled = value * (1.0 + mod[at, 1:2])
        xhat = (acts[0, at, :].astype(F32) - mean) * inv
        sums[0] += jnp.sum(scaled, 0, keepdims=True)
        sums[1] += jnp.sum(scaled * xhat, 0, keepdims=True)

    backward_products(stream, parts, start, grad, (slope_a, slope_b), in_buf, out_buf, total, before, last)
    count = len(outs) // 2
    padded = outs[0].shape[0] - 16
    tail = pack_sums(*sums)
    for place in range(count):
        offset = pl.multiple_of(order[2 * place] * rows, 8)
        outs[count + place][...] = full[pl.ds(offset, rows), :]
        offset = pl.multiple_of(order[2 * place + 1] * rows, 8)
        block = full[pl.ds(offset, rows), :]
        if padded > rows:
            block = jnp.concatenate([block, jnp.zeros((padded - rows, tokens), F32)], 0)
        outs[place][:padded, :] = block.astype(BF16)
        outs[place][padded:, :] = tail
    sums_out[0:1, :] = sums[0]
    sums_out[1:2, :] = sums[1]


def backward_last(order, grad, before, slope_a, slope_b, acts, stats, mod, w_in, w_out, start, blocks, name):
    hidden, features = w_in.shape[1:]
    tokens, part, rows, count = before.shape[0], hidden - start, features // blocks, blocks // 2
    outs = pl.pallas_call(
        functools.partial(backward_last_kernel, start, rows),
        out_shape=[struct((-(-rows // 16) * 16 + 16, tokens), BF16)] * count
        + [struct((rows, tokens), F32)] * count
        + [struct((2, tokens), F32)],
        in_specs=[SCALARS] + [WHOLE] * 7 + [HELD, HELD],
        out_specs=[WHOLE] * (blocks + 1),
        scratch_shapes=layer_scratch(part, features)
        + [
            pltpu.VMEM((tokens, features), F32),
            pltpu.VMEM((features, tokens), F32),
            pltpu.SemaphoreType.DMA((2 * len(pieces(start, hidden)),)),
        ],
        name=name,
        **layer_params(part, features, tokens, 0),
    )(order, grad, before, slope_a, slope_b, acts, stats, mod, w_in, w_out)
    return outs[:count], outs[count:-1], outs[-1]


def fold_kernel(rows, count, *refs):
    got, kept, (sums, *outs) = refs[:count], refs[count : 2 * count], refs[2 * count :]
    more = unpack_sums(got[0][-16:, :])
    plain, along = sums[0:1, :] + more[0], sums[1:2, :] + more[1]
    tail = pack_sums(plain, along)
    padded = got[0].shape[0] - 16
    for place in range(count // 2):
        even, odd = 2 * place, 2 * place + 1
        outs[count // 2 + place][...] = kept[even][...] + got[even][:rows, :].astype(F32)
        block = kept[odd][...] + got[odd][:rows, :].astype(F32)
        if padded > rows:
            block = jnp.concatenate([block, jnp.zeros((padded - rows, block.shape[1]), F32)], 0)
        outs[place][:padded, :] = block.astype(BF16)
        outs[place][padded:, :] = tail
    outs[-1][0:1, :] = plain
    outs[-1][1:2, :] = along


def fold(got, kept, sums):
    count, (rows, tokens) = len(kept), kept[0].shape
    outs = pl.pallas_call(
        functools.partial(fold_kernel, rows, count),
        out_shape=[struct(got[0].shape, BF16)] * (count // 2)
        + [struct((rows, tokens), F32)] * (count // 2)
        + [struct((2, tokens), F32)],
        in_specs=[WHOLE] * (2 * count + 1),
        out_specs=[WHOLE] * (count + 1),
        name="fold",
        **params(2 * count * rows * tokens, 8 * count * rows * tokens, grant=12),
    )(*got, *kept, sums)
    return outs[: count // 2], outs[count // 2 : -1], outs[-1]


def prepare_kernel(blocks, order, acts, modulation, own, arrived, weight, *refs):
    outs, (normed, stats, cot0, cot1, full, buf, sem) = refs[:blocks], refs[blocks:]
    load = pltpu.make_async_copy(weight, buf, sem)
    load.start()
    group = order[blocks]
    control = group == 0
    half = cot0.shape[1]
    lanes = pl.ds(pl.multiple_of(group * half, half), half)
    cot0[...] = jnp.where(control, own[:, lanes], arrived[:, lanes])
    mine = jnp.where(control, arrived[:, lanes], own[:, lanes])
    cot1[...] = mine
    normalize(acts, modulation, normed, stats)
    load.wait()
    full[...] = lax.dot_general(mine, buf[...], (((0,), (0,)), ((), ())), preferred_element_type=F32).T
    write_blocks(order, full, outs)


def prepare(order, acts, modulation, own, arrived, weight, blocks):
    rows, tokens = own.shape
    half, features = tokens // 2, weight.shape[1]
    outs = pl.pallas_call(
        functools.partial(prepare_kernel, blocks),
        out_shape=[struct((rows, half), F32)]
        + [struct((rows, half), BF16)] * (blocks - 1)
        + [
            struct((tokens, features), BF16),
            struct((2, tokens), F32),
            struct((rows, half), BF16),
            struct((rows, half), BF16),
        ],
        in_specs=[SCALARS] + [WHOLE] * 4 + [HELD],
        out_specs=[WHOLE] * (blocks + 4),
        scratch_shapes=[
            pltpu.VMEM((features, half), F32),
            pltpu.VMEM(weight.shape, BF16),
            pltpu.SemaphoreType.DMA(()),
        ],
        name="prepare",
        **params(2 * weight.size * half, 2 * weight.size + 4 * blocks * rows * half, grant=50),
    )(order, acts, modulation, own, arrived, weight)
    return outs[0], outs[1:blocks], *outs[blocks:]


def residual_kernel(order, weight, *refs):
    stack, (result, full, stage) = refs[:-3], refs[-3:]
    values = [lambda value=value: value[...] for value in stack]
    place_blocks(full, slice(None), stage, order, values, stack[0].shape[0])
    result[...] = jnp.dot(weight[...], full[...], preferred_element_type=F32)


def residual_rows(order, weight, stack):
    blocks, (rows, half) = len(stack), stack[0].shape
    return pl.pallas_call(
        residual_kernel,
        out_shape=struct((rows, half), F32),
        in_specs=[SCALARS] + [WHOLE] * (blocks + 1),
        out_specs=WHOLE,
        scratch_shapes=[pltpu.VMEM((blocks * rows, half), BF16), staging(rows, blocks * rows, half)],
        name="residual_rows",
        **params(2 * weight.size * half, 2 * weight.size + 4 * blocks * rows * half, grant=12),
    )(order, weight, *stack)


def zero_grad_kernel(blocks, first, count, order, dp_order, *refs):
    cots, refs = (refs[:count], refs[count : 2 * count]), refs[2 * count :]
    stacks = []
    while len(refs) > (9 if first else 6):
        stacks.append((refs[:blocks], refs[blocks : 2 * blocks]))
        refs = refs[2 * blocks :]
    before = None
    if first:
        before, out, lhs, rhs, stage, parked, loads, buf, sems = refs
    else:
        buf, lhs, rhs, stage, parked, loads = refs
    rows, half = cots[0][0].shape
    group = order[blocks]
    moves, places = [], []
    for part in range(count):
        slot = part // 2 * 2 + (dp_order[first + part] & 1)
        for side, owner in enumerate((group, 1 - group)):
            lanes = pl.ds(pl.multiple_of((slot * 2 + owner) * half, half), half)
            moves.append((cots[side][part], lhs.at[:, lanes]))
            values = []
            for place in range(blocks):
                source = stacks[part][side][place] if len(stacks) == count else stacks[0][side][place].at[part]
                if rows % 16:
                    at = (part * 2 + side) * blocks + place
                    target = parked.at[at]
                    values.append(lambda at=at: parked[at])
                else:
                    offset = pl.multiple_of(order[side * (blocks + 1) + place] * rows, 16)
                    target = rhs.at[pl.ds(offset, rows), lanes]
                moves.append((source, target))
            places.append((lanes, values, side * (blocks + 1)))
    moves = [pltpu.make_async_copy(a, b, loads.at[k]) for k, (a, b) in enumerate(moves)]
    for move in moves:
        move.start()
    for move in moves:
        move.wait()
    if rows % 16:
        for lanes, values, shift in places:
            place_blocks(rhs, lanes, stage, order, values, rows, shift)
    copies = []
    for k, (start, size) in enumerate(pieces(0, blocks * rows)):
        columns = pl.ds(start, size)
        value = against_rows(lhs[...], rhs[columns, :])
        buf[:, columns] = value if before is None else before[:, columns] + value
        if before is not None:
            copies.append(pltpu.make_async_copy(buf.at[:, columns], out.at[:, columns], sems.at[k]))
            copies[-1].start()
    for copy in copies:
        copy.wait()


def zero_projection_grad(order, dp_order, first, cots, cots_other, stacks, before, name):
    blocks, (rows, half) = len(stacks[0][0]), cots[0].shape
    count = len(cots)
    features, tokens = blocks * rows, count * 2 * half
    flat = [block for pair in stacks for side in pair for block in side]
    extra = [] if before is None else [before]
    scratch = [
        pltpu.VMEM((rows, tokens), BF16),
        pltpu.VMEM((features, tokens), BF16),
        staging(rows, features, half),
        pltpu.VMEM((count * 2 * blocks, rows, half) if rows % 16 else (1, 8, 128), BF16),
        pltpu.SemaphoreType.DMA((count * 2 * (blocks + 1),)),
    ]
    if extra:
        scratch += [
            pltpu.VMEM((rows, features), F32),
            pltpu.SemaphoreType.DMA((len(pieces(0, features)),)),
        ]
    return pl.pallas_call(
        functools.partial(zero_grad_kernel, blocks, first, count),
        out_shape=struct((rows, features), F32),
        in_specs=[SCALARS] * 2 + [HELD] * (2 * count + len(flat)) + [WHOLE] * len(extra),
        out_specs=HELD if extra else WHOLE,
        scratch_shapes=scratch,
        name=name,
        **params(2 * tokens * rows * features, 4 * rows * features + 2 * tokens * (rows + features), grant=28),
    )(order, dp_order, *cots, *cots_other, *flat, *extra)


def steps(values, level, *during):
    got = [step(value, level) for value in values]
    return list(lax.optimization_barrier((tuple(got),) + during)[0]) if during else got


def direct(values, *during):
    got = [send(value, place + 1) for place, value in enumerate(values)]
    return list(lax.optimization_barrier((tuple(got),) + during)[0])


def local(acts, modulation, w_in, w_out, zero_weight, cotangent):
    own_cot = cotangent[0]
    features, tokens = acts.shape[1:]
    hidden = w_in.shape[1]
    rows = own_cot.shape[0]
    half = tokens // 2
    blocks, levels = lax.axis_size("fsdp"), stages()
    parts = lax.axis_size("dp")
    group = lax.axis_index("grp").astype(jnp.int32)
    me = lax.axis_index("fsdp").astype(jnp.int32)
    is_control = group == 0
    places = block_order(group, me)
    order = jnp.concatenate([places, group[None], block_order(1 - group, me)])
    dp_order = lax.axis_index("dp").astype(jnp.int32) ^ jnp.arange(parts, dtype=jnp.int32)

    arrived = swap_grp(own_cot)
    own_term, sent, normed, stats, cot0, cot1 = prepare(
        order, acts, modulation, own_cot, arrived, zero_weight, blocks
    )
    split, cut = split_rows(hidden)
    slope_a, total, mod = forward_first(after(normed, *sent), modulation, w_in, w_out, split, "forward_first")
    own_mod = block_of(mod, me, rows)
    own_gate = own_mod[:, 2:3]
    got = direct(sent, total)
    up_half = own_term + cot0.astype(F32) + sum(value.astype(F32) for value in got)
    up_rows = jnp.where(is_control, jnp.concatenate([up_half, swap_grp(up_half)], 1), own_cot.astype(F32))
    grad_rows = (own_gate * up_rows).astype(BF16)

    slope_b, kept, sent = forward_last(
        order, after(normed, grad_rows), total, w_in, w_out, split, blocks, "forward_last"
    )
    gathered = [grad_rows] + direct([grad_rows] * (blocks - 1), kept)
    grad, total = backward_first(
        order, after(gathered, *sent), slope_a, slope_b, w_in, w_out, cut, "backward_first"
    )
    got = direct(sent, total)
    own_values = block_of(acts[0], me, rows).astype(F32)
    sums = own_values + own_gate * (kept + sum(value.astype(F32) for value in got))
    out_rows = sums.astype(BF16)

    out_half = jnp.where(is_control, out_rows[:, :half], swap_grp(out_rows[:, half:]))
    far = gather_dp(out_half)[1:]
    sent, kept, token_sums = backward_last(
        order, after(grad, out_half), total, slope_a, slope_b, acts, stats, mod, w_in, w_out, cut, blocks, "backward_last"
    )
    near = [out_half, step(out_half, 0)]
    far, near, sent, kept, token_sums = lax.optimization_barrier((far, near, sent, kept, token_sums))
    for level in range(1, levels):
        near = near + steps(near, level)
    near_other = [swap_grp(value) for value in near]
    residual = residual_rows(order, zero_weight, near)
    cots = gather_dp(after(cot1, token_sums))
    cots_other = [swap_grp(value) for value in cots]

    gathers = [[far[0]], [jnp.stack(far[1:])]]
    for level in range(levels):
        got = steps(sent, level)
        gathers = [blocks_so_far + steps(blocks_so_far, level) for blocks_so_far in gathers]
        if level + 1 < levels:
            sent, kept, token_sums = fold(got, kept, token_sums)
    more = unpack_sums(got[0][-16:])
    plain, along = token_sums[0:1] + more[0], token_sums[1:2] + more[1]
    kept = [kept[0] + got[0][:rows].astype(F32)]
    mean, inv = stats[0:1], stats[1:2]
    back = inv * (
        kept[0] * (1.0 + own_mod[:, 1:2]) - plain / features - (own_values - mean) * inv * (along / features)
    )
    residual = jnp.concatenate([swap_grp(residual), residual], 1)
    block_rows = jnp.where(is_control, out_rows, (sums + residual).astype(BF16))

    stacks = [(near, near_other)] + [(mine, [swap_grp(value) for value in mine]) for mine in gathers]
    zero_grad = zero_projection_grad(
        order, dp_order, 0, cots[:2], cots_other[:2], stacks[:2], None, "zero_projection_grad_first"
    )
    zero_grad = zero_projection_grad(
        order, dp_order, 2, cots[2:], cots_other[2:], stacks[2:], zero_grad, "zero_projection_grad_last"
    )
    return (block_rows[None], (up_rows + back)[None], zero_grad)


def solution(mesh):
    placed = (
        P("grp", None, "dp"),
        P("grp", None, None),
        P("grp", "fsdp", None),
        P("grp", "fsdp", None),
        P("fsdp", None),
        P("grp", "fsdp", "dp"),
    )
    return jax.shard_map(
        local,
        mesh=mesh,
        in_specs=placed,
        out_specs=(P("grp", "fsdp", "dp"), P("grp", "fsdp", "dp"), P("fsdp", None)),
        check_vma=False,
    )
```

```python
import functools

import jax
import jax.numpy as jnp
from jax import lax
from jax.experimental import pallas as pl
from jax.experimental.pallas import tpu as pltpu
from jax.sharding import PartitionSpec as P

EPSILON = 1e-06
SQRT_2_OVER_PI = 0.7978845608028654
CHUNK = 512
AHEAD = 3
MIB = 1024 * 1024
F32, BF16 = jnp.float32, jnp.bfloat16
WHOLE = pl.BlockSpec(memory_space=pltpu.VMEM)
HELD = pl.BlockSpec(memory_space=pltpu.HBM)
SCALARS = pl.BlockSpec(memory_space=pltpu.SMEM)


def pieces(start, stop, size=CHUNK):
    return [(at, min(size, stop - at)) for at in range(start, stop, size)]


def split_rows(hidden):
    units = hidden // CHUNK
    return CHUNK * max(units // 2, 1), (hidden - 1) // CHUNK * CHUNK


def after(value, *others):
    return lax.optimization_barrier((value,) + others)[0]


def swap_grp(value):
    return lax.ppermute(value, "grp", [(0, 1), (1, 0)])


def stages():
    return (lax.axis_size("fsdp") - 1).bit_length()


def step(value, stage):
    length, bits = lax.axis_size("fsdp"), stages()
    pairs = []
    for group, bit in ((0, stage), (1, bits - 1 - stage)):
        pairs += [(group * length + i, group * length + (i ^ (1 << bit))) for i in range(length)]
    return lax.ppermute(value, ("grp", "fsdp"), pairs)


def block_order(group, me):
    length, bits = lax.axis_size("fsdp"), stages()
    turned = [sum(((v >> b) & 1) << (bits - 1 - b) for b in range(bits)) for v in range(length)]
    up, down = jnp.arange(length, dtype=jnp.int32), jnp.array(turned, jnp.int32)
    return me ^ jnp.where(group == 0, up, down)


def send(value, place):
    length, bits = lax.axis_size("fsdp"), stages()
    turned = sum(((place >> b) & 1) << (bits - 1 - b) for b in range(bits))
    pairs = []
    for group, mask in ((0, place), (1, turned)):
        pairs += [(group * length + i, group * length + (i ^ mask)) for i in range(length)]
    return lax.ppermute(value, ("grp", "fsdp"), pairs)


def gather_dp(value):
    length = lax.axis_size("dp")
    return [value] + [
        lax.ppermute(value, "dp", [(i, i ^ mask) for i in range(length)]) for mask in range(1, length)
    ]


def block_of(value, index, rows):
    return lax.dynamic_slice_in_dim(value, index * rows, rows, 0)


def split_three(value):
    high = value.astype(BF16)
    rest = value - high.astype(F32)
    mid = rest.astype(BF16)
    return high, mid, (rest - mid.astype(F32)).astype(BF16)


def pack_sums(plain, along):
    tail = [part.astype(F32) for part in split_three(plain) + split_three(along)]
    return jnp.concatenate(tail + [jnp.zeros((10, plain.shape[1]), F32)], 0).astype(BF16)


def unpack_sums(tail):
    tail = tail.astype(F32)
    return tail[0:1] + tail[1:2] + tail[2:3], tail[3:4] + tail[4:5] + tail[5:6]


def gelu_and_slope(v):
    square = v * v
    t = jnp.tanh(SQRT_2_OVER_PI * (v + 0.044715 * (square * v)))
    rise = 0.5 * (1.0 + t)
    slope = rise + 0.5 * v * (1.0 - t * t) * (SQRT_2_OVER_PI * (1.0 + (3 * 0.044715) * square))
    return v * rise, slope


class Stream:
    def __init__(self, first, first_buf, second, second_buf, parts, base, sems):
        def copy(weight, buf, part):
            return weight.at[0, pl.ds(part[0], part[1]), :], buf.at[pl.ds(part[0] - base, part[1]), :]

        pairs = [copy(first, first_buf, parts[0])]
        for k, part in enumerate(parts):
            if k + 1 < len(parts):
                pairs.append(copy(first, first_buf, parts[k + 1]))
            pairs.append(copy(second, second_buf, part))
        self.copies = [pltpu.make_async_copy(a, b, sems.at[k]) for k, (a, b) in enumerate(pairs)]
        self.next = 0
        for item in self.copies[:AHEAD]:
            item.start()

    def take(self):
        k = self.next
        self.copies[k].wait()
        if k + AHEAD < len(self.copies):
            self.copies[k + AHEAD].start()
        self.next = k + 1


def pipelined(parts, product, finish):
    held = None
    for part in parts:
        value = product(*part)
        if held is not None:
            finish(*held, False)
        held = part + (value,)
    finish(*held, True)


def params(flops, moved, transcendentals=0, grant=50):
    return dict(
        compiler_params=pltpu.CompilerParams(vmem_limit_bytes=grant * MIB),
        cost_estimate=pl.CostEstimate(flops=flops, bytes_accessed=moved, transcendentals=transcendentals),
    )


def struct(shape, dtype):
    return jax.ShapeDtypeStruct(shape, dtype)


def staging(rows, features, lanes):
    return pltpu.VMEM((features, lanes) if rows % 16 else (8, 128), F32)


def place_blocks(target, lanes, stage, order, blocks, rows, first=0):
    for place, value in enumerate(blocks):
        if rows % 16:
            stage[pl.ds(pl.multiple_of(order[first + place] * rows, 8), rows), :] = value().astype(F32)
        else:
            target[pl.ds(pl.multiple_of(order[first + place] * rows, 16), rows), lanes] = value()
    if rows % 16:
        target[:, lanes] = stage[...].astype(target.dtype)


def turn_modulation(modulation, columns):
    for start, size in pieces(0, modulation.shape[2], 128):
        rows = modulation[0, :, pl.ds(start, size)]
        columns[pl.ds(start, size), :] = jnp.concatenate([rows, jnp.zeros((5, size), F32)], 0).T


def normalize(acts, modulation, normed, stats):
    features, tokens = acts.shape[1:]
    parts = pieces(0, features, 128)
    total = jnp.zeros((1, tokens), F32)
    for start, size in parts:
        total += jnp.sum(acts[0, pl.ds(start, size), :].astype(F32), 0, keepdims=True)
    mean = total / features
    total = jnp.zeros((1, tokens), F32)
    for start, size in parts:
        centred = acts[0, pl.ds(start, size), :].astype(F32) - mean
        total += jnp.sum(centred * centred, 0, keepdims=True)
    inv = lax.rsqrt(total / features + EPSILON)
    stats[0:1, :] = mean
    stats[1:2, :] = inv
    for start, size in parts:
        rows = pl.ds(start, size)
        xhat = (acts[0, rows, :].astype(F32) - mean) * inv
        shift, scale = modulation[0, 0:1, rows], modulation[0, 1:2, rows]
        normed[:, rows] = (xhat.T * (1.0 + scale) + shift).astype(BF16)


def against_rows(columns, weight):
    return lax.dot_general(columns, weight, (((1,), (1,)), ((), ())), preferred_element_type=F32)


def accumulate(total, part, weight, before, finish):
    for at, size in pieces(0, weight.shape[1]):
        columns = pl.ds(at, size)
        value = jnp.dot(part, weight[:, columns], preferred_element_type=F32)
        if before is not None:
            value = value + before[:, columns]
        if finish is None:
            total[:, columns] = value
        else:
            finish(at, size, value)


def forward_products(stream, parts, base, normed, in_buf, out_buf, slope_out, total, before, last):
    state = [before]

    def product(at, size):
        stream.take()
        return against_rows(normed[...], in_buf[pl.ds(at - base, size), :])

    def finish(at, size, pre, final):
        rows = pl.ds(at - base, size)
        hidden, slope = gelu_and_slope(pre)
        slope_out[:, rows] = slope
        stream.take()
        accumulate(total, hidden.astype(BF16), out_buf.at[rows, :], state[0], last if final else None)
        state[0] = total

    pipelined(parts, product, finish)


def forward_first_kernel(normed, modulation, w_in, w_out, slope_out, total, mod, in_buf, out_buf, sems):
    parts = pieces(0, slope_out.shape[1])
    stream = Stream(w_in, in_buf, w_out, out_buf, parts, 0, sems)
    turn_modulation(modulation, mod)
    forward_products(stream, parts, 0, normed, in_buf, out_buf, slope_out, total, None, None)


def forward_last_kernel(start, order, normed, before, w_in, w_out, slope_out, *refs):
    outs, (in_buf, out_buf, total, full, sems) = refs[:-5], refs[-5:]
    parts = pieces(start, start + slope_out.shape[1])
    stream = Stream(w_in, in_buf, w_out, out_buf, parts, start, sems)

    def last(at, size, value):
        full[pl.ds(at, size), :] = value.T

    forward_products(stream, parts, start, normed, in_buf, out_buf, slope_out, total, before, last)
    write_blocks(order, full, outs)


def layer_scratch(part, features):
    return [
        pltpu.VMEM((part, features), BF16),
        pltpu.VMEM((part, features), BF16),
    ]


def layer_params(part, features, tokens, transcendentals):
    return params(4 * part * features * tokens, 4 * part * features + 4 * features * tokens, transcendentals)


def forward_first(normed, modulation, w_in, w_out, part, name):
    tokens, features = normed.shape
    return pl.pallas_call(
        forward_first_kernel,
        out_shape=(struct((tokens, part), F32), struct((tokens, features), F32), struct((features, 8), F32)),
        in_specs=[WHOLE, WHOLE, HELD, HELD],
        out_specs=[WHOLE] * 3,
        scratch_shapes=layer_scratch(part, features) + [pltpu.SemaphoreType.DMA((2 * len(pieces(0, part)),))],
        name=name,
        **layer_params(part, features, tokens, part * tokens),
    )(normed, modulation, w_in, w_out)


def forward_last(order, normed, before, w_in, w_out, start, blocks, name):
    hidden, features = w_in.shape[1:]
    tokens, part, rows = before.shape[0], hidden - start, features // blocks
    slope, *outs = pl.pallas_call(
        functools.partial(forward_last_kernel, start),
        out_shape=[struct((tokens, part), F32), struct((rows, tokens), F32)]
        + [struct((rows, tokens), BF16)] * (blocks - 1),
        in_specs=[SCALARS, WHOLE, WHOLE, HELD, HELD],
        out_specs=[WHOLE] * (blocks + 1),
        scratch_shapes=layer_scratch(part, features)
        + [
            pltpu.VMEM((tokens, features), F32),
            pltpu.VMEM((features, tokens), F32),
            pltpu.SemaphoreType.DMA((2 * len(pieces(start, hidden)),)),
        ],
        name=name,
        **layer_params(part, features, tokens, part * tokens),
    )(order, normed, before, w_in, w_out)
    return slope, outs[0], outs[1:]


def write_blocks(order, full, outs):
    for place, target in enumerate(outs):
        rows = target.shape[0]
        offset = pl.multiple_of(order[place] * rows, 8)
        target[...] = full[pl.ds(offset, rows), :].astype(target.dtype)


def backward_products(stream, parts, base, grad, slopes, in_buf, out_buf, total, before, last):
    state = [before]

    def product(at, size):
        stream.take()
        return against_rows(grad[...], out_buf[pl.ds(at - base, size), :])

    def finish(at, size, value, final):
        rows = pl.ds(at - base, size)
        seen = slopes[0].shape[1]
        slope = slopes[0][:, pl.ds(at, size)] if at < seen else slopes[1][:, pl.ds(at - seen, size)]
        stream.take()
        accumulate(total, (value * slope).astype(BF16), in_buf.at[rows, :], state[0], last if final else None)
        state[0] = total

    pipelined(parts, product, finish)


def backward_first_kernel(blocks, part, order, *refs):
    pieces_in, (slope_a, slope_b, w_in, w_out, grad, total, in_buf, out_buf, full, stage, sems) = refs[:blocks], refs[blocks:]
    parts = pieces(0, part)
    stream = Stream(w_out, out_buf, w_in, in_buf, parts, 0, sems)
    values = [lambda ref=ref: ref[...] for ref in pieces_in]
    place_blocks(full, slice(None), stage, order, values, pieces_in[0].shape[0])
    for start, size in pieces(0, full.shape[0], 128):
        rows = pl.ds(start, size)
        grad[:, rows] = full[rows, :].astype(F32).T.astype(BF16)
    backward_products(stream, parts, 0, grad, (slope_a, slope_b), in_buf, out_buf, total, None, None)


def backward_first(order, gathered, slope_a, slope_b, w_in, w_out, part, name):
    hidden, features = w_in.shape[1:]
    blocks, (rows, tokens) = len(gathered), gathered[0].shape
    return pl.pallas_call(
        functools.partial(backward_first_kernel, blocks, part),
        out_shape=(struct((tokens, features), BF16), struct((tokens, features), F32)),
        in_specs=[SCALARS] + [WHOLE] * (blocks + 2) + [HELD, HELD],
        out_specs=[WHOLE] * 2,
        scratch_shapes=layer_scratch(part, features)
        + [
            pltpu.VMEM((features, tokens), BF16),
            staging(rows, features, tokens),
            pltpu.SemaphoreType.DMA((2 * len(pieces(0, part)),)),
        ],
        name=name,
        **layer_params(part, features, tokens, 0),
    )(order, *gathered, slope_a, slope_b, w_in, w_out)


def backward_last_kernel(start, rows, order, grad, before, slope_a, slope_b, acts, stats, mod, w_in, w_out, *refs):
    outs, (sums_out, in_buf, out_buf, total, full, sems) = refs[:-6], refs[-6:]
    hidden, (features, tokens) = w_in.shape[1], full.shape
    parts = pieces(start, hidden)
    stream = Stream(w_out, out_buf, w_in, in_buf, parts, start, sems)
    mean, inv = stats[0:1, :], stats[1:2, :]
    sums = [jnp.zeros((1, tokens), F32), jnp.zeros((1, tokens), F32)]

    def last(at, size, value):
        at = pl.ds(at, size)
        value = value.T
        full[at, :] = value
        scaled = value * (1.0 + mod[at, 1:2])
        xhat = (acts[0, at, :].astype(F32) - mean) * inv
        sums[0] += jnp.sum(scaled, 0, keepdims=True)
        sums[1] += jnp.sum(scaled * xhat, 0, keepdims=True)

    backward_products(stream, parts, start, grad, (slope_a, slope_b), in_buf, out_buf, total, before, last)
    count = len(outs) // 2
    padded = outs[0].shape[0] - 16
    tail = pack_sums(*sums)
    for place in range(count):
        offset = pl.multiple_of(order[2 * place] * rows, 8)
        outs[count + place][...] = full[pl.ds(offset, rows), :]
        offset = pl.multiple_of(order[2 * place + 1] * rows, 8)
        block = full[pl.ds(offset, rows), :]
        if padded > rows:
            block = jnp.concatenate([block, jnp.zeros((padded - rows, tokens), F32)], 0)
        outs[place][:padded, :] = block.astype(BF16)
        outs[place][padded:, :] = tail
    sums_out[0:1, :] = sums[0]
    sums_out[1:2, :] = sums[1]


def backward_last(order, grad, before, slope_a, slope_b, acts, stats, mod, w_in, w_out, start, blocks, name):
    hidden, features = w_in.shape[1:]
    tokens, part, rows, count = before.shape[0], hidden - start, features // blocks, blocks // 2
    outs = pl.pallas_call(
        functools.partial(backward_last_kernel, start, rows),
        out_shape=[struct((-(-rows // 16) * 16 + 16, tokens), BF16)] * count
        + [struct((rows, tokens), F32)] * count
        + [struct((2, tokens), F32)],
        in_specs=[SCALARS] + [WHOLE] * 7 + [HELD, HELD],
        out_specs=[WHOLE] * (blocks + 1),
        scratch_shapes=layer_scratch(part, features)
        + [
            pltpu.VMEM((tokens, features), F32),
            pltpu.VMEM((features, tokens), F32),
            pltpu.SemaphoreType.DMA((2 * len(pieces(start, hidden)),)),
        ],
        name=name,
        **layer_params(part, features, tokens, 0),
    )(order, grad, before, slope_a, slope_b, acts, stats, mod, w_in, w_out)
    return outs[:count], outs[count:-1], outs[-1]


def fold_kernel(rows, count, *refs):
    got, kept, (sums, *outs) = refs[:count], refs[count : 2 * count], refs[2 * count :]
    more = unpack_sums(got[0][-16:, :])
    plain, along = sums[0:1, :] + more[0], sums[1:2, :] + more[1]
    tail = pack_sums(plain, along)
    padded = got[0].shape[0] - 16
    for place in range(count // 2):
        even, odd = 2 * place, 2 * place + 1
        outs[count // 2 + place][...] = kept[even][...] + got[even][:rows, :].astype(F32)
        block = kept[odd][...] + got[odd][:rows, :].astype(F32)
        if padded > rows:
            block = jnp.concatenate([block, jnp.zeros((padded - rows, block.shape[1]), F32)], 0)
        outs[place][:padded, :] = block.astype(BF16)
        outs[place][padded:, :] = tail
    outs[-1][0:1, :] = plain
    outs[-1][1:2, :] = along


def fold(got, kept, sums):
    count, (rows, tokens) = len(kept), kept[0].shape
    outs = pl.pallas_call(
        functools.partial(fold_kernel, rows, count),
        out_shape=[struct(got[0].shape, BF16)] * (count // 2)
        + [struct((rows, tokens), F32)] * (count // 2)
        + [struct((2, tokens), F32)],
        in_specs=[WHOLE] * (2 * count + 1),
        out_specs=[WHOLE] * (count + 1),
        name="fold",
        **params(2 * count * rows * tokens, 8 * count * rows * tokens, grant=12),
    )(*got, *kept, sums)
    return outs[: count // 2], outs[count // 2 : -1], outs[-1]


def prepare_kernel(blocks, order, acts, modulation, own, arrived, weight, *refs):
    outs, (normed, stats, cot0, cot1, full, buf, sem) = refs[:blocks], refs[blocks:]
    load = pltpu.make_async_copy(weight, buf, sem)
    load.start()
    group = order[blocks]
    control = group == 0
    half = cot0.shape[1]
    lanes = pl.ds(pl.multiple_of(group * half, half), half)
    cot0[...] = jnp.where(control, own[:, lanes], arrived[:, lanes])
    mine = jnp.where(control, arrived[:, lanes], own[:, lanes])
    cot1[...] = mine
    normalize(acts, modulation, normed, stats)
    load.wait()
    full[...] = lax.dot_general(mine, buf[...], (((0,), (0,)), ((), ())), preferred_element_type=F32).T
    write_blocks(order, full, outs)


def prepare(order, acts, modulation, own, arrived, weight, blocks):
    rows, tokens = own.shape
    half, features = tokens // 2, weight.shape[1]
    outs = pl.pallas_call(
        functools.partial(prepare_kernel, blocks),
        out_shape=[struct((rows, half), F32)]
        + [struct((rows, half), BF16)] * (blocks - 1)
        + [
            struct((tokens, features), BF16),
            struct((2, tokens), F32),
            struct((rows, half), BF16),
            struct((rows, half), BF16),
        ],
        in_specs=[SCALARS] + [WHOLE] * 4 + [HELD],
        out_specs=[WHOLE] * (blocks + 4),
        scratch_shapes=[
            pltpu.VMEM((features, half), F32),
            pltpu.VMEM(weight.shape, BF16),
            pltpu.SemaphoreType.DMA(()),
        ],
        name="prepare",
        **params(2 * weight.size * half, 2 * weight.size + 4 * blocks * rows * half, grant=50),
    )(order, acts, modulation, own, arrived, weight)
    return outs[0], outs[1:blocks], *outs[blocks:]


def residual_kernel(order, weight, *refs):
    stack, (result, full, stage) = refs[:-3], refs[-3:]
    values = [lambda value=value: value[...] for value in stack]
    place_blocks(full, slice(None), stage, order, values, stack[0].shape[0])
    result[...] = jnp.dot(weight[...], full[...], preferred_element_type=F32)


def residual_rows(order, weight, stack):
    blocks, (rows, half) = len(stack), stack[0].shape
    return pl.pallas_call(
        residual_kernel,
        out_shape=struct((rows, half), F32),
        in_specs=[SCALARS] + [WHOLE] * (blocks + 1),
        out_specs=WHOLE,
        scratch_shapes=[pltpu.VMEM((blocks * rows, half), BF16), staging(rows, blocks * rows, half)],
        name="residual_rows",
        **params(2 * weight.size * half, 2 * weight.size + 4 * blocks * rows * half, grant=12),
    )(order, weight, *stack)


def zero_grad_kernel(blocks, first, count, order, dp_order, *refs):
    cots, refs = (refs[:count], refs[count : 2 * count]), refs[2 * count :]
    stacks = []
    while len(refs) > (9 if first else 6):
        stacks.append((refs[:blocks], refs[blocks : 2 * blocks]))
        refs = refs[2 * blocks :]
    before = None
    if first:
        before, out, lhs, rhs, stage, parked, loads, buf, sems = refs
    else:
        buf, lhs, rhs, stage, parked, loads = refs
    rows, half = cots[0][0].shape
    group = order[blocks]
    moves, places = [], []
    for part in range(count):
        slot = part // 2 * 2 + (dp_order[first + part] & 1)
        for side, owner in enumerate((group, 1 - group)):
            lanes = pl.ds(pl.multiple_of((slot * 2 + owner) * half, half), half)
            moves.append((cots[side][part], lhs.at[:, lanes]))
            values = []
            for place in range(blocks):
                source = stacks[part][side][place] if len(stacks) == count else stacks[0][side][place].at[part]
                if rows % 16:
                    at = (part * 2 + side) * blocks + place
                    target = parked.at[at]
                    values.append(lambda at=at: parked[at])
                else:
                    offset = pl.multiple_of(order[side * (blocks + 1) + place] * rows, 16)
                    target = rhs.at[pl.ds(offset, rows), lanes]
                moves.append((source, target))
            places.append((lanes, values, side * (blocks + 1)))
    moves = [pltpu.make_async_copy(a, b, loads.at[k]) for k, (a, b) in enumerate(moves)]
    for move in moves:
        move.start()
    for move in moves:
        move.wait()
    if rows % 16:
        for lanes, values, shift in places:
            place_blocks(rhs, lanes, stage, order, values, rows, shift)
    copies = []
    for k, (start, size) in enumerate(pieces(0, blocks * rows)):
        columns = pl.ds(start, size)
        value = against_rows(lhs[...], rhs[columns, :])
        buf[:, columns] = value if before is None else before[:, columns] + value
        if before is not None:
            copies.append(pltpu.make_async_copy(buf.at[:, columns], out.at[:, columns], sems.at[k]))
            copies[-1].start()
    for copy in copies:
        copy.wait()


def zero_projection_grad(order, dp_order, first, cots, cots_other, stacks, before, name):
    blocks, (rows, half) = len(stacks[0][0]), cots[0].shape
    count = len(cots)
    features, tokens = blocks * rows, count * 2 * half
    flat = [block for pair in stacks for side in pair for block in side]
    extra = [] if before is None else [before]
    scratch = [
        pltpu.VMEM((rows, tokens), BF16),
        pltpu.VMEM((features, tokens), BF16),
        staging(rows, features, half),
        pltpu.VMEM((count * 2 * blocks, rows, half) if rows % 16 else (1, 8, 128), BF16),
        pltpu.SemaphoreType.DMA((count * 2 * (blocks + 1),)),
    ]
    if extra:
        scratch += [
            pltpu.VMEM((rows, features), F32),
            pltpu.SemaphoreType.DMA((len(pieces(0, features)),)),
        ]
    return pl.pallas_call(
        functools.partial(zero_grad_kernel, blocks, first, count),
        out_shape=struct((rows, features), F32),
        in_specs=[SCALARS] * 2 + [HELD] * (2 * count + len(flat)) + [WHOLE] * len(extra),
        out_specs=HELD if extra else WHOLE,
        scratch_shapes=scratch,
        name=name,
        **params(2 * tokens * rows * features, 4 * rows * features + 2 * tokens * (rows + features), grant=28),
    )(order, dp_order, *cots, *cots_other, *flat, *extra)


def steps(values, level, *during):
    got = [step(value, level) for value in values]
    return list(lax.optimization_barrier((tuple(got),) + during)[0]) if during else got


def direct(values, *during):
    got = [send(value, place + 1) for place, value in enumerate(values)]
    return list(lax.optimization_barrier((tuple(got),) + during)[0])


def local(acts, modulation, w_in, w_out, zero_weight, cotangent):
    own_cot = cotangent[0]
    features, tokens = acts.shape[1:]
    hidden = w_in.shape[1]
    rows = own_cot.shape[0]
    half = tokens // 2
    blocks, levels = lax.axis_size("fsdp"), stages()
    parts = lax.axis_size("dp")
    group = lax.axis_index("grp").astype(jnp.int32)
    me = lax.axis_index("fsdp").astype(jnp.int32)
    is_control = group == 0
    places = block_order(group, me)
    order = jnp.concatenate([places, group[None], block_order(1 - group, me)])
    dp_order = lax.axis_index("dp").astype(jnp.int32) ^ jnp.arange(parts, dtype=jnp.int32)

    arrived = swap_grp(own_cot)
    own_term, sent, normed, stats, cot0, cot1 = prepare(
        order, acts, modulation, own_cot, arrived, zero_weight, blocks
    )
    split, cut = split_rows(hidden)
    slope_a, total, mod = forward_first(after(normed, *sent), modulation, w_in, w_out, split, "forward_first")
    own_mod = block_of(mod, me, rows)
    own_gate = own_mod[:, 2:3]
    got = direct(sent, total)
    up_half = own_term + cot0.astype(F32) + sum(value.astype(F32) for value in got)
    up_rows = jnp.where(is_control, jnp.concatenate([up_half, swap_grp(up_half)], 1), own_cot.astype(F32))
    grad_rows = (own_gate * up_rows).astype(BF16)

    slope_b, kept, sent = forward_last(
        order, after(normed, grad_rows), total, w_in, w_out, split, blocks, "forward_last"
    )
    gathered = [grad_rows] + direct([grad_rows] * (blocks - 1), kept)
    grad, total = backward_first(
        order, after(gathered, *sent), slope_a, slope_b, w_in, w_out, cut, "backward_first"
    )
    got = direct(sent, total)
    own_values = block_of(acts[0], me, rows).astype(F32)
    sums = own_values + own_gate * (kept + sum(value.astype(F32) for value in got))
    out_rows = sums.astype(BF16)

    out_half = jnp.where(is_control, out_rows[:, :half], swap_grp(out_rows[:, half:]))
    far = gather_dp(out_half)[1:]
    near = [out_half] + [send(out_half, place) for place in range(1, blocks)]
    sent, kept, token_sums = backward_last(
        order, after(grad, out_half), total, slope_a, slope_b, acts, stats, mod, w_in, w_out, cut, blocks, "backward_last"
    )
    far, near, sent, kept, token_sums = lax.optimization_barrier((far, near, sent, kept, token_sums))

    gathers = [[far[0]], [jnp.stack(far[1:])]]
    last = gather_dp(near[-1])[1:]
    lasts = [last[0], jnp.stack(last[1:])]
    for level in range(levels):
        got = steps(sent, level)
        final = level + 1 == levels
        for gather, end in zip(gathers, lasts):
            gather += steps(gather[:-1], level) + [end] if final else steps(gather, level)
        if level == 0:
            cot1, near = after((cot1, near), got)
            cots = gather_dp(cot1)
            near_other = [swap_grp(value) for value in near]
            residual = residual_rows(order, zero_weight, near)
        if not final:
            sent, kept, token_sums = fold(got, kept, token_sums)
    cots_other = [swap_grp(value) for value in cots]
    more = unpack_sums(got[0][-16:])
    plain, along = token_sums[0:1] + more[0], token_sums[1:2] + more[1]
    kept = [kept[0] + got[0][:rows].astype(F32)]
    mean, inv = stats[0:1], stats[1:2]
    back = inv * (
        kept[0] * (1.0 + own_mod[:, 1:2]) - plain / features - (own_values - mean) * inv * (along / features)
    )
    residual = jnp.concatenate([swap_grp(residual), residual], 1)
    block_rows = jnp.where(is_control, out_rows, (sums + residual).astype(BF16))

    stacks = [(near, near_other)] + [(mine, [swap_grp(value) for value in mine]) for mine in gathers]
    zero_grad = zero_projection_grad(
        order, dp_order, 0, cots[:2], cots_other[:2], stacks[:2], None, "zero_projection_grad_first"
    )
    zero_grad = zero_projection_grad(
        order, dp_order, 2, cots[2:], cots_other[2:], stacks[2:], zero_grad, "zero_projection_grad_last"
    )
    return (block_rows[None], (up_rows + back)[None], zero_grad)


def solution(mesh):
    placed = (
        P("grp", None, "dp"),
        P("grp", None, None),
        P("grp", "fsdp", None),
        P("grp", "fsdp", None),
        P("fsdp", None),
        P("grp", "fsdp", "dp"),
    )
    return jax.shard_map(
        local,
        mesh=mesh,
        in_specs=placed,
        out_specs=(P("grp", "fsdp", "dp"), P("grp", "fsdp", "dp"), P("fsdp", None)),
        check_vma=False,
    )
```

```python
import functools

import jax
import jax.numpy as jnp
from jax import lax
from jax.experimental import pallas as pl
from jax.experimental.pallas import tpu as pltpu
from jax.sharding import PartitionSpec as P

EPSILON = 1e-06
SQRT_2_OVER_PI = 0.7978845608028654
CHUNK = 512
AHEAD = 3
MIB = 1024 * 1024
F32, BF16 = jnp.float32, jnp.bfloat16
WHOLE = pl.BlockSpec(memory_space=pltpu.VMEM)
HELD = pl.BlockSpec(memory_space=pltpu.HBM)
ANYWHERE = pl.BlockSpec(memory_space=pl.ANY)
SCALARS = pl.BlockSpec(memory_space=pltpu.SMEM)


def pieces(start, stop, size=CHUNK):
    return [(at, min(size, stop - at)) for at in range(start, stop, size)]


def split_rows(hidden):
    units = hidden // CHUNK
    return CHUNK * max(units // 2, 1), (hidden - 1) // CHUNK * CHUNK


def after(value, *others):
    return lax.optimization_barrier((value,) + others)[0]


def swap_grp(value):
    return lax.ppermute(value, "grp", [(0, 1), (1, 0)])


def stages():
    return (lax.axis_size("fsdp") - 1).bit_length()


def step(value, stage):
    length, bits = lax.axis_size("fsdp"), stages()
    pairs = []
    for group, bit in ((0, stage), (1, bits - 1 - stage)):
        pairs += [(group * length + i, group * length + (i ^ (1 << bit))) for i in range(length)]
    return lax.ppermute(value, ("grp", "fsdp"), pairs)


def block_order(group, me):
    length, bits = lax.axis_size("fsdp"), stages()
    turned = [sum(((v >> b) & 1) << (bits - 1 - b) for b in range(bits)) for v in range(length)]
    up, down = jnp.arange(length, dtype=jnp.int32), jnp.array(turned, jnp.int32)
    return me ^ jnp.where(group == 0, up, down)


def send(value, place):
    length, bits = lax.axis_size("fsdp"), stages()
    turned = sum(((place >> b) & 1) << (bits - 1 - b) for b in range(bits))
    pairs = []
    for group, mask in ((0, place), (1, turned)):
        pairs += [(group * length + i, group * length + (i ^ mask)) for i in range(length)]
    return lax.ppermute(value, ("grp", "fsdp"), pairs)


def gather_dp(value):
    length = lax.axis_size("dp")
    return [value] + [
        lax.ppermute(value, "dp", [(i, i ^ mask) for i in range(length)]) for mask in range(1, length)
    ]


def block_of(value, index, rows):
    return lax.dynamic_slice_in_dim(value, index * rows, rows, 0)


def split_three(value):
    high = value.astype(BF16)
    rest = value - high.astype(F32)
    mid = rest.astype(BF16)
    return high, mid, (rest - mid.astype(F32)).astype(BF16)


def pack_sums(plain, along):
    tail = [part.astype(F32) for part in split_three(plain) + split_three(along)]
    return jnp.concatenate(tail + [jnp.zeros((10, plain.shape[1]), F32)], 0).astype(BF16)


def unpack_sums(tail):
    tail = tail.astype(F32)
    return tail[0:1] + tail[1:2] + tail[2:3], tail[3:4] + tail[4:5] + tail[5:6]


def gelu_and_slope(v):
    square = v * v
    t = jnp.tanh(SQRT_2_OVER_PI * (v + 0.044715 * (square * v)))
    rise = 0.5 * (1.0 + t)
    slope = rise + 0.5 * v * (1.0 - t * t) * (SQRT_2_OVER_PI * (1.0 + (3 * 0.044715) * square))
    return v * rise, slope


class Stream:
    def __init__(self, first, first_buf, second, second_buf, parts, base, sems):
        def copy(weight, buf, part):
            return weight.at[0, pl.ds(part[0], part[1]), :], buf.at[pl.ds(part[0] - base, part[1]), :]

        pairs = [copy(first, first_buf, parts[0])]
        for k, part in enumerate(parts):
            if k + 1 < len(parts):
                pairs.append(copy(first, first_buf, parts[k + 1]))
            pairs.append(copy(second, second_buf, part))
        self.copies = [pltpu.make_async_copy(a, b, sems.at[k]) for k, (a, b) in enumerate(pairs)]
        self.next = 0
        for item in self.copies[:AHEAD]:
            item.start()

    def take(self):
        k = self.next
        self.copies[k].wait()
        if k + AHEAD < len(self.copies):
            self.copies[k + AHEAD].start()
        self.next = k + 1


def pipelined(parts, product, finish):
    held = None
    for part in parts:
        value = product(*part)
        if held is not None:
            finish(*held, False)
        held = part + (value,)
    finish(*held, True)


def params(flops, moved, transcendentals=0, grant=50):
    return dict(
        compiler_params=pltpu.CompilerParams(vmem_limit_bytes=grant * MIB),
        cost_estimate=pl.CostEstimate(flops=flops, bytes_accessed=moved, transcendentals=transcendentals),
    )


def struct(shape, dtype):
    return jax.ShapeDtypeStruct(shape, dtype)


def staging(rows, features, lanes):
    return pltpu.VMEM((features, lanes) if rows % 16 else (8, 128), F32)


def place_blocks(target, lanes, stage, order, blocks, rows, first=0):
    for place, value in enumerate(blocks):
        if rows % 16:
            stage[pl.ds(pl.multiple_of(order[first + place] * rows, 8), rows), :] = value().astype(F32)
        else:
            target[pl.ds(pl.multiple_of(order[first + place] * rows, 16), rows), lanes] = value()
    if rows % 16:
        target[:, lanes] = stage[...].astype(target.dtype)


def turn_modulation(modulation, columns):
    for start, size in pieces(0, modulation.shape[2], 128):
        rows = modulation[0, :, pl.ds(start, size)]
        columns[pl.ds(start, size), :] = jnp.concatenate([rows, jnp.zeros((5, size), F32)], 0).T


def normalize(acts, modulation, normed, stats):
    features, tokens = acts.shape[1:]
    parts = pieces(0, features, 128)
    total = jnp.zeros((1, tokens), F32)
    for start, size in parts:
        total += jnp.sum(acts[0, pl.ds(start, size), :].astype(F32), 0, keepdims=True)
    mean = total / features
    total = jnp.zeros((1, tokens), F32)
    for start, size in parts:
        centred = acts[0, pl.ds(start, size), :].astype(F32) - mean
        total += jnp.sum(centred * centred, 0, keepdims=True)
    inv = lax.rsqrt(total / features + EPSILON)
    stats[0:1, :] = mean
    stats[1:2, :] = inv
    for start, size in parts:
        rows = pl.ds(start, size)
        xhat = (acts[0, rows, :].astype(F32) - mean) * inv
        shift, scale = modulation[0, 0:1, rows], modulation[0, 1:2, rows]
        normed[:, rows] = (xhat.T * (1.0 + scale) + shift).astype(BF16)


def against_rows(columns, weight):
    return lax.dot_general(columns, weight, (((1,), (1,)), ((), ())), preferred_element_type=F32)


def accumulate(total, part, weight, before, finish):
    for at, size in pieces(0, weight.shape[1]):
        columns = pl.ds(at, size)
        value = jnp.dot(part, weight[:, columns], preferred_element_type=F32)
        if before is not None:
            value = value + before[:, columns]
        if finish is None:
            total[:, columns] = value
        else:
            finish(at, size, value)


def forward_products(stream, parts, base, normed, in_buf, out_buf, slope_out, total, before, last):
    state = [before]

    def product(at, size):
        stream.take()
        return against_rows(normed[...], in_buf[pl.ds(at - base, size), :])

    def finish(at, size, pre, final):
        rows = pl.ds(at - base, size)
        hidden, slope = gelu_and_slope(pre)
        slope_out[:, rows] = slope
        stream.take()
        accumulate(total, hidden.astype(BF16), out_buf.at[rows, :], state[0], last if final else None)
        state[0] = total

    pipelined(parts, product, finish)


def forward_first_kernel(normed, modulation, w_in, w_out, slope_out, total, mod, in_buf, out_buf, sems):
    parts = pieces(0, slope_out.shape[1])
    stream = Stream(w_in, in_buf, w_out, out_buf, parts, 0, sems)
    turn_modulation(modulation, mod)
    forward_products(stream, parts, 0, normed, in_buf, out_buf, slope_out, total, None, None)


def forward_last_kernel(start, order, normed, before, w_in, w_out, slope_out, *refs):
    outs, (in_buf, out_buf, total, full, sems) = refs[:-5], refs[-5:]
    parts = pieces(start, start + slope_out.shape[1])
    stream = Stream(w_in, in_buf, w_out, out_buf, parts, start, sems)

    def last(at, size, value):
        full[pl.ds(at, size), :] = value.T

    forward_products(stream, parts, start, normed, in_buf, out_buf, slope_out, total, before, last)
    write_blocks(order, full, outs)


def layer_scratch(part, features):
    return [
        pltpu.VMEM((part, features), BF16),
        pltpu.VMEM((part, features), BF16),
    ]


def layer_params(part, features, tokens, transcendentals):
    return params(4 * part * features * tokens, 4 * part * features + 4 * features * tokens, transcendentals)


def forward_first(normed, modulation, w_in, w_out, part, name):
    tokens, features = normed.shape
    return pl.pallas_call(
        forward_first_kernel,
        out_shape=(struct((tokens, part), F32), struct((tokens, features), F32), struct((features, 8), F32)),
        in_specs=[WHOLE, WHOLE, HELD, HELD],
        out_specs=[WHOLE] * 3,
        scratch_shapes=layer_scratch(part, features) + [pltpu.SemaphoreType.DMA((2 * len(pieces(0, part)),))],
        name=name,
        **layer_params(part, features, tokens, part * tokens),
    )(normed, modulation, w_in, w_out)


def forward_last(order, normed, before, w_in, w_out, start, blocks, name):
    hidden, features = w_in.shape[1:]
    tokens, part, rows = before.shape[0], hidden - start, features // blocks
    slope, *outs = pl.pallas_call(
        functools.partial(forward_last_kernel, start),
        out_shape=[struct((tokens, part), F32), struct((rows, tokens), F32)]
        + [struct((rows, tokens), BF16)] * (blocks - 1),
        in_specs=[SCALARS, WHOLE, WHOLE, HELD, HELD],
        out_specs=[WHOLE] * (blocks + 1),
        scratch_shapes=layer_scratch(part, features)
        + [
            pltpu.VMEM((tokens, features), F32),
            pltpu.VMEM((features, tokens), F32),
            pltpu.SemaphoreType.DMA((2 * len(pieces(start, hidden)),)),
        ],
        name=name,
        **layer_params(part, features, tokens, part * tokens),
    )(order, normed, before, w_in, w_out)
    return slope, outs[0], outs[1:]


def write_blocks(order, full, outs):
    for place, target in enumerate(outs):
        rows = target.shape[0]
        offset = pl.multiple_of(order[place] * rows, 8)
        target[...] = full[pl.ds(offset, rows), :].astype(target.dtype)


def backward_products(stream, parts, base, grad, slopes, in_buf, out_buf, total, before, last):
    state = [before]

    def product(at, size):
        stream.take()
        return against_rows(grad[...], out_buf[pl.ds(at - base, size), :])

    def finish(at, size, value, final):
        rows = pl.ds(at - base, size)
        seen = slopes[0].shape[1]
        slope = slopes[0][:, pl.ds(at, size)] if at < seen else slopes[1][:, pl.ds(at - seen, size)]
        stream.take()
        accumulate(total, (value * slope).astype(BF16), in_buf.at[rows, :], state[0], last if final else None)
        state[0] = total

    pipelined(parts, product, finish)


def backward_first_kernel(blocks, part, order, *refs):
    pieces_in, (slope_a, slope_b, w_in, w_out, grad, total, in_buf, out_buf, full, stage, sems) = refs[:blocks], refs[blocks:]
    parts = pieces(0, part)
    stream = Stream(w_out, out_buf, w_in, in_buf, parts, 0, sems)
    values = [lambda ref=ref: ref[...] for ref in pieces_in]
    place_blocks(full, slice(None), stage, order, values, pieces_in[0].shape[0])
    for start, size in pieces(0, full.shape[0], 128):
        rows = pl.ds(start, size)
        grad[:, rows] = full[rows, :].astype(F32).T.astype(BF16)
    backward_products(stream, parts, 0, grad, (slope_a, slope_b), in_buf, out_buf, total, None, None)


def backward_first(order, gathered, slope_a, slope_b, w_in, w_out, part, name):
    hidden, features = w_in.shape[1:]
    blocks, (rows, tokens) = len(gathered), gathered[0].shape
    return pl.pallas_call(
        functools.partial(backward_first_kernel, blocks, part),
        out_shape=(struct((tokens, features), BF16), struct((tokens, features), F32)),
        in_specs=[SCALARS] + [WHOLE] * (blocks + 2) + [HELD, HELD],
        out_specs=[WHOLE] * 2,
        scratch_shapes=layer_scratch(part, features)
        + [
            pltpu.VMEM((features, tokens), BF16),
            staging(rows, features, tokens),
            pltpu.SemaphoreType.DMA((2 * len(pieces(0, part)),)),
        ],
        name=name,
        **layer_params(part, features, tokens, 0),
    )(order, *gathered, slope_a, slope_b, w_in, w_out)


def backward_last_kernel(start, rows, order, grad, before, slope_a, slope_b, acts, stats, mod, w_in, w_out, *refs):
    outs, (sums_out, in_buf, out_buf, total, full, sems) = refs[:-6], refs[-6:]
    hidden, (features, tokens) = w_in.shape[1], full.shape
    parts = pieces(start, hidden)
    stream = Stream(w_out, out_buf, w_in, in_buf, parts, start, sems)
    mean, inv = stats[0:1, :], stats[1:2, :]
    sums = [jnp.zeros((1, tokens), F32), jnp.zeros((1, tokens), F32)]

    def last(at, size, value):
        at = pl.ds(at, size)
        value = value.T
        full[at, :] = value
        scaled = value * (1.0 + mod[at, 1:2])
        xhat = (acts[0, at, :].astype(F32) - mean) * inv
        sums[0] += jnp.sum(scaled, 0, keepdims=True)
        sums[1] += jnp.sum(scaled * xhat, 0, keepdims=True)

    backward_products(stream, parts, start, grad, (slope_a, slope_b), in_buf, out_buf, total, before, last)
    count = len(outs) // 2
    padded = outs[0].shape[0] - 16
    tail = pack_sums(*sums)
    for place in range(count):
        offset = pl.multiple_of(order[2 * place] * rows, 8)
        outs[count + place][...] = full[pl.ds(offset, rows), :]
        offset = pl.multiple_of(order[2 * place + 1] * rows, 8)
        block = full[pl.ds(offset, rows), :]
        if padded > rows:
            block = jnp.concatenate([block, jnp.zeros((padded - rows, tokens), F32)], 0)
        outs[place][:padded, :] = block.astype(BF16)
        outs[place][padded:, :] = tail
    sums_out[0:1, :] = sums[0]
    sums_out[1:2, :] = sums[1]


def backward_last(order, grad, before, slope_a, slope_b, acts, stats, mod, w_in, w_out, start, blocks, name):
    hidden, features = w_in.shape[1:]
    tokens, part, rows, count = before.shape[0], hidden - start, features // blocks, blocks // 2
    outs = pl.pallas_call(
        functools.partial(backward_last_kernel, start, rows),
        out_shape=[struct((-(-rows // 16) * 16 + 16, tokens), BF16)] * count
        + [struct((rows, tokens), F32)] * count
        + [struct((2, tokens), F32)],
        in_specs=[SCALARS] + [WHOLE] * 7 + [HELD, HELD],
        out_specs=[WHOLE] * (blocks + 1),
        scratch_shapes=layer_scratch(part, features)
        + [
            pltpu.VMEM((tokens, features), F32),
            pltpu.VMEM((features, tokens), F32),
            pltpu.SemaphoreType.DMA((2 * len(pieces(start, hidden)),)),
        ],
        name=name,
        **layer_params(part, features, tokens, 0),
    )(order, grad, before, slope_a, slope_b, acts, stats, mod, w_in, w_out)
    return outs[:count], outs[count:-1], outs[-1]


def fold_kernel(rows, count, *refs):
    got, kept, (sums, *outs) = refs[:count], refs[count : 2 * count], refs[2 * count :]
    more = unpack_sums(got[0][-16:, :])
    plain, along = sums[0:1, :] + more[0], sums[1:2, :] + more[1]
    tail = pack_sums(plain, along)
    padded = got[0].shape[0] - 16
    for place in range(count // 2):
        even, odd = 2 * place, 2 * place + 1
        outs[count // 2 + place][...] = kept[even][...] + got[even][:rows, :].astype(F32)
        block = kept[odd][...] + got[odd][:rows, :].astype(F32)
        if padded > rows:
            block = jnp.concatenate([block, jnp.zeros((padded - rows, block.shape[1]), F32)], 0)
        outs[place][:padded, :] = block.astype(BF16)
        outs[place][padded:, :] = tail
    outs[-1][0:1, :] = plain
    outs[-1][1:2, :] = along


def fold(got, kept, sums):
    count, (rows, tokens) = len(kept), kept[0].shape
    outs = pl.pallas_call(
        functools.partial(fold_kernel, rows, count),
        out_shape=[struct(got[0].shape, BF16)] * (count // 2)
        + [struct((rows, tokens), F32)] * (count // 2)
        + [struct((2, tokens), F32)],
        in_specs=[WHOLE] * (2 * count + 1),
        out_specs=[WHOLE] * (count + 1),
        name="fold",
        **params(2 * count * rows * tokens, 8 * count * rows * tokens, grant=12),
    )(*got, *kept, sums)
    return outs[: count // 2], outs[count // 2 : -1], outs[-1]


def prepare_kernel(blocks, order, acts, modulation, own, arrived, weight, *refs):
    outs, (normed, stats, cot0, cot1_rows, full, buf, sem) = refs[:blocks], refs[blocks:]
    load = pltpu.make_async_copy(weight, buf, sem)
    load.start()
    group = order[blocks]
    control = group == 0
    half = cot0.shape[1]
    lanes = pl.ds(pl.multiple_of(group * half, half), half)
    cot0[...] = jnp.where(control, own[:, lanes], arrived[:, lanes])
    mine = jnp.where(control, arrived[:, lanes], own[:, lanes])
    cot1_rows[...] = jnp.where(control, arrived[...], own[...])
    normalize(acts, modulation, normed, stats)
    load.wait()
    full[...] = lax.dot_general(mine, buf[...], (((0,), (0,)), ((), ())), preferred_element_type=F32).T
    write_blocks(order, full, outs)


def prepare(order, acts, modulation, own, arrived, weight, blocks):
    rows, tokens = own.shape
    half, features = tokens // 2, weight.shape[1]
    outs = pl.pallas_call(
        functools.partial(prepare_kernel, blocks),
        out_shape=[struct((rows, half), F32)]
        + [struct((rows, half), BF16)] * (blocks - 1)
        + [
            struct((tokens, features), BF16),
            struct((2, tokens), F32),
            struct((rows, half), BF16),
            struct((rows, tokens), BF16),
        ],
        in_specs=[SCALARS] + [WHOLE] * 4 + [HELD],
        out_specs=[WHOLE] * (blocks + 4),
        scratch_shapes=[
            pltpu.VMEM((features, half), F32),
            pltpu.VMEM(weight.shape, BF16),
            pltpu.SemaphoreType.DMA(()),
        ],
        name="prepare",
        **params(2 * weight.size * half, 2 * weight.size + 4 * blocks * rows * half, grant=50),
    )(order, acts, modulation, own, arrived, weight)
    return outs[0], outs[1:blocks], *outs[blocks:]


def residual_kernel(order, weight, *refs):
    stack, (result, full, stage) = refs[:-3], refs[-3:]
    values = [lambda value=value: value[0] for value in stack]
    place_blocks(full, slice(None), stage, order, values, stack[0].shape[1])
    result[...] = jnp.dot(weight[...], full[...], preferred_element_type=F32)


def residual_rows(order, weight, stack):
    blocks, (_, rows, half) = len(stack), stack[0].shape
    return pl.pallas_call(
        residual_kernel,
        out_shape=struct((rows, half), F32),
        in_specs=[SCALARS] + [WHOLE] * (blocks + 1),
        out_specs=WHOLE,
        scratch_shapes=[pltpu.VMEM((blocks * rows, half), BF16), staging(rows, blocks * rows, half)],
        name="residual_rows",
        **params(2 * weight.size * half, 2 * weight.size + 4 * blocks * rows * half, grant=12),
    )(order, weight, *stack)


def zero_grad_kernel(blocks, first, count, order, dp_order, *refs):
    cots, refs = refs[:count], refs[count:]
    sides, refs = (refs[:blocks], refs[blocks : 2 * blocks]), refs[2 * blocks :]
    before = None
    if first:
        before, out, lhs, rhs, stage, parked, loads, buf, sems = refs
    else:
        buf, lhs, rhs, stage, parked, loads = refs
    rows, half = sides[0][0].shape[1:]
    group = order[blocks]
    moves, places = [], []
    for part in range(count):
        slot = part // 2 * 2 + (dp_order[first + part] & 1)
        both = pl.ds(pl.multiple_of(slot * 2 * half, 2 * half), 2 * half)
        moves.append((cots[part], lhs.at[:, both]))
        for side, owner in enumerate((group, 1 - group)):
            lanes = pl.ds(pl.multiple_of((slot * 2 + owner) * half, half), half)
            values = []
            for place in range(blocks):
                if rows % 16:
                    at = (part * 2 + side) * blocks + place
                    target = parked.at[at]
                    values.append(lambda at=at: parked[at])
                else:
                    offset = pl.multiple_of(order[side * (blocks + 1) + place] * rows, 16)
                    target = rhs.at[pl.ds(offset, rows), lanes]
                moves.append((sides[side][place].at[part], target))
            places.append((lanes, values, side * (blocks + 1)))
    moves = [pltpu.make_async_copy(a, b, loads.at[k]) for k, (a, b) in enumerate(moves)]
    for move in moves:
        move.start()
    for move in moves:
        move.wait()
    if rows % 16:
        for lanes, values, shift in places:
            place_blocks(rhs, lanes, stage, order, values, rows, shift)
    copies = []
    for k, (start, size) in enumerate(pieces(0, blocks * rows)):
        columns = pl.ds(start, size)
        value = against_rows(lhs[...], rhs[columns, :])
        buf[:, columns] = value if before is None else before[:, columns] + value
        if before is not None:
            copies.append(pltpu.make_async_copy(buf.at[:, columns], out.at[:, columns], sems.at[k]))
            copies[-1].start()
    for copy in copies:
        copy.wait()


def zero_projection_grad(order, dp_order, first, cots, mine, other, before, name):
    blocks, (count, rows, half) = len(mine), mine[0].shape
    features, tokens = blocks * rows, count * 2 * half
    extra = [] if before is None else [before]
    scratch = [
        pltpu.VMEM((rows, tokens), BF16),
        pltpu.VMEM((features, tokens), BF16),
        staging(rows, features, half),
        pltpu.VMEM((count * 2 * blocks, rows, half) if rows % 16 else (1, 8, 128), BF16),
        pltpu.SemaphoreType.DMA((count * (2 * blocks + 1),)),
    ]
    if extra:
        scratch += [
            pltpu.VMEM((rows, features), F32),
            pltpu.SemaphoreType.DMA((len(pieces(0, features)),)),
        ]
    return pl.pallas_call(
        functools.partial(zero_grad_kernel, blocks, first, count),
        out_shape=struct((rows, features), F32),
        in_specs=[SCALARS] * 2 + [ANYWHERE] * (count + 2 * blocks) + [WHOLE] * len(extra),
        out_specs=HELD if extra else WHOLE,
        scratch_shapes=scratch,
        name=name,
        **params(2 * tokens * rows * features, 4 * rows * features + 2 * tokens * (rows + features), grant=28),
    )(order, dp_order, *cots, *mine, *other, *extra)


def steps(values, level, *during):
    got = [step(value, level) for value in values]
    return list(lax.optimization_barrier((tuple(got),) + during)[0]) if during else got


def direct(values, *during):
    got = [send(value, place + 1) for place, value in enumerate(values)]
    return list(lax.optimization_barrier((tuple(got),) + during)[0])


def local(acts, modulation, w_in, w_out, zero_weight, cotangent):
    own_cot = cotangent[0]
    features, tokens = acts.shape[1:]
    hidden = w_in.shape[1]
    rows = own_cot.shape[0]
    half = tokens // 2
    blocks, levels = lax.axis_size("fsdp"), stages()
    parts = lax.axis_size("dp")
    group = lax.axis_index("grp").astype(jnp.int32)
    me = lax.axis_index("fsdp").astype(jnp.int32)
    is_control = group == 0
    places = block_order(group, me)
    order = jnp.concatenate([places, group[None], block_order(1 - group, me)])
    dp_order = lax.axis_index("dp").astype(jnp.int32) ^ jnp.arange(parts, dtype=jnp.int32)

    arrived = swap_grp(own_cot)
    own_term, sent, normed, stats, cot0, cot1_rows = prepare(
        order, acts, modulation, own_cot, arrived, zero_weight, blocks
    )
    split, cut = split_rows(hidden)
    slope_a, total, mod = forward_first(after(normed, *sent), modulation, w_in, w_out, split, "forward_first")
    own_mod = block_of(mod, me, rows)
    own_gate = own_mod[:, 2:3]
    got = direct(sent, total)
    up_half = own_term + cot0.astype(F32) + sum(value.astype(F32) for value in got)
    up_rows = jnp.where(is_control, jnp.concatenate([up_half, swap_grp(up_half)], 1), own_cot.astype(F32))
    grad_rows = (own_gate * up_rows).astype(BF16)

    slope_b, kept, sent = forward_last(
        order, after(normed, grad_rows), total, w_in, w_out, split, blocks, "forward_last"
    )
    gathered = [grad_rows] + direct([grad_rows] * (blocks - 1), kept)
    grad, total = backward_first(
        order, after(gathered, *sent), slope_a, slope_b, w_in, w_out, cut, "backward_first"
    )
    got = direct(sent, total)
    own_values = block_of(acts[0], me, rows).astype(F32)
    sums = own_values + own_gate * (kept + sum(value.astype(F32) for value in got))
    out_rows = sums.astype(BF16)

    out_half = jnp.where(is_control, out_rows[:, :half], swap_grp(out_rows[:, half:]))
    far = gather_dp(out_half)[1:]
    sent, kept, token_sums = backward_last(
        order, after(grad, out_half), total, slope_a, slope_b, acts, stats, mod, w_in, w_out, cut, blocks, "backward_last"
    )
    far, out_half, sent, kept, token_sums = lax.optimization_barrier((far, out_half, sent, kept, token_sums))

    gathers = [[jnp.stack([out_half, far[0]])], [jnp.stack(far[1:])]]
    cots = gather_dp(after(cot1_rows, token_sums))
    for level in range(levels):
        got = steps(sent, level)
        gathers = [gather + steps(gather, level) for gather in gathers]
        if level + 1 < levels:
            sent, kept, token_sums = fold(got, kept, token_sums)
    more = unpack_sums(got[0][-16:])
    plain, along = token_sums[0:1] + more[0], token_sums[1:2] + more[1]
    kept = [kept[0] + got[0][:rows].astype(F32)]
    mean, inv = stats[0:1], stats[1:2]
    back = inv * (
        kept[0] * (1.0 + own_mod[:, 1:2]) - plain / features - (own_values - mean) * inv * (along / features)
    )
    residual = residual_rows(order, zero_weight, gathers[0])
    residual = jnp.concatenate([swap_grp(residual), residual], 1)
    block_rows = jnp.where(is_control, out_rows, (sums + residual).astype(BF16))

    others = [[swap_grp(value) for value in gather] for gather in gathers]
    zero_grad = zero_projection_grad(
        order, dp_order, 0, cots[:2], gathers[0], others[0], None, "zero_projection_grad_first"
    )
    zero_grad = zero_projection_grad(
        order, dp_order, 2, cots[2:], gathers[1], others[1], zero_grad, "zero_projection_grad_last"
    )
    return (block_rows[None], (up_rows + back)[None], zero_grad)


def solution(mesh):
    placed = (
        P("grp", None, "dp"),
        P("grp", None, None),
        P("grp", "fsdp", None),
        P("grp", "fsdp", None),
        P("fsdp", None),
        P("grp", "fsdp", "dp"),
    )
    return jax.shard_map(
        local,
        mesh=mesh,
        in_specs=placed,
        out_specs=(P("grp", "fsdp", "dp"), P("grp", "fsdp", "dp"), P("fsdp", None)),
        check_vma=False,
    )
```

```python
import functools

import jax
import jax.numpy as jnp
from jax import lax
from jax.experimental import pallas as pl
from jax.experimental.pallas import tpu as pltpu
from jax.sharding import PartitionSpec as P

EPSILON = 1e-06
SQRT_2_OVER_PI = 0.7978845608028654
CHUNK = 512
AHEAD = 3
MIB = 1024 * 1024
F32, BF16 = jnp.float32, jnp.bfloat16
WHOLE = pl.BlockSpec(memory_space=pltpu.VMEM)
HELD = pl.BlockSpec(memory_space=pltpu.HBM)
ANYWHERE = pl.BlockSpec(memory_space=pl.ANY)
SCALARS = pl.BlockSpec(memory_space=pltpu.SMEM)


def pieces(start, stop, size=CHUNK):
    return [(at, min(size, stop - at)) for at in range(start, stop, size)]


def split_rows(hidden):
    units = hidden // CHUNK
    return CHUNK * max(units // 2, 1), (hidden - 1) // CHUNK * CHUNK


def after(value, *others):
    return lax.optimization_barrier((value,) + others)[0]


def swap_grp(value):
    return lax.ppermute(value, "grp", [(0, 1), (1, 0)])


def stages():
    return (lax.axis_size("fsdp") - 1).bit_length()


def step(value, stage):
    length, bits = lax.axis_size("fsdp"), stages()
    pairs = []
    for group, bit in ((0, stage), (1, bits - 1 - stage)):
        pairs += [(group * length + i, group * length + (i ^ (1 << bit))) for i in range(length)]
    return lax.ppermute(value, ("grp", "fsdp"), pairs)


def block_order(group, me):
    length, bits = lax.axis_size("fsdp"), stages()
    turned = [sum(((v >> b) & 1) << (bits - 1 - b) for b in range(bits)) for v in range(length)]
    up, down = jnp.arange(length, dtype=jnp.int32), jnp.array(turned, jnp.int32)
    return me ^ jnp.where(group == 0, up, down)


def send(value, place):
    length, bits = lax.axis_size("fsdp"), stages()
    turned = sum(((place >> b) & 1) << (bits - 1 - b) for b in range(bits))
    pairs = []
    for group, mask in ((0, place), (1, turned)):
        pairs += [(group * length + i, group * length + (i ^ mask)) for i in range(length)]
    return lax.ppermute(value, ("grp", "fsdp"), pairs)


def gather_dp(value):
    length = lax.axis_size("dp")
    return [value] + [
        lax.ppermute(value, "dp", [(i, i ^ mask) for i in range(length)]) for mask in range(1, length)
    ]


def block_of(value, index, rows):
    return lax.dynamic_slice_in_dim(value, index * rows, rows, 0)


def split_three(value):
    high = value.astype(BF16)
    rest = value - high.astype(F32)
    mid = rest.astype(BF16)
    return high, mid, (rest - mid.astype(F32)).astype(BF16)


def pack_sums(plain, along):
    tail = [part.astype(F32) for part in split_three(plain) + split_three(along)]
    return jnp.concatenate(tail + [jnp.zeros((10, plain.shape[1]), F32)], 0).astype(BF16)


def unpack_sums(tail):
    tail = tail.astype(F32)
    return tail[0:1] + tail[1:2] + tail[2:3], tail[3:4] + tail[4:5] + tail[5:6]


def gelu_and_slope(v):
    square = v * v
    t = jnp.tanh(SQRT_2_OVER_PI * (v + 0.044715 * (square * v)))
    rise = 0.5 * (1.0 + t)
    slope = rise + 0.5 * v * (1.0 - t * t) * (SQRT_2_OVER_PI * (1.0 + (3 * 0.044715) * square))
    return v * rise, slope


class Stream:
    def __init__(self, first, first_buf, second, second_buf, parts, base, sems):
        def copy(weight, buf, part):
            return weight.at[0, pl.ds(part[0], part[1]), :], buf.at[pl.ds(part[0] - base, part[1]), :]

        pairs = [copy(first, first_buf, parts[0])]
        for k, part in enumerate(parts):
            if k + 1 < len(parts):
                pairs.append(copy(first, first_buf, parts[k + 1]))
            pairs.append(copy(second, second_buf, part))
        self.copies = [pltpu.make_async_copy(a, b, sems.at[k]) for k, (a, b) in enumerate(pairs)]
        self.next = 0
        for item in self.copies[:AHEAD]:
            item.start()

    def take(self):
        k = self.next
        self.copies[k].wait()
        if k + AHEAD < len(self.copies):
            self.copies[k + AHEAD].start()
        self.next = k + 1


def pipelined(parts, product, finish):
    held = None
    for part in parts:
        value = product(*part)
        if held is not None:
            finish(*held, False)
        held = part + (value,)
    finish(*held, True)


def params(flops, moved, transcendentals=0, grant=50):
    return dict(
        compiler_params=pltpu.CompilerParams(vmem_limit_bytes=grant * MIB),
        cost_estimate=pl.CostEstimate(flops=flops, bytes_accessed=moved, transcendentals=transcendentals),
    )


def struct(shape, dtype):
    return jax.ShapeDtypeStruct(shape, dtype)


def staging(rows, features, lanes):
    return pltpu.VMEM((features, lanes) if rows % 16 else (8, 128), F32)


def place_blocks(target, lanes, stage, order, blocks, rows, first=0):
    for place, value in enumerate(blocks):
        if rows % 16:
            stage[pl.ds(pl.multiple_of(order[first + place] * rows, 8), rows), :] = value().astype(F32)
        else:
            target[pl.ds(pl.multiple_of(order[first + place] * rows, 16), rows), lanes] = value()
    if rows % 16:
        target[:, lanes] = stage[...].astype(target.dtype)


def turn_modulation(modulation, columns):
    for start, size in pieces(0, modulation.shape[2], 128):
        rows = modulation[0, :, pl.ds(start, size)]
        columns[pl.ds(start, size), :] = jnp.concatenate([rows, jnp.zeros((5, size), F32)], 0).T


def normalize(acts, modulation, normed, stats):
    features, tokens = acts.shape[1:]
    parts = pieces(0, features, 128)
    total = jnp.zeros((1, tokens), F32)
    for start, size in parts:
        total += jnp.sum(acts[0, pl.ds(start, size), :].astype(F32), 0, keepdims=True)
    mean = total / features
    total = jnp.zeros((1, tokens), F32)
    for start, size in parts:
        centred = acts[0, pl.ds(start, size), :].astype(F32) - mean
        total += jnp.sum(centred * centred, 0, keepdims=True)
    inv = lax.rsqrt(total / features + EPSILON)
    stats[0:1, :] = mean
    stats[1:2, :] = inv
    for start, size in parts:
        rows = pl.ds(start, size)
        xhat = (acts[0, rows, :].astype(F32) - mean) * inv
        shift, scale = modulation[0, 0:1, rows], modulation[0, 1:2, rows]
        normed[:, rows] = (xhat.T * (1.0 + scale) + shift).astype(BF16)


def against_rows(columns, weight):
    return lax.dot_general(columns, weight, (((1,), (1,)), ((), ())), preferred_element_type=F32)


def accumulate(total, part, weight, before, finish):
    for at, size in pieces(0, weight.shape[1]):
        columns = pl.ds(at, size)
        value = jnp.dot(part, weight[:, columns], preferred_element_type=F32)
        if before is not None:
            value = value + before[:, columns]
        if finish is None:
            total[:, columns] = value
        else:
            finish(at, size, value)


def forward_products(stream, parts, base, normed, in_buf, out_buf, slope_out, total, before, last):
    state = [before]

    def product(at, size):
        stream.take()
        return against_rows(normed[...], in_buf[pl.ds(at - base, size), :])

    def finish(at, size, pre, final):
        rows = pl.ds(at - base, size)
        hidden, slope = gelu_and_slope(pre)
        slope_out[:, rows] = slope
        stream.take()
        accumulate(total, hidden.astype(BF16), out_buf.at[rows, :], state[0], last if final else None)
        state[0] = total

    pipelined(parts, product, finish)


def forward_first_kernel(normed, modulation, w_in, w_out, slope_out, total, mod, in_buf, out_buf, sems):
    parts = pieces(0, slope_out.shape[1])
    stream = Stream(w_in, in_buf, w_out, out_buf, parts, 0, sems)
    turn_modulation(modulation, mod)
    forward_products(stream, parts, 0, normed, in_buf, out_buf, slope_out, total, None, None)


def forward_last_kernel(start, order, normed, before, w_in, w_out, slope_out, *refs):
    outs, (in_buf, out_buf, total, full, sems) = refs[:-5], refs[-5:]
    parts = pieces(start, start + slope_out.shape[1])
    stream = Stream(w_in, in_buf, w_out, out_buf, parts, start, sems)

    def last(at, size, value):
        full[pl.ds(at, size), :] = value.T

    forward_products(stream, parts, start, normed, in_buf, out_buf, slope_out, total, before, last)
    write_blocks(order, full, outs)


def layer_scratch(part, features):
    return [
        pltpu.VMEM((part, features), BF16),
        pltpu.VMEM((part, features), BF16),
    ]


def layer_params(part, features, tokens, transcendentals):
    return params(4 * part * features * tokens, 4 * part * features + 4 * features * tokens, transcendentals)


def forward_first(normed, modulation, w_in, w_out, part, name):
    tokens, features = normed.shape
    return pl.pallas_call(
        forward_first_kernel,
        out_shape=(struct((tokens, part), F32), struct((tokens, features), F32), struct((features, 8), F32)),
        in_specs=[WHOLE, WHOLE, HELD, HELD],
        out_specs=[WHOLE] * 3,
        scratch_shapes=layer_scratch(part, features) + [pltpu.SemaphoreType.DMA((2 * len(pieces(0, part)),))],
        name=name,
        **layer_params(part, features, tokens, part * tokens),
    )(normed, modulation, w_in, w_out)


def forward_last(order, normed, before, w_in, w_out, start, blocks, name):
    hidden, features = w_in.shape[1:]
    tokens, part, rows = before.shape[0], hidden - start, features // blocks
    slope, *outs = pl.pallas_call(
        functools.partial(forward_last_kernel, start),
        out_shape=[struct((tokens, part), F32), struct((rows, tokens), F32)]
        + [struct((rows, tokens), BF16)] * (blocks - 1),
        in_specs=[SCALARS, WHOLE, WHOLE, HELD, HELD],
        out_specs=[WHOLE] * (blocks + 1),
        scratch_shapes=layer_scratch(part, features)
        + [
            pltpu.VMEM((tokens, features), F32),
            pltpu.VMEM((features, tokens), F32),
            pltpu.SemaphoreType.DMA((2 * len(pieces(start, hidden)),)),
        ],
        name=name,
        **layer_params(part, features, tokens, part * tokens),
    )(order, normed, before, w_in, w_out)
    return slope, outs[0], outs[1:]


def write_blocks(order, full, outs):
    for place, target in enumerate(outs):
        rows = target.shape[0]
        offset = pl.multiple_of(order[place] * rows, 8)
        target[...] = full[pl.ds(offset, rows), :].astype(target.dtype)


def backward_products(stream, parts, base, grad, slopes, in_buf, out_buf, total, before, last):
    state = [before]

    def product(at, size):
        stream.take()
        return against_rows(grad[...], out_buf[pl.ds(at - base, size), :])

    def finish(at, size, value, final):
        rows = pl.ds(at - base, size)
        seen = slopes[0].shape[1]
        slope = slopes[0][:, pl.ds(at, size)] if at < seen else slopes[1][:, pl.ds(at - seen, size)]
        stream.take()
        accumulate(total, (value * slope).astype(BF16), in_buf.at[rows, :], state[0], last if final else None)
        state[0] = total

    pipelined(parts, product, finish)


def backward_first_kernel(blocks, part, order, *refs):
    pieces_in, (slope_a, slope_b, w_in, w_out, grad, total, in_buf, out_buf, full, stage, sems) = refs[:blocks], refs[blocks:]
    parts = pieces(0, part)
    stream = Stream(w_out, out_buf, w_in, in_buf, parts, 0, sems)
    values = [lambda ref=ref: ref[...] for ref in pieces_in]
    place_blocks(full, slice(None), stage, order, values, pieces_in[0].shape[0])
    for start, size in pieces(0, full.shape[0], 128):
        rows = pl.ds(start, size)
        grad[:, rows] = full[rows, :].astype(F32).T.astype(BF16)
    backward_products(stream, parts, 0, grad, (slope_a, slope_b), in_buf, out_buf, total, None, None)


def backward_first(order, gathered, slope_a, slope_b, w_in, w_out, part, name):
    hidden, features = w_in.shape[1:]
    blocks, (rows, tokens) = len(gathered), gathered[0].shape
    return pl.pallas_call(
        functools.partial(backward_first_kernel, blocks, part),
        out_shape=(struct((tokens, features), BF16), struct((tokens, features), F32)),
        in_specs=[SCALARS] + [WHOLE] * (blocks + 2) + [HELD, HELD],
        out_specs=[WHOLE] * 2,
        scratch_shapes=layer_scratch(part, features)
        + [
            pltpu.VMEM((features, tokens), BF16),
            staging(rows, features, tokens),
            pltpu.SemaphoreType.DMA((2 * len(pieces(0, part)),)),
        ],
        name=name,
        **layer_params(part, features, tokens, 0),
    )(order, *gathered, slope_a, slope_b, w_in, w_out)


def backward_last_kernel(start, rows, order, grad, before, slope_a, slope_b, acts, stats, mod, w_in, w_out, *refs):
    outs, (sums_out, in_buf, out_buf, total, full, sems) = refs[:-6], refs[-6:]
    hidden, (features, tokens) = w_in.shape[1], full.shape
    parts = pieces(start, hidden)
    stream = Stream(w_out, out_buf, w_in, in_buf, parts, start, sems)
    mean, inv = stats[0:1, :], stats[1:2, :]
    sums = [jnp.zeros((1, tokens), F32), jnp.zeros((1, tokens), F32)]

    def last(at, size, value):
        at = pl.ds(at, size)
        value = value.T
        full[at, :] = value
        scaled = value * (1.0 + mod[at, 1:2])
        xhat = (acts[0, at, :].astype(F32) - mean) * inv
        sums[0] += jnp.sum(scaled, 0, keepdims=True)
        sums[1] += jnp.sum(scaled * xhat, 0, keepdims=True)

    backward_products(stream, parts, start, grad, (slope_a, slope_b), in_buf, out_buf, total, before, last)
    count = len(outs) // 2
    padded = outs[0].shape[0] - 16
    tail = pack_sums(*sums)
    for place in range(count):
        offset = pl.multiple_of(order[2 * place] * rows, 8)
        outs[count + place][...] = full[pl.ds(offset, rows), :]
        offset = pl.multiple_of(order[2 * place + 1] * rows, 8)
        block = full[pl.ds(offset, rows), :]
        if padded > rows:
            block = jnp.concatenate([block, jnp.zeros((padded - rows, tokens), F32)], 0)
        outs[place][:padded, :] = block.astype(BF16)
        outs[place][padded:, :] = tail
    sums_out[0:1, :] = sums[0]
    sums_out[1:2, :] = sums[1]


def backward_last(order, grad, before, slope_a, slope_b, acts, stats, mod, w_in, w_out, start, blocks, name):
    hidden, features = w_in.shape[1:]
    tokens, part, rows, count = before.shape[0], hidden - start, features // blocks, blocks // 2
    outs = pl.pallas_call(
        functools.partial(backward_last_kernel, start, rows),
        out_shape=[struct((-(-rows // 16) * 16 + 16, tokens), BF16)] * count
        + [struct((rows, tokens), F32)] * count
        + [struct((2, tokens), F32)],
        in_specs=[SCALARS] + [WHOLE] * 7 + [HELD, HELD],
        out_specs=[WHOLE] * (blocks + 1),
        scratch_shapes=layer_scratch(part, features)
        + [
            pltpu.VMEM((tokens, features), F32),
            pltpu.VMEM((features, tokens), F32),
            pltpu.SemaphoreType.DMA((2 * len(pieces(start, hidden)),)),
        ],
        name=name,
        **layer_params(part, features, tokens, 0),
    )(order, grad, before, slope_a, slope_b, acts, stats, mod, w_in, w_out)
    return outs[:count], outs[count:-1], outs[-1]


def fold_kernel(rows, count, *refs):
    got, kept, (sums, *outs) = refs[:count], refs[count : 2 * count], refs[2 * count :]
    more = unpack_sums(got[0][-16:, :])
    plain, along = sums[0:1, :] + more[0], sums[1:2, :] + more[1]
    tail = pack_sums(plain, along)
    padded = got[0].shape[0] - 16
    for place in range(count // 2):
        even, odd = 2 * place, 2 * place + 1
        outs[count // 2 + place][...] = kept[even][...] + got[even][:rows, :].astype(F32)
        block = kept[odd][...] + got[odd][:rows, :].astype(F32)
        if padded > rows:
            block = jnp.concatenate([block, jnp.zeros((padded - rows, block.shape[1]), F32)], 0)
        outs[place][:padded, :] = block.astype(BF16)
        outs[place][padded:, :] = tail
    outs[-1][0:1, :] = plain
    outs[-1][1:2, :] = along


def fold(got, kept, sums):
    count, (rows, tokens) = len(kept), kept[0].shape
    outs = pl.pallas_call(
        functools.partial(fold_kernel, rows, count),
        out_shape=[struct(got[0].shape, BF16)] * (count // 2)
        + [struct((rows, tokens), F32)] * (count // 2)
        + [struct((2, tokens), F32)],
        in_specs=[WHOLE] * (2 * count + 1),
        out_specs=[WHOLE] * (count + 1),
        name="fold",
        **params(2 * count * rows * tokens, 8 * count * rows * tokens, grant=12),
    )(*got, *kept, sums)
    return outs[: count // 2], outs[count // 2 : -1], outs[-1]


def prepare_kernel(blocks, order, acts, modulation, own, arrived, weight, *refs):
    outs, (normed, stats, cot0, cot1, full, buf, sem) = refs[:blocks], refs[blocks:]
    load = pltpu.make_async_copy(weight, buf, sem)
    load.start()
    group = order[blocks]
    control = group == 0
    half = cot0.shape[1]
    lanes = pl.ds(pl.multiple_of(group * half, half), half)
    cot0[...] = jnp.where(control, own[:, lanes], arrived[:, lanes])
    mine = jnp.where(control, arrived[:, lanes], own[:, lanes])
    cot1[...] = mine
    normalize(acts, modulation, normed, stats)
    load.wait()
    full[...] = lax.dot_general(mine, buf[...], (((0,), (0,)), ((), ())), preferred_element_type=F32).T
    write_blocks(order, full, outs)


def prepare(order, acts, modulation, own, arrived, weight, blocks):
    rows, tokens = own.shape
    half, features = tokens // 2, weight.shape[1]
    outs = pl.pallas_call(
        functools.partial(prepare_kernel, blocks),
        out_shape=[struct((rows, half), F32)]
        + [struct((rows, half), BF16)] * (blocks - 1)
        + [
            struct((tokens, features), BF16),
            struct((2, tokens), F32),
            struct((rows, half), BF16),
            struct((rows, half), BF16),
        ],
        in_specs=[SCALARS] + [WHOLE] * 4 + [HELD],
        out_specs=[WHOLE] * (blocks + 4),
        scratch_shapes=[
            pltpu.VMEM((features, half), F32),
            pltpu.VMEM(weight.shape, BF16),
            pltpu.SemaphoreType.DMA(()),
        ],
        name="prepare",
        **params(2 * weight.size * half, 2 * weight.size + 4 * blocks * rows * half, grant=50),
    )(order, acts, modulation, own, arrived, weight)
    return outs[0], outs[1:blocks], *outs[blocks:]


def residual_kernel(order, weight, *refs):
    stack, (result, full, stage) = refs[:-3], refs[-3:]
    values = [lambda value=value: value[...] for value in stack]
    place_blocks(full, slice(None), stage, order, values, stack[0].shape[0])
    result[...] = jnp.dot(weight[...], full[...], preferred_element_type=F32)


def residual_rows(order, weight, stack):
    blocks, (rows, half) = len(stack), stack[0].shape
    return pl.pallas_call(
        residual_kernel,
        out_shape=struct((rows, half), F32),
        in_specs=[SCALARS] + [WHOLE] * (blocks + 1),
        out_specs=WHOLE,
        scratch_shapes=[pltpu.VMEM((blocks * rows, half), BF16), staging(rows, blocks * rows, half)],
        name="residual_rows",
        **params(2 * weight.size * half, 2 * weight.size + 4 * blocks * rows * half, grant=12),
    )(order, weight, *stack)


def zero_grad_kernel(blocks, first, count, order, dp_order, *refs):
    cots, refs = (refs[:count], refs[count : 2 * count]), refs[2 * count :]
    stacks = []
    while len(refs) > (9 if first else 6):
        stacks.append((refs[:blocks], refs[blocks : 2 * blocks]))
        refs = refs[2 * blocks :]
    before = None
    if first:
        before, out, lhs, rhs, stage, parked, loads, buf, sems = refs
    else:
        buf, lhs, rhs, stage, parked, loads = refs
    rows, half = cots[0][0].shape
    group = order[blocks]
    moves, places = [], []
    for part in range(count):
        slot = part // 2 * 2 + (dp_order[first + part] & 1)
        for side, owner in enumerate((group, 1 - group)):
            lanes = pl.ds(pl.multiple_of((slot * 2 + owner) * half, half), half)
            moves.append((cots[side][part], lhs.at[:, lanes]))
            values = []
            for place in range(blocks):
                source = stacks[part][side][place] if len(stacks) == count else stacks[0][side][place].at[part]
                if rows % 16:
                    at = (part * 2 + side) * blocks + place
                    target = parked.at[at]
                    values.append(lambda at=at: parked[at])
                else:
                    offset = pl.multiple_of(order[side * (blocks + 1) + place] * rows, 16)
                    target = rhs.at[pl.ds(offset, rows), lanes]
                moves.append((source, target))
            places.append((lanes, values, side * (blocks + 1)))
    moves = [pltpu.make_async_copy(a, b, loads.at[k]) for k, (a, b) in enumerate(moves)]
    for move in moves:
        move.start()
    for move in moves:
        move.wait()
    if rows % 16:
        for lanes, values, shift in places:
            place_blocks(rhs, lanes, stage, order, values, rows, shift)
    copies = []
    for k, (start, size) in enumerate(pieces(0, blocks * rows)):
        columns = pl.ds(start, size)
        value = against_rows(lhs[...], rhs[columns, :])
        buf[:, columns] = value if before is None else before[:, columns] + value
        if before is not None:
            copies.append(pltpu.make_async_copy(buf.at[:, columns], out.at[:, columns], sems.at[k]))
            copies[-1].start()
    for copy in copies:
        copy.wait()


def zero_projection_grad(order, dp_order, first, cots, cots_other, stacks, before, name):
    blocks, (rows, half) = len(stacks[0][0]), cots[0].shape
    count = len(cots)
    features, tokens = blocks * rows, count * 2 * half
    flat = [block for pair in stacks for side in pair for block in side]
    extra = [] if before is None else [before]
    scratch = [
        pltpu.VMEM((rows, tokens), BF16),
        pltpu.VMEM((features, tokens), BF16),
        staging(rows, features, half),
        pltpu.VMEM((count * 2 * blocks, rows, half) if rows % 16 else (1, 8, 128), BF16),
        pltpu.SemaphoreType.DMA((count * 2 * (blocks + 1),)),
    ]
    if extra:
        scratch += [
            pltpu.VMEM((rows, features), F32),
            pltpu.SemaphoreType.DMA((len(pieces(0, features)),)),
        ]
    return pl.pallas_call(
        functools.partial(zero_grad_kernel, blocks, first, count),
        out_shape=struct((rows, features), F32),
        in_specs=[SCALARS] * 2 + [ANYWHERE] * (2 * count + len(flat)) + [WHOLE] * len(extra),
        out_specs=HELD if extra else WHOLE,
        scratch_shapes=scratch,
        name=name,
        **params(2 * tokens * rows * features, 4 * rows * features + 2 * tokens * (rows + features), grant=28),
    )(order, dp_order, *cots, *cots_other, *flat, *extra)


def steps(values, level, *during):
    got = [step(value, level) for value in values]
    return list(lax.optimization_barrier((tuple(got),) + during)[0]) if during else got


def direct(values, *during):
    got = [send(value, place + 1) for place, value in enumerate(values)]
    return list(lax.optimization_barrier((tuple(got),) + during)[0])


def local(acts, modulation, w_in, w_out, zero_weight, cotangent):
    own_cot = cotangent[0]
    features, tokens = acts.shape[1:]
    hidden = w_in.shape[1]
    rows = own_cot.shape[0]
    half = tokens // 2
    blocks, levels = lax.axis_size("fsdp"), stages()
    parts = lax.axis_size("dp")
    group = lax.axis_index("grp").astype(jnp.int32)
    me = lax.axis_index("fsdp").astype(jnp.int32)
    is_control = group == 0
    places = block_order(group, me)
    order = jnp.concatenate([places, group[None], block_order(1 - group, me)])
    dp_order = lax.axis_index("dp").astype(jnp.int32) ^ jnp.arange(parts, dtype=jnp.int32)

    arrived = swap_grp(own_cot)
    own_term, sent, normed, stats, cot0, cot1 = prepare(
        order, acts, modulation, own_cot, arrived, zero_weight, blocks
    )
    split, cut = split_rows(hidden)
    slope_a, total, mod = forward_first(after(normed, *sent), modulation, w_in, w_out, split, "forward_first")
    own_mod = block_of(mod, me, rows)
    own_gate = own_mod[:, 2:3]
    got = direct(sent, total)
    up_half = own_term + cot0.astype(F32) + sum(value.astype(F32) for value in got)
    up_rows = jnp.where(is_control, jnp.concatenate([up_half, swap_grp(up_half)], 1), own_cot.astype(F32))
    grad_rows = (own_gate * up_rows).astype(BF16)

    slope_b, kept, sent = forward_last(
        order, after(normed, grad_rows), total, w_in, w_out, split, blocks, "forward_last"
    )
    gathered = [grad_rows] + direct([grad_rows] * (blocks - 1), kept)
    grad, total = backward_first(
        order, after(gathered, *sent), slope_a, slope_b, w_in, w_out, cut, "backward_first"
    )
    got = direct(sent, total)
    own_values = block_of(acts[0], me, rows).astype(F32)
    sums = own_values + own_gate * (kept + sum(value.astype(F32) for value in got))
    out_rows = sums.astype(BF16)

    out_half = jnp.where(is_control, out_rows[:, :half], swap_grp(out_rows[:, half:]))
    far = gather_dp(out_half)[1:]
    near = [out_half] + [send(out_half, place) for place in range(1, blocks)]
    sent, kept, token_sums = backward_last(
        order, after(grad, out_half), total, slope_a, slope_b, acts, stats, mod, w_in, w_out, cut, blocks, "backward_last"
    )
    far, near, sent, kept, token_sums = lax.optimization_barrier((far, near, sent, kept, token_sums))

    gathers = [[far[0]], [jnp.stack(far[1:])]]
    cots = gather_dp(after(cot1, token_sums))
    for level in range(levels):
        got = steps(sent, level)
        gathers = [gather + steps(gather, level) for gather in gathers]
        if level == 0:
            got, gathers, cots = lax.optimization_barrier((got, gathers, cots))
        if level + 1 < levels:
            sent, kept, token_sums = fold(got, kept, token_sums)
        if level == 0:
            near = after(near, sent[0])
            near_other = [swap_grp(value) for value in near]
            cots_other = [swap_grp(value) for value in cots]
            residual = residual_rows(order, zero_weight, near)
    more = unpack_sums(got[0][-16:])
    plain, along = token_sums[0:1] + more[0], token_sums[1:2] + more[1]
    kept = [kept[0] + got[0][:rows].astype(F32)]
    mean, inv = stats[0:1], stats[1:2]
    back = inv * (
        kept[0] * (1.0 + own_mod[:, 1:2]) - plain / features - (own_values - mean) * inv * (along / features)
    )
    residual = jnp.concatenate([swap_grp(residual), residual], 1)
    block_rows = jnp.where(is_control, out_rows, (sums + residual).astype(BF16))

    stacks = [(near, near_other)] + [(mine, [swap_grp(value) for value in mine]) for mine in gathers]
    zero_grad = zero_projection_grad(
        order, dp_order, 0, cots[:2], cots_other[:2], stacks[:2], None, "zero_projection_grad_first"
    )
    zero_grad = zero_projection_grad(
        order, dp_order, 2, cots[2:], cots_other[2:], stacks[2:], zero_grad, "zero_projection_grad_last"
    )
    return (block_rows[None], (up_rows + back)[None], zero_grad)


def solution(mesh):
    placed = (
        P("grp", None, "dp"),
        P("grp", None, None),
        P("grp", "fsdp", None),
        P("grp", "fsdp", None),
        P("fsdp", None),
        P("grp", "fsdp", "dp"),
    )
    return jax.shard_map(
        local,
        mesh=mesh,
        in_specs=placed,
        out_specs=(P("grp", "fsdp", "dp"), P("grp", "fsdp", "dp"), P("fsdp", None)),
        check_vma=False,
    )
```

```python
import functools

import jax
import jax.numpy as jnp
from jax import lax
from jax.experimental import pallas as pl
from jax.experimental.pallas import tpu as pltpu
from jax.sharding import PartitionSpec as P

EPSILON = 1e-06
SQRT_2_OVER_PI = 0.7978845608028654
CHUNK = 512
AHEAD = 3
MIB = 1024 * 1024
F32, BF16 = jnp.float32, jnp.bfloat16
WHOLE = pl.BlockSpec(memory_space=pltpu.VMEM)
HELD = pl.BlockSpec(memory_space=pltpu.HBM)
ANYWHERE = pl.BlockSpec(memory_space=pl.ANY)
SCALARS = pl.BlockSpec(memory_space=pltpu.SMEM)


def pieces(start, stop, size=CHUNK):
    return [(at, min(size, stop - at)) for at in range(start, stop, size)]


def split_rows(hidden):
    return CHUNK * max(hidden // CHUNK // 2, 1)


def after(value, *others):
    return lax.optimization_barrier((value,) + others)[0]


def swap_grp(value):
    return lax.ppermute(value, "grp", [(0, 1), (1, 0)])


def stages():
    return (lax.axis_size("fsdp") - 1).bit_length()


def step(value, stage):
    length, bits = lax.axis_size("fsdp"), stages()
    pairs = []
    for group, bit in ((0, stage), (1, bits - 1 - stage)):
        pairs += [(group * length + i, group * length + (i ^ (1 << bit))) for i in range(length)]
    return lax.ppermute(value, ("grp", "fsdp"), pairs)


def block_order(group, me):
    length, bits = lax.axis_size("fsdp"), stages()
    turned = [sum(((v >> b) & 1) << (bits - 1 - b) for b in range(bits)) for v in range(length)]
    up, down = jnp.arange(length, dtype=jnp.int32), jnp.array(turned, jnp.int32)
    return me ^ jnp.where(group == 0, up, down)


def send(value, place):
    length, bits = lax.axis_size("fsdp"), stages()
    turned = sum(((place >> b) & 1) << (bits - 1 - b) for b in range(bits))
    pairs = []
    for group, mask in ((0, place), (1, turned)):
        pairs += [(group * length + i, group * length + (i ^ mask)) for i in range(length)]
    return lax.ppermute(value, ("grp", "fsdp"), pairs)


def gather_dp(value, first=1, stop=None):
    length = lax.axis_size("dp")
    return [
        lax.ppermute(value, "dp", [(i, i ^ mask) for i in range(length)]) for mask in range(first, stop or length)
    ]


def block_of(value, index, rows):
    return lax.dynamic_slice_in_dim(value, index * rows, rows, 0)


def split_three(value):
    high = value.astype(BF16)
    rest = value - high.astype(F32)
    mid = rest.astype(BF16)
    return high, mid, (rest - mid.astype(F32)).astype(BF16)


def pack_sums(plain, along):
    tail = [part.astype(F32) for part in split_three(plain) + split_three(along)]
    return jnp.concatenate(tail + [jnp.zeros((10, plain.shape[1]), F32)], 0).astype(BF16)


def unpack_sums(tail):
    tail = tail.astype(F32)
    return tail[0:1] + tail[1:2] + tail[2:3], tail[3:4] + tail[4:5] + tail[5:6]


def gelu_and_slope(v):
    square = v * v
    t = jnp.tanh(SQRT_2_OVER_PI * (v + 0.044715 * (square * v)))
    rise = 0.5 * (1.0 + t)
    slope = rise + 0.5 * v * (1.0 - t * t) * (SQRT_2_OVER_PI * (1.0 + (3 * 0.044715) * square))
    return v * rise, slope


class Stream:
    def __init__(self, first, first_buf, second, second_buf, parts, base, sems):
        def copy(weight, buf, part):
            return weight.at[0, pl.ds(part[0], part[1]), :], buf.at[pl.ds(part[0] - base, part[1]), :]

        pairs = [copy(first, first_buf, parts[0])]
        for k, part in enumerate(parts):
            if k + 1 < len(parts):
                pairs.append(copy(first, first_buf, parts[k + 1]))
            pairs.append(copy(second, second_buf, part))
        self.copies = [pltpu.make_async_copy(a, b, sems.at[k]) for k, (a, b) in enumerate(pairs)]
        self.next = 0
        for item in self.copies[:AHEAD]:
            item.start()

    def take(self):
        k = self.next
        self.copies[k].wait()
        if k + AHEAD < len(self.copies):
            self.copies[k + AHEAD].start()
        self.next = k + 1


def pipelined(parts, product, finish):
    held = None
    for part in parts:
        value = product(*part)
        if held is not None:
            finish(*held, False)
        held = part + (value,)
    finish(*held, True)


def params(flops, moved, transcendentals=0, grant=50):
    return dict(
        compiler_params=pltpu.CompilerParams(vmem_limit_bytes=grant * MIB),
        cost_estimate=pl.CostEstimate(flops=flops, bytes_accessed=moved, transcendentals=transcendentals),
    )


def struct(shape, dtype):
    return jax.ShapeDtypeStruct(shape, dtype)


def staging(rows, features, lanes):
    return pltpu.VMEM((features, lanes) if rows % 16 else (8, 128), F32)


def place_blocks(target, lanes, stage, order, blocks, rows, first=0):
    for place, value in enumerate(blocks):
        if rows % 16:
            stage[pl.ds(pl.multiple_of(order[first + place] * rows, 8), rows), :] = value().astype(F32)
        else:
            target[pl.ds(pl.multiple_of(order[first + place] * rows, 16), rows), lanes] = value()
    if rows % 16:
        target[:, lanes] = stage[...].astype(target.dtype)


def turn_modulation(modulation, columns):
    for start, size in pieces(0, modulation.shape[2], 128):
        rows = modulation[0, :, pl.ds(start, size)]
        columns[pl.ds(start, size), :] = jnp.concatenate([rows, jnp.zeros((5, size), F32)], 0).T


def normalize(acts, modulation, normed, stats):
    features, tokens = acts.shape[1:]
    parts = pieces(0, features, 128)
    total = jnp.zeros((1, tokens), F32)
    for start, size in parts:
        total += jnp.sum(acts[0, pl.ds(start, size), :].astype(F32), 0, keepdims=True)
    mean = total / features
    total = jnp.zeros((1, tokens), F32)
    for start, size in parts:
        centred = acts[0, pl.ds(start, size), :].astype(F32) - mean
        total += jnp.sum(centred * centred, 0, keepdims=True)
    inv = lax.rsqrt(total / features + EPSILON)
    stats[0:1, :] = mean
    stats[1:2, :] = inv
    for start, size in parts:
        rows = pl.ds(start, size)
        xhat = (acts[0, rows, :].astype(F32) - mean) * inv
        shift, scale = modulation[0, 0:1, rows], modulation[0, 1:2, rows]
        normed[:, rows] = (xhat.T * (1.0 + scale) + shift).astype(BF16)


def against_rows(columns, weight):
    return lax.dot_general(columns, weight, (((1,), (1,)), ((), ())), preferred_element_type=F32)


def accumulate(total, part, weight, before, finish):
    for at, size in pieces(0, weight.shape[1]):
        columns = pl.ds(at, size)
        value = jnp.dot(part, weight[:, columns], preferred_element_type=F32)
        if before is not None:
            value = value + before[:, columns]
        if finish is None:
            total[:, columns] = value
        else:
            finish(at, size, value)


def forward_products(stream, parts, base, normed, in_buf, out_buf, slope_out, total, before, last):
    state = [before]

    def product(at, size):
        stream.take()
        return against_rows(normed[...], in_buf[pl.ds(at - base, size), :])

    def finish(at, size, pre, final):
        rows = pl.ds(at - base, size)
        hidden, slope = gelu_and_slope(pre)
        slope_out[:, rows] = slope
        stream.take()
        accumulate(total, hidden.astype(BF16), out_buf.at[rows, :], state[0], last if final else None)
        state[0] = total

    pipelined(parts, product, finish)


def forward_first_kernel(normed, modulation, w_in, w_out, slope_out, total, mod, in_buf, out_buf, sems):
    parts = pieces(0, slope_out.shape[1])
    stream = Stream(w_in, in_buf, w_out, out_buf, parts, 0, sems)
    turn_modulation(modulation, mod)
    forward_products(stream, parts, 0, normed, in_buf, out_buf, slope_out, total, None, None)


def forward_last_kernel(start, order, normed, before, w_in, w_out, slope_out, *refs):
    outs, (in_buf, out_buf, total, full, sems) = refs[:-5], refs[-5:]
    parts = pieces(start, start + slope_out.shape[1])
    stream = Stream(w_in, in_buf, w_out, out_buf, parts, start, sems)

    def last(at, size, value):
        full[pl.ds(at, size), :] = value.T

    forward_products(stream, parts, start, normed, in_buf, out_buf, slope_out, total, before, last)
    write_blocks(order, full, outs)


def layer_scratch(part, features):
    return [
        pltpu.VMEM((part, features), BF16),
        pltpu.VMEM((part, features), BF16),
    ]


def layer_params(part, features, tokens, transcendentals):
    return params(4 * part * features * tokens, 4 * part * features + 4 * features * tokens, transcendentals)


def forward_first(normed, modulation, w_in, w_out, part, name):
    tokens, features = normed.shape
    return pl.pallas_call(
        forward_first_kernel,
        out_shape=(struct((tokens, part), F32), struct((tokens, features), F32), struct((features, 8), F32)),
        in_specs=[WHOLE, WHOLE, HELD, HELD],
        out_specs=[WHOLE] * 3,
        scratch_shapes=layer_scratch(part, features) + [pltpu.SemaphoreType.DMA((2 * len(pieces(0, part)),))],
        name=name,
        **layer_params(part, features, tokens, part * tokens),
    )(normed, modulation, w_in, w_out)


def forward_last(order, normed, before, w_in, w_out, start, blocks, name):
    hidden, features = w_in.shape[1:]
    tokens, part, rows = before.shape[0], hidden - start, features // blocks
    slope, *outs = pl.pallas_call(
        functools.partial(forward_last_kernel, start),
        out_shape=[struct((tokens, part), F32), struct((rows, tokens), F32)]
        + [struct((rows, tokens), BF16)] * (blocks - 1),
        in_specs=[SCALARS, WHOLE, WHOLE, HELD, HELD],
        out_specs=[WHOLE] * (blocks + 1),
        scratch_shapes=layer_scratch(part, features)
        + [
            pltpu.VMEM((tokens, features), F32),
            pltpu.VMEM((features, tokens), F32),
            pltpu.SemaphoreType.DMA((2 * len(pieces(start, hidden)),)),
        ],
        name=name,
        **layer_params(part, features, tokens, part * tokens),
    )(order, normed, before, w_in, w_out)
    return slope, outs[0], outs[1:]


def write_blocks(order, full, outs):
    for place, target in enumerate(outs):
        rows = target.shape[0]
        offset = pl.multiple_of(order[place] * rows, 8)
        target[...] = full[pl.ds(offset, rows), :].astype(target.dtype)


def backward_products(stream, parts, base, grad, slopes, in_buf, out_buf, total, before, last):
    state = [before]

    def product(at, size):
        stream.take()
        return against_rows(grad[...], out_buf[pl.ds(at - base, size), :])

    def finish(at, size, value, final):
        rows = pl.ds(at - base, size)
        seen = slopes[0].shape[1]
        slope = slopes[0][:, pl.ds(at, size)] if at < seen else slopes[1][:, pl.ds(at - seen, size)]
        stream.take()
        accumulate(total, (value * slope).astype(BF16), in_buf.at[rows, :], state[0], last if final else None)
        state[0] = total

    pipelined(parts, product, finish)


def backward_kernel(blocks, rows, order, *refs):
    gathered, refs = refs[:blocks], refs[blocks:]
    slope_a, slope_b, acts, stats, mod, w_in, w_out, *refs = refs
    outs, (sums_out, in_buf, out_buf, total, full, grad, gate_grad, stage, sems) = refs[:-9], refs[-9:]
    hidden, (features, tokens) = w_in.shape[1], full.shape
    parts = pieces(0, hidden)
    stream = Stream(w_out, out_buf, w_in, in_buf, parts, 0, sems)
    values = [lambda ref=ref: ref[...] for ref in gathered]
    place_blocks(gate_grad, slice(None), stage, order, values, rows)
    for start, size in pieces(0, features, 128):
        some = pl.ds(start, size)
        grad[:, some] = gate_grad[some, :].astype(F32).T.astype(BF16)
    mean, inv = stats[0:1, :], stats[1:2, :]
    sums = [jnp.zeros((1, tokens), F32), jnp.zeros((1, tokens), F32)]

    def last(at, size, value):
        at = pl.ds(at, size)
        value = value.T
        full[at, :] = value
        scaled = value * (1.0 + mod[at, 1:2])
        xhat = (acts[0, at, :].astype(F32) - mean) * inv
        sums[0] += jnp.sum(scaled, 0, keepdims=True)
        sums[1] += jnp.sum(scaled * xhat, 0, keepdims=True)

    backward_products(stream, parts, 0, grad, (slope_a, slope_b), in_buf, out_buf, total, None, last)
    count = len(outs) // 2
    padded = outs[0].shape[0] - 16
    tail = pack_sums(*sums)
    for place in range(count):
        offset = pl.multiple_of(order[2 * place] * rows, 8)
        outs[count + place][...] = full[pl.ds(offset, rows), :]
        offset = pl.multiple_of(order[2 * place + 1] * rows, 8)
        block = full[pl.ds(offset, rows), :]
        if padded > rows:
            block = jnp.concatenate([block, jnp.zeros((padded - rows, tokens), F32)], 0)
        outs[place][:padded, :] = block.astype(BF16)
        outs[place][padded:, :] = tail
    sums_out[0:1, :] = sums[0]
    sums_out[1:2, :] = sums[1]


def backward(order, gathered, slope_a, slope_b, acts, stats, mod, w_in, w_out, name):
    hidden, features = w_in.shape[1:]
    blocks, (rows, tokens) = len(gathered), gathered[0].shape
    count = blocks // 2
    outs = pl.pallas_call(
        functools.partial(backward_kernel, blocks, rows),
        out_shape=[struct((-(-rows // 16) * 16 + 16, tokens), BF16)] * count
        + [struct((rows, tokens), F32)] * count
        + [struct((2, tokens), F32)],
        in_specs=[SCALARS] + [WHOLE] * (blocks + 5) + [HELD, HELD],
        out_specs=[WHOLE] * (blocks + 1),
        scratch_shapes=layer_scratch(hidden, features)
        + [
            pltpu.VMEM((tokens, features), F32),
            pltpu.VMEM((features, tokens), F32),
            pltpu.VMEM((tokens, features), BF16),
            pltpu.VMEM((features, tokens), BF16),
            staging(rows, features, tokens),
            pltpu.SemaphoreType.DMA((2 * len(pieces(0, hidden)),)),
        ],
        name=name,
        **layer_params(hidden, features, tokens, 0),
    )(order, *gathered, slope_a, slope_b, acts, stats, mod, w_in, w_out)
    return outs[:count], outs[count:-1], outs[-1]


def fold_kernel(rows, count, *refs):
    got, kept, (sums, *outs) = refs[:count], refs[count : 2 * count], refs[2 * count :]
    more = unpack_sums(got[0][-16:, :])
    plain, along = sums[0:1, :] + more[0], sums[1:2, :] + more[1]
    tail = pack_sums(plain, along)
    padded = got[0].shape[0] - 16
    for place in range(count // 2):
        even, odd = 2 * place, 2 * place + 1
        outs[count // 2 + place][...] = kept[even][...] + got[even][:rows, :].astype(F32)
        block = kept[odd][...] + got[odd][:rows, :].astype(F32)
        if padded > rows:
            block = jnp.concatenate([block, jnp.zeros((padded - rows, block.shape[1]), F32)], 0)
        outs[place][:padded, :] = block.astype(BF16)
        outs[place][padded:, :] = tail
    outs[-1][0:1, :] = plain
    outs[-1][1:2, :] = along


def fold(got, kept, sums):
    count, (rows, tokens) = len(kept), kept[0].shape
    outs = pl.pallas_call(
        functools.partial(fold_kernel, rows, count),
        out_shape=[struct(got[0].shape, BF16)] * (count // 2)
        + [struct((rows, tokens), F32)] * (count // 2)
        + [struct((2, tokens), F32)],
        in_specs=[WHOLE] * (2 * count + 1),
        out_specs=[WHOLE] * (count + 1),
        name="fold",
        **params(2 * count * rows * tokens, 8 * count * rows * tokens, grant=12),
    )(*got, *kept, sums)
    return outs[: count // 2], outs[count // 2 : -1], outs[-1]


def prepare_kernel(blocks, order, acts, modulation, own, arrived, weight, *refs):
    outs, (normed, stats, cot0, cot1_rows, full, buf, sem) = refs[:blocks], refs[blocks:]
    load = pltpu.make_async_copy(weight, buf, sem)
    load.start()
    group = order[blocks]
    control = group == 0
    half = cot0.shape[1]
    lanes = pl.ds(pl.multiple_of(group * half, half), half)
    cot0[...] = jnp.where(control, own[:, lanes], arrived[:, lanes])
    mine = jnp.where(control, arrived[:, lanes], own[:, lanes])
    cot1_rows[...] = jnp.where(control, arrived[...], own[...])
    normalize(acts, modulation, normed, stats)
    load.wait()
    full[...] = lax.dot_general(mine, buf[...], (((0,), (0,)), ((), ())), preferred_element_type=F32).T
    write_blocks(order, full, outs)


def prepare(order, acts, modulation, own, arrived, weight, blocks):
    rows, tokens = own.shape
    half, features = tokens // 2, weight.shape[1]
    outs = pl.pallas_call(
        functools.partial(prepare_kernel, blocks),
        out_shape=[struct((rows, half), F32)]
        + [struct((rows, half), BF16)] * (blocks - 1)
        + [
            struct((tokens, features), BF16),
            struct((2, tokens), F32),
            struct((rows, half), BF16),
            struct((rows, tokens), BF16),
        ],
        in_specs=[SCALARS] + [WHOLE] * 4 + [HELD],
        out_specs=[WHOLE] * (blocks + 4),
        scratch_shapes=[
            pltpu.VMEM((features, half), F32),
            pltpu.VMEM(weight.shape, BF16),
            pltpu.SemaphoreType.DMA(()),
        ],
        name="prepare",
        **params(2 * weight.size * half, 2 * weight.size + 4 * blocks * rows * half, grant=50),
    )(order, acts, modulation, own, arrived, weight)
    return outs[0], outs[1:blocks], *outs[blocks:]


def residual_kernel(order, weight, *refs):
    stack, (result, full, stage) = refs[:-3], refs[-3:]
    values = [lambda value=value: value[...] for value in stack]
    place_blocks(full, slice(None), stage, order, values, stack[0].shape[0])
    result[...] = jnp.dot(weight[...], full[...], preferred_element_type=F32)


def residual_rows(order, weight, stack):
    blocks, (rows, half) = len(stack), stack[0].shape
    return pl.pallas_call(
        residual_kernel,
        out_shape=struct((rows, half), F32),
        in_specs=[SCALARS] + [WHOLE] * (blocks + 1),
        out_specs=WHOLE,
        scratch_shapes=[pltpu.VMEM((blocks * rows, half), BF16), staging(rows, blocks * rows, half)],
        name="residual_rows",
        **params(2 * weight.size * half, 2 * weight.size + 4 * blocks * rows * half, grant=12),
    )(order, weight, *stack)


def zero_grad_kernel(blocks, first, count, order, dp_order, *refs):
    cots, refs = refs[:count], refs[count:]
    stacks = []
    while len(refs) > (9 if first else 6):
        stacks.append((refs[:blocks], refs[blocks : 2 * blocks]))
        refs = refs[2 * blocks :]
    before = None
    if first:
        before, out, lhs, rhs, stage, parked, loads, buf, sems = refs
    else:
        buf, lhs, rhs, stage, parked, loads = refs
    rows, half = stacks[0][0][0].shape[-2:]
    group = order[blocks]
    moves, places = [], []
    for part in range(count):
        slot = part // 2 * 2 + (dp_order[first + part] & 1)
        both = pl.ds(pl.multiple_of(slot * 2 * half, 2 * half), 2 * half)
        moves.append((cots[part], lhs.at[:, both]))
        for side, owner in enumerate((group, 1 - group)):
            lanes = pl.ds(pl.multiple_of((slot * 2 + owner) * half, half), half)
            values = []
            for place in range(blocks):
                if rows % 16:
                    at = (part * 2 + side) * blocks + place
                    target = parked.at[at]
                    values.append(lambda at=at: parked[at])
                else:
                    offset = pl.multiple_of(order[side * (blocks + 1) + place] * rows, 16)
                    target = rhs.at[pl.ds(offset, rows), lanes]
                source = stacks[part][side][place] if len(stacks) == count else stacks[0][side][place].at[part]
                moves.append((source, target))
            places.append((lanes, values, side * (blocks + 1)))
    moves = [pltpu.make_async_copy(a, b, loads.at[k]) for k, (a, b) in enumerate(moves)]
    for move in moves:
        move.start()
    for move in moves:
        move.wait()
    if rows % 16:
        for lanes, values, shift in places:
            place_blocks(rhs, lanes, stage, order, values, rows, shift)
    copies = []
    for k, (start, size) in enumerate(pieces(0, blocks * rows)):
        columns = pl.ds(start, size)
        value = against_rows(lhs[...], rhs[columns, :])
        buf[:, columns] = value if before is None else before[:, columns] + value
        if before is not None:
            copies.append(pltpu.make_async_copy(buf.at[:, columns], out.at[:, columns], sems.at[k]))
            copies[-1].start()
    for copy in copies:
        copy.wait()


def zero_projection_grad(order, dp_order, first, cots, stacks, before, name):
    blocks, (rows, half) = len(stacks[0][0]), stacks[0][0][0].shape[-2:]
    count = len(cots)
    flat = [block for pair in stacks for side in pair for block in side]
    features, tokens = blocks * rows, count * 2 * half
    extra = [] if before is None else [before]
    scratch = [
        pltpu.VMEM((rows, tokens), BF16),
        pltpu.VMEM((features, tokens), BF16),
        staging(rows, features, half),
        pltpu.VMEM((count * 2 * blocks, rows, half) if rows % 16 else (1, 8, 128), BF16),
        pltpu.SemaphoreType.DMA((count * (2 * blocks + 1),)),
    ]
    if extra:
        scratch += [
            pltpu.VMEM((rows, features), F32),
            pltpu.SemaphoreType.DMA((len(pieces(0, features)),)),
        ]
    return pl.pallas_call(
        functools.partial(zero_grad_kernel, blocks, first, count),
        out_shape=struct((rows, features), F32),
        in_specs=[SCALARS] * 2 + [ANYWHERE] * (count + len(flat)) + [WHOLE] * len(extra),
        out_specs=HELD if extra else WHOLE,
        scratch_shapes=scratch,
        name=name,
        **params(2 * tokens * rows * features, 4 * rows * features + 2 * tokens * (rows + features), grant=28),
    )(order, dp_order, *cots, *flat, *extra)


def steps(values, level, *during):
    got = [step(value, level) for value in values]
    return list(lax.optimization_barrier((tuple(got),) + during)[0]) if during else got


def direct(values, *during):
    got = [send(value, place + 1) for place, value in enumerate(values)]
    return list(lax.optimization_barrier((tuple(got),) + during)[0])


def local(acts, modulation, w_in, w_out, zero_weight, cotangent):
    own_cot = cotangent[0]
    features, tokens = acts.shape[1:]
    hidden = w_in.shape[1]
    rows = own_cot.shape[0]
    half = tokens // 2
    blocks, levels = lax.axis_size("fsdp"), stages()
    parts = lax.axis_size("dp")
    group = lax.axis_index("grp").astype(jnp.int32)
    me = lax.axis_index("fsdp").astype(jnp.int32)
    is_control = group == 0
    places = block_order(group, me)
    order = jnp.concatenate([places, group[None], block_order(1 - group, me)])
    dp_order = lax.axis_index("dp").astype(jnp.int32) ^ jnp.arange(parts, dtype=jnp.int32)

    arrived = swap_grp(own_cot)
    own_term, sent, normed, stats, cot0, cot1_rows = prepare(
        order, acts, modulation, own_cot, arrived, zero_weight, blocks
    )
    split = split_rows(hidden)
    slope_a, total, mod = forward_first(after(normed, *sent), modulation, w_in, w_out, split, "forward_first")
    own_mod = block_of(mod, me, rows)
    own_gate = own_mod[:, 2:3]
    got = direct(sent, total)
    up_half = own_term + cot0.astype(F32) + sum(value.astype(F32) for value in got)
    up_rows = jnp.where(is_control, jnp.concatenate([up_half, swap_grp(up_half)], 1), own_cot.astype(F32))
    grad_rows = (own_gate * up_rows).astype(BF16)

    slope_b, kept, sent = forward_last(
        order, after(normed, grad_rows), total, w_in, w_out, split, blocks, "forward_last"
    )
    got, cot_near = lax.optimization_barrier((
        [send(grad_rows, place) for place in range(1, blocks)], gather_dp(cot1_rows, 1, 2), kept
    ))[:2]
    gathered, cots = [grad_rows] + got, [cot1_rows] + cot_near
    norm_sent, norm_kept, token_sums = backward(
        order, after(gathered, *sent), slope_a, slope_b, acts, stats, mod, w_in, w_out, "backward"
    )
    got, cot_far = lax.optimization_barrier((
        [send(value, place + 1) for place, value in enumerate(sent)], gather_dp(cots[0], 2, 3), token_sums
    ))[:2]
    cots = cots + cot_far
    own_values = block_of(acts[0], me, rows).astype(F32)
    sums = own_values + own_gate * (kept + sum(value.astype(F32) for value in got))
    out_rows = sums.astype(BF16)

    out_half = jnp.where(is_control, out_rows[:, :half], swap_grp(out_rows[:, half:]))
    far = gather_dp(out_half)
    sent, kept = after((norm_sent, norm_kept), out_half)
    for level in range(levels):
        got = steps(sent, level)
        if level == 0:
            got, nearest = lax.optimization_barrier((got, far[0]))
            near = [after(out_half, got[0])]
        near = near + steps(near, level)
        if level + 1 < levels:
            sent, kept, token_sums = fold(got, kept, token_sums)
    gathers = [[nearest], [jnp.stack(far[1:])]]
    for level in range(levels):
        gathers = [gather + steps(gather, level) for gather in gathers]
        if level == 0:
            gathers, first = lax.optimization_barrier((gathers, cots[0]))
            cots = cots + gather_dp(first, 3)
    more = unpack_sums(got[0][-16:])
    plain, along = token_sums[0:1] + more[0], token_sums[1:2] + more[1]
    kept = [kept[0] + got[0][:rows].astype(F32)]
    mean, inv = stats[0:1], stats[1:2]
    back = inv * (
        kept[0] * (1.0 + own_mod[:, 1:2]) - plain / features - (own_values - mean) * inv * (along / features)
    )
    residual = residual_rows(order, zero_weight, near)
    residual = jnp.concatenate([swap_grp(residual), residual], 1)
    block_rows = jnp.where(is_control, out_rows, (sums + residual).astype(BF16))

    stacks = [(mine, [swap_grp(value) for value in mine]) for mine in [near] + gathers]
    zero_grad = zero_projection_grad(order, dp_order, 0, cots[:2], stacks[:2], None, "zero_projection_grad_first")
    zero_grad = zero_projection_grad(order, dp_order, 2, cots[2:], stacks[2:], zero_grad, "zero_projection_grad_last")
    return (block_rows[None], (up_rows + back)[None], zero_grad)


def solution(mesh):
    placed = (
        P("grp", None, "dp"),
        P("grp", None, None),
        P("grp", "fsdp", None),
        P("grp", "fsdp", None),
        P("fsdp", None),
        P("grp", "fsdp", "dp"),
    )
    return jax.shard_map(
        local,
        mesh=mesh,
        in_specs=placed,
        out_specs=(P("grp", "fsdp", "dp"), P("grp", "fsdp", "dp"), P("fsdp", None)),
        check_vma=False,
    )
```

```python
import functools

import jax
import jax.numpy as jnp
from jax import lax
from jax.experimental import pallas as pl
from jax.experimental.pallas import tpu as pltpu
from jax.sharding import PartitionSpec as P

EPSILON = 1e-06
SQRT_2_OVER_PI = 0.7978845608028654
CHUNK = 512
AHEAD = 3
MIB = 1024 * 1024
F32, BF16 = jnp.float32, jnp.bfloat16
WHOLE = pl.BlockSpec(memory_space=pltpu.VMEM)
HELD = pl.BlockSpec(memory_space=pltpu.HBM)
ANYWHERE = pl.BlockSpec(memory_space=pl.ANY)
SCALARS = pl.BlockSpec(memory_space=pltpu.SMEM)


def pieces(start, stop, size=CHUNK):
    return [(at, min(size, stop - at)) for at in range(start, stop, size)]


def split_rows(hidden):
    return CHUNK * max(hidden // CHUNK // 2, 1)


def after(value, *others):
    return lax.optimization_barrier((value,) + others)[0]


def swap_grp(value):
    return lax.ppermute(value, "grp", [(0, 1), (1, 0)])


def stages():
    return (lax.axis_size("fsdp") - 1).bit_length()


def step(value, stage):
    length, bits = lax.axis_size("fsdp"), stages()
    pairs = []
    for group, bit in ((0, stage), (1, bits - 1 - stage)):
        pairs += [(group * length + i, group * length + (i ^ (1 << bit))) for i in range(length)]
    return lax.ppermute(value, ("grp", "fsdp"), pairs)


def block_order(group, me):
    length, bits = lax.axis_size("fsdp"), stages()
    turned = [sum(((v >> b) & 1) << (bits - 1 - b) for b in range(bits)) for v in range(length)]
    up, down = jnp.arange(length, dtype=jnp.int32), jnp.array(turned, jnp.int32)
    return me ^ jnp.where(group == 0, up, down)


def send(value, place):
    length, bits = lax.axis_size("fsdp"), stages()
    turned = sum(((place >> b) & 1) << (bits - 1 - b) for b in range(bits))
    pairs = []
    for group, mask in ((0, place), (1, turned)):
        pairs += [(group * length + i, group * length + (i ^ mask)) for i in range(length)]
    return lax.ppermute(value, ("grp", "fsdp"), pairs)


def gather_dp(value, first=1, stop=None):
    length = lax.axis_size("dp")
    return [
        lax.ppermute(value, "dp", [(i, i ^ mask) for i in range(length)]) for mask in range(first, stop or length)
    ]


def block_of(value, index, rows):
    return lax.dynamic_slice_in_dim(value, index * rows, rows, 0)


def split_three(value):
    high = value.astype(BF16)
    rest = value - high.astype(F32)
    mid = rest.astype(BF16)
    return high, mid, (rest - mid.astype(F32)).astype(BF16)


def pack_sums(plain, along):
    tail = [part.astype(F32) for part in split_three(plain) + split_three(along)]
    return jnp.concatenate(tail + [jnp.zeros((10, plain.shape[1]), F32)], 0).astype(BF16)


def unpack_sums(tail):
    tail = tail.astype(F32)
    return tail[0:1] + tail[1:2] + tail[2:3], tail[3:4] + tail[4:5] + tail[5:6]


def gelu_and_slope(v):
    square = v * v
    t = jnp.tanh(SQRT_2_OVER_PI * (v + 0.044715 * (square * v)))
    rise = 0.5 * (1.0 + t)
    slope = rise + 0.5 * v * (1.0 - t * t) * (SQRT_2_OVER_PI * (1.0 + (3 * 0.044715) * square))
    return v * rise, slope


class Stream:
    def __init__(self, first, first_buf, second, second_buf, parts, base, sems):
        def copy(weight, buf, part):
            return weight.at[0, pl.ds(part[0], part[1]), :], buf.at[pl.ds(part[0] - base, part[1]), :]

        pairs = [copy(first, first_buf, parts[0])]
        for k, part in enumerate(parts):
            if k + 1 < len(parts):
                pairs.append(copy(first, first_buf, parts[k + 1]))
            pairs.append(copy(second, second_buf, part))
        self.copies = [pltpu.make_async_copy(a, b, sems.at[k]) for k, (a, b) in enumerate(pairs)]
        self.next = 0
        for item in self.copies[:AHEAD]:
            item.start()

    def take(self):
        k = self.next
        self.copies[k].wait()
        if k + AHEAD < len(self.copies):
            self.copies[k + AHEAD].start()
        self.next = k + 1


def pipelined(parts, product, finish):
    held = None
    for part in parts:
        value = product(*part)
        if held is not None:
            finish(*held, False)
        held = part + (value,)
    finish(*held, True)


def params(flops, moved, transcendentals=0, grant=50):
    return dict(
        compiler_params=pltpu.CompilerParams(vmem_limit_bytes=grant * MIB),
        cost_estimate=pl.CostEstimate(flops=flops, bytes_accessed=moved, transcendentals=transcendentals),
    )


def struct(shape, dtype):
    return jax.ShapeDtypeStruct(shape, dtype)


def staging(rows, features, lanes):
    return pltpu.VMEM((features, lanes) if rows % 16 else (8, 128), F32)


def place_blocks(target, lanes, stage, order, blocks, rows, first=0):
    for place, value in enumerate(blocks):
        if rows % 16:
            stage[pl.ds(pl.multiple_of(order[first + place] * rows, 8), rows), :] = value().astype(F32)
        else:
            target[pl.ds(pl.multiple_of(order[first + place] * rows, 16), rows), lanes] = value()
    if rows % 16:
        target[:, lanes] = stage[...].astype(target.dtype)


def turn_modulation(modulation, columns):
    for start, size in pieces(0, modulation.shape[2], 128):
        rows = modulation[0, :, pl.ds(start, size)]
        columns[pl.ds(start, size), :] = jnp.concatenate([rows, jnp.zeros((5, size), F32)], 0).T


def normalize(acts, modulation, normed, stats):
    features, tokens = acts.shape[1:]
    parts = pieces(0, features, 128)
    total = jnp.zeros((1, tokens), F32)
    for start, size in parts:
        total += jnp.sum(acts[0, pl.ds(start, size), :].astype(F32), 0, keepdims=True)
    mean = total / features
    total = jnp.zeros((1, tokens), F32)
    for start, size in parts:
        centred = acts[0, pl.ds(start, size), :].astype(F32) - mean
        total += jnp.sum(centred * centred, 0, keepdims=True)
    inv = lax.rsqrt(total / features + EPSILON)
    stats[0:1, :] = mean
    stats[1:2, :] = inv
    for start, size in parts:
        rows = pl.ds(start, size)
        xhat = (acts[0, rows, :].astype(F32) - mean) * inv
        shift, scale = modulation[0, 0:1, rows], modulation[0, 1:2, rows]
        normed[:, rows] = (xhat.T * (1.0 + scale) + shift).astype(BF16)


def against_rows(columns, weight):
    return lax.dot_general(columns, weight, (((1,), (1,)), ((), ())), preferred_element_type=F32)


def accumulate(total, part, weight, before, finish):
    for at, size in pieces(0, weight.shape[1]):
        columns = pl.ds(at, size)
        value = jnp.dot(part, weight[:, columns], preferred_element_type=F32)
        if before is not None:
            value = value + before[:, columns]
        if finish is None:
            total[:, columns] = value
        else:
            finish(at, size, value)


def forward_products(stream, parts, base, normed, in_buf, out_buf, slope_out, total, before, last):
    state = [before]

    def product(at, size):
        stream.take()
        return against_rows(normed[...], in_buf[pl.ds(at - base, size), :])

    def finish(at, size, pre, final):
        rows = pl.ds(at - base, size)
        hidden, slope = gelu_and_slope(pre)
        slope_out[:, rows] = slope
        stream.take()
        accumulate(total, hidden.astype(BF16), out_buf.at[rows, :], state[0], last if final else None)
        state[0] = total

    pipelined(parts, product, finish)


def forward_first_kernel(normed, modulation, w_in, w_out, slope_out, total, mod, in_buf, out_buf, sems):
    parts = pieces(0, slope_out.shape[1])
    stream = Stream(w_in, in_buf, w_out, out_buf, parts, 0, sems)
    turn_modulation(modulation, mod)
    forward_products(stream, parts, 0, normed, in_buf, out_buf, slope_out, total, None, None)


def forward_last_kernel(start, order, normed, before, w_in, w_out, slope_out, *refs):
    outs, (in_buf, out_buf, total, full, sems) = refs[:-5], refs[-5:]
    parts = pieces(start, start + slope_out.shape[1])
    stream = Stream(w_in, in_buf, w_out, out_buf, parts, start, sems)

    def last(at, size, value):
        full[pl.ds(at, size), :] = value.T

    forward_products(stream, parts, start, normed, in_buf, out_buf, slope_out, total, before, last)
    write_blocks(order, full, outs)


def layer_scratch(part, features):
    return [
        pltpu.VMEM((part, features), BF16),
        pltpu.VMEM((part, features), BF16),
    ]


def layer_params(part, features, tokens, transcendentals):
    return params(4 * part * features * tokens, 4 * part * features + 4 * features * tokens, transcendentals)


def forward_first(normed, modulation, w_in, w_out, part, name):
    tokens, features = normed.shape
    return pl.pallas_call(
        forward_first_kernel,
        out_shape=(struct((tokens, part), F32), struct((tokens, features), F32), struct((features, 8), F32)),
        in_specs=[WHOLE, WHOLE, HELD, HELD],
        out_specs=[WHOLE] * 3,
        scratch_shapes=layer_scratch(part, features) + [pltpu.SemaphoreType.DMA((2 * len(pieces(0, part)),))],
        name=name,
        **layer_params(part, features, tokens, part * tokens),
    )(normed, modulation, w_in, w_out)


def forward_last(order, normed, before, w_in, w_out, start, blocks, name):
    hidden, features = w_in.shape[1:]
    tokens, part, rows = before.shape[0], hidden - start, features // blocks
    slope, *outs = pl.pallas_call(
        functools.partial(forward_last_kernel, start),
        out_shape=[struct((tokens, part), F32), struct((rows, tokens), F32)]
        + [struct((rows, tokens), BF16)] * (blocks - 1),
        in_specs=[SCALARS, WHOLE, WHOLE, HELD, HELD],
        out_specs=[WHOLE] * (blocks + 1),
        scratch_shapes=layer_scratch(part, features)
        + [
            pltpu.VMEM((tokens, features), F32),
            pltpu.VMEM((features, tokens), F32),
            pltpu.SemaphoreType.DMA((2 * len(pieces(start, hidden)),)),
        ],
        name=name,
        **layer_params(part, features, tokens, part * tokens),
    )(order, normed, before, w_in, w_out)
    return slope, outs[0], outs[1:]


def write_blocks(order, full, outs):
    for place, target in enumerate(outs):
        rows = target.shape[0]
        offset = pl.multiple_of(order[place] * rows, 8)
        target[...] = full[pl.ds(offset, rows), :].astype(target.dtype)


def backward_products(stream, parts, base, grad, slopes, in_buf, out_buf, total, before, last):
    state = [before]

    def product(at, size):
        stream.take()
        return against_rows(grad[...], out_buf[pl.ds(at - base, size), :])

    def finish(at, size, value, final):
        rows = pl.ds(at - base, size)
        seen = slopes[0].shape[1]
        slope = slopes[0][:, pl.ds(at, size)] if at < seen else slopes[1][:, pl.ds(at - seen, size)]
        stream.take()
        accumulate(total, (value * slope).astype(BF16), in_buf.at[rows, :], state[0], last if final else None)
        state[0] = total

    pipelined(parts, product, finish)


def backward_kernel(blocks, rows, order, *refs):
    gathered, refs = refs[:blocks], refs[blocks:]
    slope_a, slope_b, acts, stats, mod, w_in, w_out, *refs = refs
    outs, (sums_out, in_buf, out_buf, total, full, grad, gate_grad, stage, sems) = refs[:-9], refs[-9:]
    hidden, (features, tokens) = w_in.shape[1], full.shape
    parts = pieces(0, hidden)
    stream = Stream(w_out, out_buf, w_in, in_buf, parts, 0, sems)
    values = [lambda ref=ref: ref[...] for ref in gathered]
    place_blocks(gate_grad, slice(None), stage, order, values, rows)
    for start, size in pieces(0, features, 128):
        some = pl.ds(start, size)
        grad[:, some] = gate_grad[some, :].astype(F32).T.astype(BF16)
    mean, inv = stats[0:1, :], stats[1:2, :]
    sums = [jnp.zeros((1, tokens), F32), jnp.zeros((1, tokens), F32)]

    def last(at, size, value):
        at = pl.ds(at, size)
        value = value.T
        full[at, :] = value
        scaled = value * (1.0 + mod[at, 1:2])
        xhat = (acts[0, at, :].astype(F32) - mean) * inv
        sums[0] += jnp.sum(scaled, 0, keepdims=True)
        sums[1] += jnp.sum(scaled * xhat, 0, keepdims=True)

    backward_products(stream, parts, 0, grad, (slope_a, slope_b), in_buf, out_buf, total, None, last)
    count = len(outs) // 2
    padded = outs[0].shape[0] - 16
    tail = pack_sums(*sums)
    for place in range(count):
        offset = pl.multiple_of(order[2 * place] * rows, 8)
        outs[count + place][...] = full[pl.ds(offset, rows), :]
        offset = pl.multiple_of(order[2 * place + 1] * rows, 8)
        block = full[pl.ds(offset, rows), :]
        if padded > rows:
            block = jnp.concatenate([block, jnp.zeros((padded - rows, tokens), F32)], 0)
        outs[place][:padded, :] = block.astype(BF16)
        outs[place][padded:, :] = tail
    sums_out[0:1, :] = sums[0]
    sums_out[1:2, :] = sums[1]


def backward(order, gathered, slope_a, slope_b, acts, stats, mod, w_in, w_out, name):
    hidden, features = w_in.shape[1:]
    blocks, (rows, tokens) = len(gathered), gathered[0].shape
    count = blocks // 2
    outs = pl.pallas_call(
        functools.partial(backward_kernel, blocks, rows),
        out_shape=[struct((-(-rows // 16) * 16 + 16, tokens), BF16)] * count
        + [struct((rows, tokens), F32)] * count
        + [struct((2, tokens), F32)],
        in_specs=[SCALARS] + [WHOLE] * (blocks + 5) + [HELD, HELD],
        out_specs=[WHOLE] * (blocks + 1),
        scratch_shapes=layer_scratch(hidden, features)
        + [
            pltpu.VMEM((tokens, features), F32),
            pltpu.VMEM((features, tokens), F32),
            pltpu.VMEM((tokens, features), BF16),
            pltpu.VMEM((features, tokens), BF16),
            staging(rows, features, tokens),
            pltpu.SemaphoreType.DMA((2 * len(pieces(0, hidden)),)),
        ],
        name=name,
        **layer_params(hidden, features, tokens, 0),
    )(order, *gathered, slope_a, slope_b, acts, stats, mod, w_in, w_out)
    return outs[:count], outs[count:-1], outs[-1]


def fold_kernel(rows, count, *refs):
    got, kept, (sums, *outs) = refs[:count], refs[count : 2 * count], refs[2 * count :]
    more = unpack_sums(got[0][-16:, :])
    plain, along = sums[0:1, :] + more[0], sums[1:2, :] + more[1]
    tail = pack_sums(plain, along)
    padded = got[0].shape[0] - 16
    for place in range(count // 2):
        even, odd = 2 * place, 2 * place + 1
        outs[count // 2 + place][...] = kept[even][...] + got[even][:rows, :].astype(F32)
        block = kept[odd][...] + got[odd][:rows, :].astype(F32)
        if padded > rows:
            block = jnp.concatenate([block, jnp.zeros((padded - rows, block.shape[1]), F32)], 0)
        outs[place][:padded, :] = block.astype(BF16)
        outs[place][padded:, :] = tail
    outs[-1][0:1, :] = plain
    outs[-1][1:2, :] = along


def fold(got, kept, sums):
    count, (rows, tokens) = len(kept), kept[0].shape
    outs = pl.pallas_call(
        functools.partial(fold_kernel, rows, count),
        out_shape=[struct(got[0].shape, BF16)] * (count // 2)
        + [struct((rows, tokens), F32)] * (count // 2)
        + [struct((2, tokens), F32)],
        in_specs=[WHOLE] * (2 * count + 1),
        out_specs=[WHOLE] * (count + 1),
        name="fold",
        **params(2 * count * rows * tokens, 8 * count * rows * tokens, grant=12),
    )(*got, *kept, sums)
    return outs[: count // 2], outs[count // 2 : -1], outs[-1]


def prepare_kernel(blocks, order, acts, modulation, own, arrived, weight, *refs):
    outs, (normed, stats, cot0, cot1_rows, full, buf, sem) = refs[:blocks], refs[blocks:]
    load = pltpu.make_async_copy(weight, buf, sem)
    load.start()
    group = order[blocks]
    control = group == 0
    half = cot0.shape[1]
    lanes = pl.ds(pl.multiple_of(group * half, half), half)
    cot0[...] = jnp.where(control, own[:, lanes], arrived[:, lanes])
    mine = jnp.where(control, arrived[:, lanes], own[:, lanes])
    cot1_rows[...] = jnp.where(control, arrived[...], own[...])
    normalize(acts, modulation, normed, stats)
    load.wait()
    full[...] = lax.dot_general(mine, buf[...], (((0,), (0,)), ((), ())), preferred_element_type=F32).T
    write_blocks(order, full, outs)


def prepare(order, acts, modulation, own, arrived, weight, blocks):
    rows, tokens = own.shape
    half, features = tokens // 2, weight.shape[1]
    outs = pl.pallas_call(
        functools.partial(prepare_kernel, blocks),
        out_shape=[struct((rows, half), F32)]
        + [struct((rows, half), BF16)] * (blocks - 1)
        + [
            struct((tokens, features), BF16),
            struct((2, tokens), F32),
            struct((rows, half), BF16),
            struct((rows, tokens), BF16),
        ],
        in_specs=[SCALARS] + [WHOLE] * 4 + [HELD],
        out_specs=[WHOLE] * (blocks + 4),
        scratch_shapes=[
            pltpu.VMEM((features, half), F32),
            pltpu.VMEM(weight.shape, BF16),
            pltpu.SemaphoreType.DMA(()),
        ],
        name="prepare",
        **params(2 * weight.size * half, 2 * weight.size + 4 * blocks * rows * half, grant=50),
    )(order, acts, modulation, own, arrived, weight)
    return outs[0], outs[1:blocks], *outs[blocks:]


def residual_kernel(order, weight, *refs):
    stack, (result, full, stage) = refs[:-3], refs[-3:]
    values = [lambda value=value: value[...] for value in stack]
    place_blocks(full, slice(None), stage, order, values, stack[0].shape[0])
    result[...] = jnp.dot(weight[...], full[...], preferred_element_type=F32)


def residual_rows(order, weight, stack):
    blocks, (rows, half) = len(stack), stack[0].shape
    return pl.pallas_call(
        residual_kernel,
        out_shape=struct((rows, half), F32),
        in_specs=[SCALARS] + [WHOLE] * (blocks + 1),
        out_specs=WHOLE,
        scratch_shapes=[pltpu.VMEM((blocks * rows, half), BF16), staging(rows, blocks * rows, half)],
        name="residual_rows",
        **params(2 * weight.size * half, 2 * weight.size + 4 * blocks * rows * half, grant=12),
    )(order, weight, *stack)


def zero_grad_kernel(blocks, order, dp_order, *refs):
    refs, (out, lhs, rhs, stage, parked, loads, buf, sems) = refs[:-8], refs[-8:]
    count = len(refs) - 4 * blocks
    cots, refs = refs[:count], refs[count:]
    near, far = [[refs[(k + side) * blocks : (k + side + 1) * blocks] for side in range(2)] for k in (0, 2)]
    rows, half = near[0][0].shape
    group = order[blocks]
    moves, places = [], []
    for part in range(count):
        both = pl.ds(pl.multiple_of(dp_order[part] * 2 * half, 2 * half), 2 * half)
        moves.append((cots[part], lhs.at[:, both]))
        for side, owner in enumerate((group, 1 - group)):
            lanes = pl.ds(pl.multiple_of((dp_order[part] * 2 + owner) * half, half), half)
            values = []
            for place in range(blocks):
                if rows % 16:
                    at = (part * 2 + side) * blocks + place
                    target = parked.at[at]
                    values.append(lambda at=at: parked[at])
                else:
                    offset = pl.multiple_of(order[side * (blocks + 1) + place] * rows, 16)
                    target = rhs.at[pl.ds(offset, rows), lanes]
                moves.append((near[side][place] if part == 0 else far[side][place].at[part - 1], target))
            places.append((lanes, values, side * (blocks + 1)))
    moves = [pltpu.make_async_copy(a, b, loads.at[k]) for k, (a, b) in enumerate(moves)]
    for move in moves:
        move.start()
    for move in moves:
        move.wait()
    if rows % 16:
        for lanes, values, shift in places:
            place_blocks(rhs, lanes, stage, order, values, rows, shift)
    copies = []
    for k, (start, size) in enumerate(pieces(0, blocks * rows)):
        columns = pl.ds(start, size)
        value = against_rows(lhs[...], rhs[columns, :])
        buf[:, columns] = value
        copies.append(pltpu.make_async_copy(buf.at[:, columns], out.at[:, columns], sems.at[k]))
        copies[-1].start()
    for copy in copies:
        copy.wait()


def zero_projection_grad(order, dp_order, cots, near, far, name):
    blocks, (rows, half) = len(near[0]), near[0][0].shape
    count = len(cots)
    features, tokens = blocks * rows, count * 2 * half
    flat = [block for pair in (near, far) for side in pair for block in side]
    return pl.pallas_call(
        functools.partial(zero_grad_kernel, blocks),
        out_shape=struct((rows, features), F32),
        in_specs=[SCALARS] * 2 + [ANYWHERE] * (count + len(flat)),
        out_specs=HELD,
        scratch_shapes=[
            pltpu.VMEM((rows, tokens), BF16),
            pltpu.VMEM((features, tokens), BF16),
            staging(rows, features, half),
            pltpu.VMEM((count * 2 * blocks, rows, half) if rows % 16 else (1, 8, 128), BF16),
            pltpu.SemaphoreType.DMA((count * (2 * blocks + 1),)),
            pltpu.VMEM((rows, features), F32),
            pltpu.SemaphoreType.DMA((len(pieces(0, features)),)),
        ],
        name=name,
        **params(2 * tokens * rows * features, 4 * rows * features + 2 * tokens * (rows + features), grant=32),
    )(order, dp_order, *cots, *flat)


def steps(values, level, *during):
    got = [step(value, level) for value in values]
    return list(lax.optimization_barrier((tuple(got),) + during)[0]) if during else got


def direct(values, *during):
    got = [send(value, place + 1) for place, value in enumerate(values)]
    return list(lax.optimization_barrier((tuple(got),) + during)[0])


def local(acts, modulation, w_in, w_out, zero_weight, cotangent):
    own_cot = cotangent[0]
    features, tokens = acts.shape[1:]
    hidden = w_in.shape[1]
    rows = own_cot.shape[0]
    half = tokens // 2
    blocks, levels = lax.axis_size("fsdp"), stages()
    parts = lax.axis_size("dp")
    group = lax.axis_index("grp").astype(jnp.int32)
    me = lax.axis_index("fsdp").astype(jnp.int32)
    is_control = group == 0
    places = block_order(group, me)
    order = jnp.concatenate([places, group[None], block_order(1 - group, me)])
    dp_order = lax.axis_index("dp").astype(jnp.int32) ^ jnp.arange(parts, dtype=jnp.int32)

    arrived = swap_grp(own_cot)
    own_term, sent, normed, stats, cot0, cot1_rows = prepare(
        order, acts, modulation, own_cot, arrived, zero_weight, blocks
    )
    split = split_rows(hidden)
    slope_a, total, mod = forward_first(after(normed, *sent), modulation, w_in, w_out, split, "forward_first")
    own_mod = block_of(mod, me, rows)
    own_gate = own_mod[:, 2:3]
    got = direct(sent, total)
    up_half = own_term + cot0.astype(F32) + sum(value.astype(F32) for value in got)
    up_rows = jnp.where(is_control, jnp.concatenate([up_half, swap_grp(up_half)], 1), own_cot.astype(F32))
    grad_rows = (own_gate * up_rows).astype(BF16)

    slope_b, kept, sent = forward_last(
        order, after(normed, grad_rows), total, w_in, w_out, split, blocks, "forward_last"
    )
    gathered = [grad_rows] + direct([grad_rows] * (blocks - 1), kept)
    norm_sent, norm_kept, token_sums = backward(
        order, after(gathered, *sent), slope_a, slope_b, acts, stats, mod, w_in, w_out, "backward"
    )
    got = direct(sent, token_sums)
    own_values = block_of(acts[0], me, rows).astype(F32)
    sums = own_values + own_gate * (kept + sum(value.astype(F32) for value in got))
    out_rows = sums.astype(BF16)

    out_half = jnp.where(is_control, out_rows[:, :half], swap_grp(out_rows[:, half:]))
    far = gather_dp(out_half)
    sent, kept = after((norm_sent, norm_kept), out_half)
    for level in range(levels):
        got = steps(sent, level)
        if level == 0:
            got, nearest = lax.optimization_barrier((got, far[0]))
            near = [after(out_half, got[0])]
        near = near + steps(near, level)
        if level + 1 < levels:
            sent, kept, token_sums = fold(got, kept, token_sums)
    others = [jnp.stack([nearest] + far[1:])]
    cots = [cot1_rows]
    for level in range(levels):
        others = others + steps(others, level)
        if level < 2:
            tied = after(cot1_rows, far if level == 0 else cots[-1])
            arrived = gather_dp(tied, 1, 3) if level == 0 else gather_dp(tied, 3)
            others, arrived = lax.optimization_barrier((others, arrived))
            cots = cots + arrived
    more = unpack_sums(got[0][-16:])
    plain, along = token_sums[0:1] + more[0], token_sums[1:2] + more[1]
    kept = [kept[0] + got[0][:rows].astype(F32)]
    mean, inv = stats[0:1], stats[1:2]
    back = inv * (
        kept[0] * (1.0 + own_mod[:, 1:2]) - plain / features - (own_values - mean) * inv * (along / features)
    )
    residual = residual_rows(order, zero_weight, near)
    residual = jnp.concatenate([swap_grp(residual), residual], 1)
    block_rows = jnp.where(is_control, out_rows, (sums + residual).astype(BF16))

    near, far = [(mine, [swap_grp(value) for value in mine]) for mine in (near, others)]
    zero_grad = zero_projection_grad(order, dp_order, cots, near, far, "zero_projection_grad")
    return (block_rows[None], (up_rows + back)[None], zero_grad)


def solution(mesh):
    placed = (
        P("grp", None, "dp"),
        P("grp", None, None),
        P("grp", "fsdp", None),
        P("grp", "fsdp", None),
        P("fsdp", None),
        P("grp", "fsdp", "dp"),
    )
    return jax.shard_map(
        local,
        mesh=mesh,
        in_specs=placed,
        out_specs=(P("grp", "fsdp", "dp"), P("grp", "fsdp", "dp"), P("fsdp", None)),
        check_vma=False,
    )
```

```python
import functools

import jax
import jax.numpy as jnp
from jax import lax
from jax.experimental import pallas as pl
from jax.experimental.pallas import tpu as pltpu
from jax.sharding import PartitionSpec as P

EPSILON = 1e-06
SQRT_2_OVER_PI = 0.7978845608028654
CHUNK = 512
AHEAD = 3
MIB = 1024 * 1024
F32, BF16 = jnp.float32, jnp.bfloat16
WHOLE = pl.BlockSpec(memory_space=pltpu.VMEM)
HELD = pl.BlockSpec(memory_space=pltpu.HBM)
ANYWHERE = pl.BlockSpec(memory_space=pl.ANY)
SCALARS = pl.BlockSpec(memory_space=pltpu.SMEM)


def pieces(start, stop, size=CHUNK):
    return [(at, min(size, stop - at)) for at in range(start, stop, size)]


def split_rows(hidden):
    return CHUNK * max(hidden // CHUNK // 2, 1)


def after(value, *others):
    return lax.optimization_barrier((value,) + others)[0]


def swap_grp(value):
    return lax.ppermute(value, "grp", [(0, 1), (1, 0)])


def stages():
    return (lax.axis_size("fsdp") - 1).bit_length()


def step(value, stage):
    length, bits = lax.axis_size("fsdp"), stages()
    pairs = []
    for group, bit in ((0, stage), (1, bits - 1 - stage)):
        pairs += [(group * length + i, group * length + (i ^ (1 << bit))) for i in range(length)]
    return lax.ppermute(value, ("grp", "fsdp"), pairs)


def block_order(group, me):
    length, bits = lax.axis_size("fsdp"), stages()
    turned = [sum(((v >> b) & 1) << (bits - 1 - b) for b in range(bits)) for v in range(length)]
    up, down = jnp.arange(length, dtype=jnp.int32), jnp.array(turned, jnp.int32)
    return me ^ jnp.where(group == 0, up, down)


def send(value, place):
    length, bits = lax.axis_size("fsdp"), stages()
    turned = sum(((place >> b) & 1) << (bits - 1 - b) for b in range(bits))
    pairs = []
    for group, mask in ((0, place), (1, turned)):
        pairs += [(group * length + i, group * length + (i ^ mask)) for i in range(length)]
    return lax.ppermute(value, ("grp", "fsdp"), pairs)


def gather_dp(value, first=1, stop=None):
    length = lax.axis_size("dp")
    return [
        lax.ppermute(value, "dp", [(i, i ^ mask) for i in range(length)]) for mask in range(first, stop or length)
    ]


def block_of(value, index, rows):
    return lax.dynamic_slice_in_dim(value, index * rows, rows, 0)


def split_three(value):
    high = value.astype(BF16)
    rest = value - high.astype(F32)
    mid = rest.astype(BF16)
    return high, mid, (rest - mid.astype(F32)).astype(BF16)


def pack_sums(plain, along):
    tail = [part.astype(F32) for part in split_three(plain) + split_three(along)]
    return jnp.concatenate(tail + [jnp.zeros((10, plain.shape[1]), F32)], 0).astype(BF16)


def unpack_sums(tail):
    tail = tail.astype(F32)
    return tail[0:1] + tail[1:2] + tail[2:3], tail[3:4] + tail[4:5] + tail[5:6]


def gelu_and_slope(v):
    square = v * v
    t = jnp.tanh(SQRT_2_OVER_PI * (v + 0.044715 * (square * v)))
    rise = 0.5 * (1.0 + t)
    slope = rise + 0.5 * v * (1.0 - t * t) * (SQRT_2_OVER_PI * (1.0 + (3 * 0.044715) * square))
    return v * rise, slope


class Stream:
    def __init__(self, first, first_buf, second, second_buf, parts, base, sems):
        def copy(weight, buf, part):
            return weight.at[0, pl.ds(part[0], part[1]), :], buf.at[pl.ds(part[0] - base, part[1]), :]

        pairs = [copy(first, first_buf, parts[0])]
        for k, part in enumerate(parts):
            if k + 1 < len(parts):
                pairs.append(copy(first, first_buf, parts[k + 1]))
            pairs.append(copy(second, second_buf, part))
        self.copies = [pltpu.make_async_copy(a, b, sems.at[k]) for k, (a, b) in enumerate(pairs)]
        self.next = 0
        for item in self.copies[:AHEAD]:
            item.start()

    def take(self):
        k = self.next
        self.copies[k].wait()
        if k + AHEAD < len(self.copies):
            self.copies[k + AHEAD].start()
        self.next = k + 1


def pipelined(parts, product, finish):
    held = None
    for part in parts:
        value = product(*part)
        if held is not None:
            finish(*held, False)
        held = part + (value,)
    finish(*held, True)


def params(flops, moved, transcendentals=0, grant=50):
    return dict(
        compiler_params=pltpu.CompilerParams(vmem_limit_bytes=grant * MIB),
        cost_estimate=pl.CostEstimate(flops=flops, bytes_accessed=moved, transcendentals=transcendentals),
    )


def struct(shape, dtype):
    return jax.ShapeDtypeStruct(shape, dtype)


def staging(rows, features, lanes):
    return pltpu.VMEM((features, lanes) if rows % 16 else (8, 128), F32)


def place_blocks(target, lanes, stage, order, blocks, rows, first=0):
    for place, value in enumerate(blocks):
        if rows % 16:
            stage[pl.ds(pl.multiple_of(order[first + place] * rows, 8), rows), :] = value().astype(F32)
        else:
            target[pl.ds(pl.multiple_of(order[first + place] * rows, 16), rows), lanes] = value()
    if rows % 16:
        target[:, lanes] = stage[...].astype(target.dtype)


def turn_modulation(modulation, columns):
    for start, size in pieces(0, modulation.shape[2], 128):
        rows = modulation[0, :, pl.ds(start, size)]
        columns[pl.ds(start, size), :] = jnp.concatenate([rows, jnp.zeros((5, size), F32)], 0).T


def normalize(acts, modulation, normed, stats):
    features, tokens = acts.shape[1:]
    parts = pieces(0, features, 128)
    total = jnp.zeros((1, tokens), F32)
    for start, size in parts:
        total += jnp.sum(acts[0, pl.ds(start, size), :].astype(F32), 0, keepdims=True)
    mean = total / features
    total = jnp.zeros((1, tokens), F32)
    for start, size in parts:
        centred = acts[0, pl.ds(start, size), :].astype(F32) - mean
        total += jnp.sum(centred * centred, 0, keepdims=True)
    inv = lax.rsqrt(total / features + EPSILON)
    stats[0:1, :] = mean
    stats[1:2, :] = inv
    for start, size in parts:
        rows = pl.ds(start, size)
        xhat = (acts[0, rows, :].astype(F32) - mean) * inv
        shift, scale = modulation[0, 0:1, rows], modulation[0, 1:2, rows]
        normed[:, rows] = (xhat.T * (1.0 + scale) + shift).astype(BF16)


def against_rows(columns, weight):
    return lax.dot_general(columns, weight, (((1,), (1,)), ((), ())), preferred_element_type=F32)


def accumulate(total, part, weight, before, finish):
    for at, size in pieces(0, weight.shape[1]):
        columns = pl.ds(at, size)
        value = jnp.dot(part, weight[:, columns], preferred_element_type=F32)
        if before is not None:
            value = value + before[:, columns]
        if finish is None:
            total[:, columns] = value
        else:
            finish(at, size, value)


def forward_products(stream, parts, base, normed, in_buf, out_buf, slope_out, total, before, last):
    state = [before]

    def product(at, size):
        stream.take()
        return against_rows(normed[...], in_buf[pl.ds(at - base, size), :])

    def finish(at, size, pre, final):
        rows = pl.ds(at - base, size)
        hidden, slope = gelu_and_slope(pre)
        slope_out[:, rows] = slope
        stream.take()
        accumulate(total, hidden.astype(BF16), out_buf.at[rows, :], state[0], last if final else None)
        state[0] = total

    pipelined(parts, product, finish)


def forward_first_kernel(normed, modulation, w_in, w_out, slope_out, total, mod, in_buf, out_buf, sems):
    parts = pieces(0, slope_out.shape[1])
    stream = Stream(w_in, in_buf, w_out, out_buf, parts, 0, sems)
    turn_modulation(modulation, mod)
    forward_products(stream, parts, 0, normed, in_buf, out_buf, slope_out, total, None, None)


def forward_last_kernel(start, order, normed, before, w_in, w_out, slope_out, *refs):
    outs, (in_buf, out_buf, total, full, sems) = refs[:-5], refs[-5:]
    parts = pieces(start, start + slope_out.shape[1])
    stream = Stream(w_in, in_buf, w_out, out_buf, parts, start, sems)

    def last(at, size, value):
        full[pl.ds(at, size), :] = value.T

    forward_products(stream, parts, start, normed, in_buf, out_buf, slope_out, total, before, last)
    write_blocks(order, full, outs)


def layer_scratch(part, features):
    return [
        pltpu.VMEM((part, features), BF16),
        pltpu.VMEM((part, features), BF16),
    ]


def layer_params(part, features, tokens, transcendentals):
    return params(4 * part * features * tokens, 4 * part * features + 4 * features * tokens, transcendentals)


def forward_first(normed, modulation, w_in, w_out, part, name):
    tokens, features = normed.shape
    return pl.pallas_call(
        forward_first_kernel,
        out_shape=(struct((tokens, part), F32), struct((tokens, features), F32), struct((features, 8), F32)),
        in_specs=[WHOLE, WHOLE, HELD, HELD],
        out_specs=[WHOLE] * 3,
        scratch_shapes=layer_scratch(part, features) + [pltpu.SemaphoreType.DMA((2 * len(pieces(0, part)),))],
        name=name,
        **layer_params(part, features, tokens, part * tokens),
    )(normed, modulation, w_in, w_out)


def forward_last(order, normed, before, w_in, w_out, start, blocks, name):
    hidden, features = w_in.shape[1:]
    tokens, part, rows = before.shape[0], hidden - start, features // blocks
    slope, *outs = pl.pallas_call(
        functools.partial(forward_last_kernel, start),
        out_shape=[struct((tokens, part), F32), struct((rows, tokens), F32)]
        + [struct((rows, tokens), BF16)] * (blocks - 1),
        in_specs=[SCALARS, WHOLE, WHOLE, HELD, HELD],
        out_specs=[WHOLE] * (blocks + 1),
        scratch_shapes=layer_scratch(part, features)
        + [
            pltpu.VMEM((tokens, features), F32),
            pltpu.VMEM((features, tokens), F32),
            pltpu.SemaphoreType.DMA((2 * len(pieces(start, hidden)),)),
        ],
        name=name,
        **layer_params(part, features, tokens, part * tokens),
    )(order, normed, before, w_in, w_out)
    return slope, outs[0], outs[1:]


def write_blocks(order, full, outs):
    for place, target in enumerate(outs):
        rows = target.shape[0]
        offset = pl.multiple_of(order[place] * rows, 8)
        target[...] = full[pl.ds(offset, rows), :].astype(target.dtype)


def backward_products(stream, parts, base, grad, slopes, in_buf, out_buf, total, before, last):
    state = [before]

    def product(at, size):
        stream.take()
        return against_rows(grad[...], out_buf[pl.ds(at - base, size), :])

    def finish(at, size, value, final):
        rows = pl.ds(at - base, size)
        seen = slopes[0].shape[1]
        slope = slopes[0][:, pl.ds(at, size)] if at < seen else slopes[1][:, pl.ds(at - seen, size)]
        stream.take()
        accumulate(total, (value * slope).astype(BF16), in_buf.at[rows, :], state[0], last if final else None)
        state[0] = total

    pipelined(parts, product, finish)


def backward_kernel(blocks, rows, order, *refs):
    gathered, refs = refs[:blocks], refs[blocks:]
    slope_a, slope_b, acts, stats, mod, w_in, w_out, *refs = refs
    outs, (sums_out, in_buf, out_buf, total, full, grad, gate_grad, stage, sems) = refs[:-9], refs[-9:]
    hidden, (features, tokens) = w_in.shape[1], full.shape
    parts = pieces(0, hidden)
    stream = Stream(w_out, out_buf, w_in, in_buf, parts, 0, sems)
    values = [lambda ref=ref: ref[...] for ref in gathered]
    place_blocks(gate_grad, slice(None), stage, order, values, rows)
    for start, size in pieces(0, features, 128):
        some = pl.ds(start, size)
        grad[:, some] = gate_grad[some, :].astype(F32).T.astype(BF16)
    mean, inv = stats[0:1, :], stats[1:2, :]
    sums = [jnp.zeros((1, tokens), F32), jnp.zeros((1, tokens), F32)]

    def last(at, size, value):
        at = pl.ds(at, size)
        value = value.T
        full[at, :] = value
        scaled = value * (1.0 + mod[at, 1:2])
        xhat = (acts[0, at, :].astype(F32) - mean) * inv
        sums[0] += jnp.sum(scaled, 0, keepdims=True)
        sums[1] += jnp.sum(scaled * xhat, 0, keepdims=True)

    backward_products(stream, parts, 0, grad, (slope_a, slope_b), in_buf, out_buf, total, None, last)
    padded = outs[-1].shape[0] - 16
    tail = pack_sums(*sums)
    for place, target in enumerate(outs):
        block = full[pl.ds(pl.multiple_of(order[place] * rows, 8), rows), :]
        if place == 0:
            target[...] = block
            continue
        if padded > rows:
            block = jnp.concatenate([block, jnp.zeros((padded - rows, tokens), F32)], 0)
        target[:padded, :] = block.astype(BF16)
        target[padded:, :] = tail
    sums_out[0:1, :] = sums[0]
    sums_out[1:2, :] = sums[1]


def backward(order, gathered, slope_a, slope_b, acts, stats, mod, w_in, w_out, name):
    hidden, features = w_in.shape[1:]
    blocks, (rows, tokens) = len(gathered), gathered[0].shape
    outs = pl.pallas_call(
        functools.partial(backward_kernel, blocks, rows),
        out_shape=[struct((rows, tokens), F32)]
        + [struct((-(-rows // 16) * 16 + 16, tokens), BF16)] * (blocks - 1)
        + [struct((2, tokens), F32)],
        in_specs=[SCALARS] + [WHOLE] * (blocks + 5) + [HELD, HELD],
        out_specs=[WHOLE] * (blocks + 1),
        scratch_shapes=layer_scratch(hidden, features)
        + [
            pltpu.VMEM((tokens, features), F32),
            pltpu.VMEM((features, tokens), F32),
            pltpu.VMEM((tokens, features), BF16),
            pltpu.VMEM((features, tokens), BF16),
            staging(rows, features, tokens),
            pltpu.SemaphoreType.DMA((2 * len(pieces(0, hidden)),)),
        ],
        name=name,
        **layer_params(hidden, features, tokens, 0),
    )(order, *gathered, slope_a, slope_b, acts, stats, mod, w_in, w_out)
    return outs[0], outs[1:-1], outs[-1]


def prepare_kernel(blocks, order, acts, modulation, own, arrived, weight, *refs):
    outs, (normed, stats, cot0, cot1_rows, full, buf, sem) = refs[:blocks], refs[blocks:]
    load = pltpu.make_async_copy(weight, buf, sem)
    load.start()
    group = order[blocks]
    control = group == 0
    half = cot0.shape[1]
    lanes = pl.ds(pl.multiple_of(group * half, half), half)
    cot0[...] = jnp.where(control, own[:, lanes], arrived[:, lanes])
    mine = jnp.where(control, arrived[:, lanes], own[:, lanes])
    cot1_rows[...] = jnp.where(control, arrived[...], own[...])
    normalize(acts, modulation, normed, stats)
    load.wait()
    full[...] = lax.dot_general(mine, buf[...], (((0,), (0,)), ((), ())), preferred_element_type=F32).T
    write_blocks(order, full, outs)


def prepare(order, acts, modulation, own, arrived, weight, blocks):
    rows, tokens = own.shape
    half, features = tokens // 2, weight.shape[1]
    outs = pl.pallas_call(
        functools.partial(prepare_kernel, blocks),
        out_shape=[struct((rows, half), F32)]
        + [struct((rows, half), BF16)] * (blocks - 1)
        + [
            struct((tokens, features), BF16),
            struct((2, tokens), F32),
            struct((rows, half), BF16),
            struct((rows, tokens), BF16),
        ],
        in_specs=[SCALARS] + [WHOLE] * 4 + [HELD],
        out_specs=[WHOLE] * (blocks + 4),
        scratch_shapes=[
            pltpu.VMEM((features, half), F32),
            pltpu.VMEM(weight.shape, BF16),
            pltpu.SemaphoreType.DMA(()),
        ],
        name="prepare",
        **params(2 * weight.size * half, 2 * weight.size + 4 * blocks * rows * half, grant=50),
    )(order, acts, modulation, own, arrived, weight)
    return outs[0], outs[1:blocks], *outs[blocks:]


def residual_kernel(order, weight, *refs):
    stack, (result, full, stage) = refs[:-3], refs[-3:]
    values = [lambda value=value: value[...] for value in stack]
    place_blocks(full, slice(None), stage, order, values, stack[0].shape[0])
    result[...] = jnp.dot(weight[...], full[...], preferred_element_type=F32)


def residual_rows(order, weight, stack):
    blocks, (rows, half) = len(stack), stack[0].shape
    return pl.pallas_call(
        residual_kernel,
        out_shape=struct((rows, half), F32),
        in_specs=[SCALARS] + [WHOLE] * (blocks + 1),
        out_specs=WHOLE,
        scratch_shapes=[pltpu.VMEM((blocks * rows, half), BF16), staging(rows, blocks * rows, half)],
        name="residual_rows",
        **params(2 * weight.size * half, 2 * weight.size + 4 * blocks * rows * half, grant=12),
    )(order, weight, *stack)


def zero_grad_kernel(blocks, order, dp_order, *refs):
    refs, (out, lhs, rhs, stage, parked, loads, buf, sems) = refs[:-8], refs[-8:]
    count = len(refs) - 4 * blocks
    cots, refs = refs[:count], refs[count:]
    near, far = [[refs[(k + side) * blocks : (k + side + 1) * blocks] for side in range(2)] for k in (0, 2)]
    rows, half = near[0][0].shape
    group = order[blocks]
    moves, places = [], []
    for part in range(count):
        both = pl.ds(pl.multiple_of(dp_order[part] * 2 * half, 2 * half), 2 * half)
        moves.append((cots[part], lhs.at[:, both]))
        for side, owner in enumerate((group, 1 - group)):
            lanes = pl.ds(pl.multiple_of((dp_order[part] * 2 + owner) * half, half), half)
            values = []
            for place in range(blocks):
                if rows % 16:
                    at = (part * 2 + side) * blocks + place
                    target = parked.at[at]
                    values.append(lambda at=at: parked[at])
                else:
                    offset = pl.multiple_of(order[side * (blocks + 1) + place] * rows, 16)
                    target = rhs.at[pl.ds(offset, rows), lanes]
                moves.append((near[side][place] if part == 0 else far[side][place].at[part - 1], target))
            places.append((lanes, values, side * (blocks + 1)))
    moves = [pltpu.make_async_copy(a, b, loads.at[k]) for k, (a, b) in enumerate(moves)]
    for move in moves:
        move.start()
    for move in moves:
        move.wait()
    if rows % 16:
        for lanes, values, shift in places:
            place_blocks(rhs, lanes, stage, order, values, rows, shift)
    copies = []
    for k, (start, size) in enumerate(pieces(0, blocks * rows)):
        columns = pl.ds(start, size)
        value = against_rows(lhs[...], rhs[columns, :])
        buf[:, columns] = value
        copies.append(pltpu.make_async_copy(buf.at[:, columns], out.at[:, columns], sems.at[k]))
        copies[-1].start()
    for copy in copies:
        copy.wait()


def zero_projection_grad(order, dp_order, cots, near, far, name):
    blocks, (rows, half) = len(near[0]), near[0][0].shape
    count = len(cots)
    features, tokens = blocks * rows, count * 2 * half
    flat = [block for pair in (near, far) for side in pair for block in side]
    return pl.pallas_call(
        functools.partial(zero_grad_kernel, blocks),
        out_shape=struct((rows, features), F32),
        in_specs=[SCALARS] * 2 + [ANYWHERE] * (count + len(flat)),
        out_specs=HELD,
        scratch_shapes=[
            pltpu.VMEM((rows, tokens), BF16),
            pltpu.VMEM((features, tokens), BF16),
            staging(rows, features, half),
            pltpu.VMEM((count * 2 * blocks, rows, half) if rows % 16 else (1, 8, 128), BF16),
            pltpu.SemaphoreType.DMA((count * (2 * blocks + 1),)),
            pltpu.VMEM((rows, features), F32),
            pltpu.SemaphoreType.DMA((len(pieces(0, features)),)),
        ],
        name=name,
        **params(2 * tokens * rows * features, 4 * rows * features + 2 * tokens * (rows + features), grant=32),
    )(order, dp_order, *cots, *flat)


def steps(values, level, *during):
    got = [step(value, level) for value in values]
    return list(lax.optimization_barrier((tuple(got),) + during)[0]) if during else got


def direct(values, *during):
    got = [send(value, place + 1) for place, value in enumerate(values)]
    return list(lax.optimization_barrier((tuple(got),) + during)[0])


def local(acts, modulation, w_in, w_out, zero_weight, cotangent):
    own_cot = cotangent[0]
    features, tokens = acts.shape[1:]
    hidden = w_in.shape[1]
    rows = own_cot.shape[0]
    half = tokens // 2
    blocks, levels = lax.axis_size("fsdp"), stages()
    parts = lax.axis_size("dp")
    group = lax.axis_index("grp").astype(jnp.int32)
    me = lax.axis_index("fsdp").astype(jnp.int32)
    is_control = group == 0
    places = block_order(group, me)
    order = jnp.concatenate([places, group[None], block_order(1 - group, me)])
    dp_order = lax.axis_index("dp").astype(jnp.int32) ^ jnp.arange(parts, dtype=jnp.int32)

    arrived = swap_grp(own_cot)
    own_term, sent, normed, stats, cot0, cot1_rows = prepare(
        order, acts, modulation, own_cot, arrived, zero_weight, blocks
    )
    split = split_rows(hidden)
    slope_a, total, mod = forward_first(after(normed, *sent), modulation, w_in, w_out, split, "forward_first")
    own_mod = block_of(mod, me, rows)
    own_gate = own_mod[:, 2:3]
    got = direct(sent, total)
    up_half = own_term + cot0.astype(F32) + sum(value.astype(F32) for value in got)
    up_rows = jnp.where(is_control, jnp.concatenate([up_half, swap_grp(up_half)], 1), own_cot.astype(F32))
    grad_rows = (own_gate * up_rows).astype(BF16)

    slope_b, kept, sent = forward_last(
        order, after(normed, grad_rows), total, w_in, w_out, split, blocks, "forward_last"
    )
    gathered = [grad_rows] + direct([grad_rows] * (blocks - 1), kept)
    norm_grad, sent_norm, token_sums = backward(
        order, after(gathered, *sent), slope_a, slope_b, acts, stats, mod, w_in, w_out, "backward"
    )
    got = direct(sent, token_sums)
    own_values = block_of(acts[0], me, rows).astype(F32)
    sums = own_values + own_gate * (kept + sum(value.astype(F32) for value in got))
    out_rows = sums.astype(BF16)

    out_half = jnp.where(is_control, out_rows[:, :half], swap_grp(out_rows[:, half:]))
    far = gather_dp(out_half, 1, 3)
    far = far + gather_dp(after(out_half, far[-1]), 3)
    got = [send(value, place + 1) for place, value in enumerate(after(sent_norm, out_half))]
    got, far = lax.optimization_barrier((got, far))
    plain, along = token_sums[0:1], token_sums[1:2]
    for value in got:
        more = unpack_sums(value[-16:])
        plain, along = plain + more[0], along + more[1]
        norm_grad = norm_grad + value[:rows].astype(F32)
    near, others, cots = [after(out_half, got[0])], [jnp.stack(far)], [cot1_rows]
    for level in range(levels):
        near = near + steps(near, level)
        others = others + steps(others, level)
        if level < 2:
            tied = after(cot1_rows, far if level == 0 else cots[-1])
            arrived = gather_dp(tied, 1, 3) if level == 0 else gather_dp(tied, 3)
            near, others, arrived = lax.optimization_barrier((near, others, arrived))
            cots = cots + arrived
    mean, inv = stats[0:1], stats[1:2]
    back = inv * (
        norm_grad * (1.0 + own_mod[:, 1:2]) - plain / features - (own_values - mean) * inv * (along / features)
    )
    residual = residual_rows(order, zero_weight, near)
    residual = jnp.concatenate([swap_grp(residual), residual], 1)
    block_rows = jnp.where(is_control, out_rows, (sums + residual).astype(BF16))

    near, far = [(mine, [swap_grp(value) for value in mine]) for mine in (near, others)]
    zero_grad = zero_projection_grad(order, dp_order, cots, near, far, "zero_projection_grad")
    return (block_rows[None], (up_rows + back)[None], zero_grad)


def solution(mesh):
    placed = (
        P("grp", None, "dp"),
        P("grp", None, None),
        P("grp", "fsdp", None),
        P("grp", "fsdp", None),
        P("fsdp", None),
        P("grp", "fsdp", "dp"),
    )
    return jax.shard_map(
        local,
        mesh=mesh,
        in_specs=placed,
        out_specs=(P("grp", "fsdp", "dp"), P("grp", "fsdp", "dp"), P("fsdp", None)),
        check_vma=False,
    )
```

```python
import functools

import jax
import jax.numpy as jnp
from jax import lax
from jax.experimental import pallas as pl
from jax.experimental.pallas import tpu as pltpu
from jax.sharding import PartitionSpec as P

EPSILON = 1e-06
SQRT_2_OVER_PI = 0.7978845608028654
CHUNK = 512
AHEAD = 3
MIB = 1024 * 1024
F32, BF16 = jnp.float32, jnp.bfloat16
WHOLE = pl.BlockSpec(memory_space=pltpu.VMEM)
HELD = pl.BlockSpec(memory_space=pltpu.HBM)
ANYWHERE = pl.BlockSpec(memory_space=pl.ANY)
SCALARS = pl.BlockSpec(memory_space=pltpu.SMEM)


def pieces(start, stop, size=CHUNK):
    return [(at, min(size, stop - at)) for at in range(start, stop, size)]


def split_rows(hidden):
    units = hidden // CHUNK
    return CHUNK * max(units // 2, 1), (hidden - 1) // CHUNK * CHUNK


def after(value, *others):
    return lax.optimization_barrier((value,) + others)[0]


def swap_grp(value):
    return lax.ppermute(value, "grp", [(0, 1), (1, 0)])


def stages():
    return (lax.axis_size("fsdp") - 1).bit_length()


def step(value, stage):
    length, bits = lax.axis_size("fsdp"), stages()
    pairs = []
    for group, bit in ((0, stage), (1, bits - 1 - stage)):
        pairs += [(group * length + i, group * length + (i ^ (1 << bit))) for i in range(length)]
    return lax.ppermute(value, ("grp", "fsdp"), pairs)


def block_order(group, me):
    length, bits = lax.axis_size("fsdp"), stages()
    turned = [sum(((v >> b) & 1) << (bits - 1 - b) for b in range(bits)) for v in range(length)]
    up, down = jnp.arange(length, dtype=jnp.int32), jnp.array(turned, jnp.int32)
    return me ^ jnp.where(group == 0, up, down)


def send(value, place):
    length, bits = lax.axis_size("fsdp"), stages()
    turned = sum(((place >> b) & 1) << (bits - 1 - b) for b in range(bits))
    pairs = []
    for group, mask in ((0, place), (1, turned)):
        pairs += [(group * length + i, group * length + (i ^ mask)) for i in range(length)]
    return lax.ppermute(value, ("grp", "fsdp"), pairs)


def gather_dp(value):
    length = lax.axis_size("dp")
    return [value] + [
        lax.ppermute(value, "dp", [(i, i ^ mask) for i in range(length)]) for mask in range(1, length)
    ]


def block_of(value, index, rows):
    return lax.dynamic_slice_in_dim(value, index * rows, rows, 0)


def split_three(value):
    high = value.astype(BF16)
    rest = value - high.astype(F32)
    mid = rest.astype(BF16)
    return high, mid, (rest - mid.astype(F32)).astype(BF16)


def pack_sums(plain, along):
    tail = [part.astype(F32) for part in split_three(plain) + split_three(along)]
    return jnp.concatenate(tail + [jnp.zeros((10, plain.shape[1]), F32)], 0).astype(BF16)


def unpack_sums(tail):
    tail = tail.astype(F32)
    return tail[0:1] + tail[1:2] + tail[2:3], tail[3:4] + tail[4:5] + tail[5:6]


def gelu_and_slope(v):
    square = v * v
    t = jnp.tanh(SQRT_2_OVER_PI * (v + 0.044715 * (square * v)))
    rise = 0.5 * (1.0 + t)
    slope = rise + 0.5 * v * (1.0 - t * t) * (SQRT_2_OVER_PI * (1.0 + (3 * 0.044715) * square))
    return v * rise, slope


class Stream:
    def __init__(self, first, first_buf, second, second_buf, parts, base, sems):
        def copy(weight, buf, part):
            return weight.at[0, pl.ds(part[0], part[1]), :], buf.at[pl.ds(part[0] - base, part[1]), :]

        pairs = [copy(first, first_buf, parts[0])]
        for k, part in enumerate(parts):
            if k + 1 < len(parts):
                pairs.append(copy(first, first_buf, parts[k + 1]))
            pairs.append(copy(second, second_buf, part))
        self.copies = [pltpu.make_async_copy(a, b, sems.at[k]) for k, (a, b) in enumerate(pairs)]
        self.next = 0
        for item in self.copies[:AHEAD]:
            item.start()

    def take(self):
        k = self.next
        self.copies[k].wait()
        if k + AHEAD < len(self.copies):
            self.copies[k + AHEAD].start()
        self.next = k + 1


def pipelined(parts, product, finish):
    held = None
    for part in parts:
        value = product(*part)
        if held is not None:
            finish(*held, False)
        held = part + (value,)
    finish(*held, True)


def params(flops, moved, transcendentals=0, grant=50):
    return dict(
        compiler_params=pltpu.CompilerParams(vmem_limit_bytes=grant * MIB),
        cost_estimate=pl.CostEstimate(flops=flops, bytes_accessed=moved, transcendentals=transcendentals),
    )


def struct(shape, dtype):
    return jax.ShapeDtypeStruct(shape, dtype)


def staging(rows, features, lanes):
    return pltpu.VMEM((features, lanes) if rows % 16 else (8, 128), F32)


def place_blocks(target, lanes, stage, order, blocks, rows, first=0):
    for place, value in enumerate(blocks):
        if rows % 16:
            stage[pl.ds(pl.multiple_of(order[first + place] * rows, 8), rows), :] = value().astype(F32)
        else:
            target[pl.ds(pl.multiple_of(order[first + place] * rows, 16), rows), lanes] = value()
    if rows % 16:
        target[:, lanes] = stage[...].astype(target.dtype)


def turn_modulation(modulation, columns):
    for start, size in pieces(0, modulation.shape[2], 128):
        rows = modulation[0, :, pl.ds(start, size)]
        columns[pl.ds(start, size), :] = jnp.concatenate([rows, jnp.zeros((5, size), F32)], 0).T


def normalize(acts, modulation, normed, stats):
    features, tokens = acts.shape[1:]
    parts = pieces(0, features, 128)
    total = jnp.zeros((1, tokens), F32)
    for start, size in parts:
        total += jnp.sum(acts[0, pl.ds(start, size), :].astype(F32), 0, keepdims=True)
    mean = total / features
    total = jnp.zeros((1, tokens), F32)
    for start, size in parts:
        centred = acts[0, pl.ds(start, size), :].astype(F32) - mean
        total += jnp.sum(centred * centred, 0, keepdims=True)
    inv = lax.rsqrt(total / features + EPSILON)
    stats[0:1, :] = mean
    stats[1:2, :] = inv
    for start, size in parts:
        rows = pl.ds(start, size)
        xhat = (acts[0, rows, :].astype(F32) - mean) * inv
        shift, scale = modulation[0, 0:1, rows], modulation[0, 1:2, rows]
        normed[:, rows] = (xhat.T * (1.0 + scale) + shift).astype(BF16)


def against_rows(columns, weight):
    return lax.dot_general(columns, weight, (((1,), (1,)), ((), ())), preferred_element_type=F32)


def accumulate(total, part, weight, before, finish):
    for at, size in pieces(0, weight.shape[1]):
        columns = pl.ds(at, size)
        value = jnp.dot(part, weight[:, columns], preferred_element_type=F32)
        if before is not None:
            value = value + before[:, columns]
        if finish is None:
            total[:, columns] = value
        else:
            finish(at, size, value)


def forward_products(stream, parts, base, normed, in_buf, out_buf, slope_out, total, before, last):
    state = [before]

    def product(at, size):
        stream.take()
        return against_rows(normed[...], in_buf[pl.ds(at - base, size), :])

    def finish(at, size, pre, final):
        rows = pl.ds(at - base, size)
        hidden, slope = gelu_and_slope(pre)
        slope_out[:, rows] = slope
        stream.take()
        accumulate(total, hidden.astype(BF16), out_buf.at[rows, :], state[0], last if final else None)
        state[0] = total

    pipelined(parts, product, finish)


def forward_first_kernel(normed, modulation, w_in, w_out, slope_out, total, mod, in_buf, out_buf, sems):
    parts = pieces(0, slope_out.shape[1])
    stream = Stream(w_in, in_buf, w_out, out_buf, parts, 0, sems)
    turn_modulation(modulation, mod)
    forward_products(stream, parts, 0, normed, in_buf, out_buf, slope_out, total, None, None)


def forward_last_kernel(start, order, normed, before, w_in, w_out, slope_out, *refs):
    outs, (in_buf, out_buf, total, full, sems) = refs[:-5], refs[-5:]
    parts = pieces(start, start + slope_out.shape[1])
    stream = Stream(w_in, in_buf, w_out, out_buf, parts, start, sems)

    def last(at, size, value):
        full[pl.ds(at, size), :] = value.T

    forward_products(stream, parts, start, normed, in_buf, out_buf, slope_out, total, before, last)
    write_blocks(order, full, outs)


def layer_scratch(part, features):
    return [
        pltpu.VMEM((part, features), BF16),
        pltpu.VMEM((part, features), BF16),
    ]


def layer_params(part, features, tokens, transcendentals):
    return params(4 * part * features * tokens, 4 * part * features + 4 * features * tokens, transcendentals)


def forward_first(normed, modulation, w_in, w_out, part, name):
    tokens, features = normed.shape
    return pl.pallas_call(
        forward_first_kernel,
        out_shape=(struct((tokens, part), F32), struct((tokens, features), F32), struct((features, 8), F32)),
        in_specs=[WHOLE, WHOLE, HELD, HELD],
        out_specs=[WHOLE] * 3,
        scratch_shapes=layer_scratch(part, features) + [pltpu.SemaphoreType.DMA((2 * len(pieces(0, part)),))],
        name=name,
        **layer_params(part, features, tokens, part * tokens),
    )(normed, modulation, w_in, w_out)


def forward_last(order, normed, before, w_in, w_out, start, blocks, name):
    hidden, features = w_in.shape[1:]
    tokens, part, rows = before.shape[0], hidden - start, features // blocks
    slope, *outs = pl.pallas_call(
        functools.partial(forward_last_kernel, start),
        out_shape=[struct((tokens, part), F32), struct((rows, tokens), F32)]
        + [struct((rows, tokens), BF16)] * (blocks - 1),
        in_specs=[SCALARS, WHOLE, WHOLE, HELD, HELD],
        out_specs=[WHOLE] * (blocks + 1),
        scratch_shapes=layer_scratch(part, features)
        + [
            pltpu.VMEM((tokens, features), F32),
            pltpu.VMEM((features, tokens), F32),
            pltpu.SemaphoreType.DMA((2 * len(pieces(start, hidden)),)),
        ],
        name=name,
        **layer_params(part, features, tokens, part * tokens),
    )(order, normed, before, w_in, w_out)
    return slope, outs[0], outs[1:]


def write_blocks(order, full, outs):
    for place, target in enumerate(outs):
        rows = target.shape[0]
        offset = pl.multiple_of(order[place] * rows, 8)
        target[...] = full[pl.ds(offset, rows), :].astype(target.dtype)


def backward_products(stream, parts, base, grad, slopes, in_buf, out_buf, total, before, last):
    state = [before]

    def product(at, size):
        stream.take()
        return against_rows(grad[...], out_buf[pl.ds(at - base, size), :])

    def finish(at, size, value, final):
        rows = pl.ds(at - base, size)
        seen = slopes[0].shape[1]
        slope = slopes[0][:, pl.ds(at, size)] if at < seen else slopes[1][:, pl.ds(at - seen, size)]
        stream.take()
        accumulate(total, (value * slope).astype(BF16), in_buf.at[rows, :], state[0], last if final else None)
        state[0] = total

    pipelined(parts, product, finish)


def backward_first_kernel(blocks, part, order, *refs):
    pieces_in, (slope_a, slope_b, w_in, w_out, grad, total, in_buf, out_buf, full, stage, sems) = refs[:blocks], refs[blocks:]
    parts = pieces(0, part)
    stream = Stream(w_out, out_buf, w_in, in_buf, parts, 0, sems)
    values = [lambda ref=ref: ref[...] for ref in pieces_in]
    place_blocks(full, slice(None), stage, order, values, pieces_in[0].shape[0])
    for start, size in pieces(0, full.shape[0], 128):
        rows = pl.ds(start, size)
        grad[:, rows] = full[rows, :].astype(F32).T.astype(BF16)
    backward_products(stream, parts, 0, grad, (slope_a, slope_b), in_buf, out_buf, total, None, None)


def backward_first(order, gathered, slope_a, slope_b, w_in, w_out, part, name):
    hidden, features = w_in.shape[1:]
    blocks, (rows, tokens) = len(gathered), gathered[0].shape
    return pl.pallas_call(
        functools.partial(backward_first_kernel, blocks, part),
        out_shape=(struct((tokens, features), BF16), struct((tokens, features), F32)),
        in_specs=[SCALARS] + [WHOLE] * (blocks + 2) + [HELD, HELD],
        out_specs=[WHOLE] * 2,
        scratch_shapes=layer_scratch(part, features)
        + [
            pltpu.VMEM((features, tokens), BF16),
            staging(rows, features, tokens),
            pltpu.SemaphoreType.DMA((2 * len(pieces(0, part)),)),
        ],
        name=name,
        **layer_params(part, features, tokens, 0),
    )(order, *gathered, slope_a, slope_b, w_in, w_out)


def backward_last_kernel(start, rows, order, grad, before, slope_a, slope_b, acts, stats, mod, w_in, w_out, *refs):
    outs, (sums_out, in_buf, out_buf, total, full, sems) = refs[:-6], refs[-6:]
    hidden, (features, tokens) = w_in.shape[1], full.shape
    parts = pieces(start, hidden)
    stream = Stream(w_out, out_buf, w_in, in_buf, parts, start, sems)
    mean, inv = stats[0:1, :], stats[1:2, :]
    sums = [jnp.zeros((1, tokens), F32), jnp.zeros((1, tokens), F32)]

    def last(at, size, value):
        at = pl.ds(at, size)
        value = value.T
        full[at, :] = value
        scaled = value * (1.0 + mod[at, 1:2])
        xhat = (acts[0, at, :].astype(F32) - mean) * inv
        sums[0] += jnp.sum(scaled, 0, keepdims=True)
        sums[1] += jnp.sum(scaled * xhat, 0, keepdims=True)

    backward_products(stream, parts, start, grad, (slope_a, slope_b), in_buf, out_buf, total, before, last)
    count = len(outs) // 2
    padded = outs[0].shape[0] - 16
    tail = pack_sums(*sums)
    for place in range(count):
        offset = pl.multiple_of(order[2 * place] * rows, 8)
        outs[count + place][...] = full[pl.ds(offset, rows), :]
        offset = pl.multiple_of(order[2 * place + 1] * rows, 8)
        block = full[pl.ds(offset, rows), :]
        if padded > rows:
            block = jnp.concatenate([block, jnp.zeros((padded - rows, tokens), F32)], 0)
        outs[place][:padded, :] = block.astype(BF16)
        outs[place][padded:, :] = tail
    sums_out[0:1, :] = sums[0]
    sums_out[1:2, :] = sums[1]


def backward_last(order, grad, before, slope_a, slope_b, acts, stats, mod, w_in, w_out, start, blocks, name):
    hidden, features = w_in.shape[1:]
    tokens, part, rows, count = before.shape[0], hidden - start, features // blocks, blocks // 2
    outs = pl.pallas_call(
        functools.partial(backward_last_kernel, start, rows),
        out_shape=[struct((-(-rows // 16) * 16 + 16, tokens), BF16)] * count
        + [struct((rows, tokens), F32)] * count
        + [struct((2, tokens), F32)],
        in_specs=[SCALARS] + [WHOLE] * 7 + [HELD, HELD],
        out_specs=[WHOLE] * (blocks + 1),
        scratch_shapes=layer_scratch(part, features)
        + [
            pltpu.VMEM((tokens, features), F32),
            pltpu.VMEM((features, tokens), F32),
            pltpu.SemaphoreType.DMA((2 * len(pieces(start, hidden)),)),
        ],
        name=name,
        **layer_params(part, features, tokens, 0),
    )(order, grad, before, slope_a, slope_b, acts, stats, mod, w_in, w_out)
    return outs[:count], outs[count:-1], outs[-1]


def fold_kernel(rows, count, *refs):
    got, kept, (sums, *outs) = refs[:count], refs[count : 2 * count], refs[2 * count :]
    more = unpack_sums(got[0][-16:, :])
    plain, along = sums[0:1, :] + more[0], sums[1:2, :] + more[1]
    tail = pack_sums(plain, along)
    padded = got[0].shape[0] - 16
    for place in range(count // 2):
        even, odd = 2 * place, 2 * place + 1
        outs[count // 2 + place][...] = kept[even][...] + got[even][:rows, :].astype(F32)
        block = kept[odd][...] + got[odd][:rows, :].astype(F32)
        if padded > rows:
            block = jnp.concatenate([block, jnp.zeros((padded - rows, block.shape[1]), F32)], 0)
        outs[place][:padded, :] = block.astype(BF16)
        outs[place][padded:, :] = tail
    outs[-1][0:1, :] = plain
    outs[-1][1:2, :] = along


def fold(got, kept, sums):
    count, (rows, tokens) = len(kept), kept[0].shape
    outs = pl.pallas_call(
        functools.partial(fold_kernel, rows, count),
        out_shape=[struct(got[0].shape, BF16)] * (count // 2)
        + [struct((rows, tokens), F32)] * (count // 2)
        + [struct((2, tokens), F32)],
        in_specs=[WHOLE] * (2 * count + 1),
        out_specs=[WHOLE] * (count + 1),
        name="fold",
        **params(2 * count * rows * tokens, 8 * count * rows * tokens, grant=12),
    )(*got, *kept, sums)
    return outs[: count // 2], outs[count // 2 : -1], outs[-1]


def prepare_kernel(blocks, order, acts, modulation, own, arrived, weight, *refs):
    outs, (normed, stats, cot0, cot1, full, buf, sem) = refs[:blocks], refs[blocks:]
    load = pltpu.make_async_copy(weight, buf, sem)
    load.start()
    group = order[blocks]
    control = group == 0
    half = cot0.shape[1]
    lanes = pl.ds(pl.multiple_of(group * half, half), half)
    cot0[...] = jnp.where(control, own[:, lanes], arrived[:, lanes])
    mine = jnp.where(control, arrived[:, lanes], own[:, lanes])
    cot1[...] = mine
    normalize(acts, modulation, normed, stats)
    load.wait()
    full[...] = lax.dot_general(mine, buf[...], (((0,), (0,)), ((), ())), preferred_element_type=F32).T
    write_blocks(order, full, outs)


def prepare(order, acts, modulation, own, arrived, weight, blocks):
    rows, tokens = own.shape
    half, features = tokens // 2, weight.shape[1]
    outs = pl.pallas_call(
        functools.partial(prepare_kernel, blocks),
        out_shape=[struct((rows, half), F32)]
        + [struct((rows, half), BF16)] * (blocks - 1)
        + [
            struct((tokens, features), BF16),
            struct((2, tokens), F32),
            struct((rows, half), BF16),
            struct((rows, half), BF16),
        ],
        in_specs=[SCALARS] + [WHOLE] * 4 + [HELD],
        out_specs=[WHOLE] * (blocks + 4),
        scratch_shapes=[
            pltpu.VMEM((features, half), F32),
            pltpu.VMEM(weight.shape, BF16),
            pltpu.SemaphoreType.DMA(()),
        ],
        name="prepare",
        **params(2 * weight.size * half, 2 * weight.size + 4 * blocks * rows * half, grant=50),
    )(order, acts, modulation, own, arrived, weight)
    return outs[0], outs[1:blocks], *outs[blocks:]


def residual_kernel(order, weight, *refs):
    stack, (result, full, stage) = refs[:-3], refs[-3:]
    values = [lambda value=value: value[...] for value in stack]
    place_blocks(full, slice(None), stage, order, values, stack[0].shape[0])
    result[...] = jnp.dot(weight[...], full[...], preferred_element_type=F32)


def residual_rows(order, weight, stack):
    blocks, (rows, half) = len(stack), stack[0].shape
    return pl.pallas_call(
        residual_kernel,
        out_shape=struct((rows, half), F32),
        in_specs=[SCALARS] + [WHOLE] * (blocks + 1),
        out_specs=WHOLE,
        scratch_shapes=[pltpu.VMEM((blocks * rows, half), BF16), staging(rows, blocks * rows, half)],
        name="residual_rows",
        **params(2 * weight.size * half, 2 * weight.size + 4 * blocks * rows * half, grant=12),
    )(order, weight, *stack)


def zero_grad_kernel(blocks, first, count, order, dp_order, *refs):
    cots, refs = (refs[:count], refs[count : 2 * count]), refs[2 * count :]
    stacks = []
    while len(refs) > (9 if first else 6):
        stacks.append((refs[:blocks], refs[blocks : 2 * blocks]))
        refs = refs[2 * blocks :]
    before = None
    if first:
        before, out, lhs, rhs, stage, parked, loads, buf, sems = refs
    else:
        buf, lhs, rhs, stage, parked, loads = refs
    rows, half = cots[0][0].shape
    group = order[blocks]
    moves, places = [], []
    for part in range(count):
        slot = part // 2 * 2 + (dp_order[first + part] & 1)
        for side, owner in enumerate((group, 1 - group)):
            lanes = pl.ds(pl.multiple_of((slot * 2 + owner) * half, half), half)
            moves.append((cots[side][part], lhs.at[:, lanes]))
            values = []
            for place in range(blocks):
                source = stacks[part][side][place] if len(stacks) == count else stacks[0][side][place].at[part]
                if rows % 16:
                    at = (part * 2 + side) * blocks + place
                    target = parked.at[at]
                    values.append(lambda at=at: parked[at])
                else:
                    offset = pl.multiple_of(order[side * (blocks + 1) + place] * rows, 16)
                    target = rhs.at[pl.ds(offset, rows), lanes]
                moves.append((source, target))
            places.append((lanes, values, side * (blocks + 1)))
    moves = [pltpu.make_async_copy(a, b, loads.at[k]) for k, (a, b) in enumerate(moves)]
    for move in moves:
        move.start()
    for move in moves:
        move.wait()
    if rows % 16:
        for lanes, values, shift in places:
            place_blocks(rhs, lanes, stage, order, values, rows, shift)
    copies = []
    for k, (start, size) in enumerate(pieces(0, blocks * rows)):
        columns = pl.ds(start, size)
        value = against_rows(lhs[...], rhs[columns, :])
        buf[:, columns] = value if before is None else before[:, columns] + value
        if before is not None:
            copies.append(pltpu.make_async_copy(buf.at[:, columns], out.at[:, columns], sems.at[k]))
            copies[-1].start()
    for copy in copies:
        copy.wait()


def zero_projection_grad(order, dp_order, first, cots, cots_other, stacks, before, name):
    blocks, (rows, half) = len(stacks[0][0]), cots[0].shape
    count = len(cots)
    features, tokens = blocks * rows, count * 2 * half
    flat = [block for pair in stacks for side in pair for block in side]
    extra = [] if before is None else [before]
    scratch = [
        pltpu.VMEM((rows, tokens), BF16),
        pltpu.VMEM((features, tokens), BF16),
        staging(rows, features, half),
        pltpu.VMEM((count * 2 * blocks, rows, half) if rows % 16 else (1, 8, 128), BF16),
        pltpu.SemaphoreType.DMA((count * 2 * (blocks + 1),)),
    ]
    if extra:
        scratch += [
            pltpu.VMEM((rows, features), F32),
            pltpu.SemaphoreType.DMA((len(pieces(0, features)),)),
        ]
    return pl.pallas_call(
        functools.partial(zero_grad_kernel, blocks, first, count),
        out_shape=struct((rows, features), F32),
        in_specs=[SCALARS] * 2 + [ANYWHERE] * (2 * count + len(flat)) + [WHOLE] * len(extra),
        out_specs=HELD if extra else WHOLE,
        scratch_shapes=scratch,
        name=name,
        **params(2 * tokens * rows * features, 4 * rows * features + 2 * tokens * (rows + features), grant=28),
    )(order, dp_order, *cots, *cots_other, *flat, *extra)


def steps(values, level, *during):
    got = [step(value, level) for value in values]
    return list(lax.optimization_barrier((tuple(got),) + during)[0]) if during else got


def direct(values, *during):
    got = [send(value, place + 1) for place, value in enumerate(values)]
    return list(lax.optimization_barrier((tuple(got),) + during)[0])


def local(acts, modulation, w_in, w_out, zero_weight, cotangent):
    own_cot = cotangent[0]
    features, tokens = acts.shape[1:]
    hidden = w_in.shape[1]
    rows = own_cot.shape[0]
    half = tokens // 2
    blocks, levels = lax.axis_size("fsdp"), stages()
    parts = lax.axis_size("dp")
    group = lax.axis_index("grp").astype(jnp.int32)
    me = lax.axis_index("fsdp").astype(jnp.int32)
    is_control = group == 0
    places = block_order(group, me)
    order = jnp.concatenate([places, group[None], block_order(1 - group, me)])
    dp_order = lax.axis_index("dp").astype(jnp.int32) ^ jnp.arange(parts, dtype=jnp.int32)

    arrived = swap_grp(own_cot)
    own_term, sent, normed, stats, cot0, cot1 = prepare(
        order, acts, modulation, own_cot, arrived, zero_weight, blocks
    )
    split, cut = split_rows(hidden)
    slope_a, total, mod = forward_first(after(normed, *sent), modulation, w_in, w_out, split, "forward_first")
    own_mod = block_of(mod, me, rows)
    own_gate = own_mod[:, 2:3]
    got = direct(sent, total)
    up_half = own_term + cot0.astype(F32) + sum(value.astype(F32) for value in got)
    up_rows = jnp.where(is_control, jnp.concatenate([up_half, swap_grp(up_half)], 1), own_cot.astype(F32))
    grad_rows = (own_gate * up_rows).astype(BF16)

    slope_b, kept, sent = forward_last(
        order, after(normed, grad_rows), total, w_in, w_out, split, blocks, "forward_last"
    )
    gathered = [grad_rows] + direct([grad_rows] * (blocks - 1), kept)
    grad, total = backward_first(
        order, after(gathered, *sent), slope_a, slope_b, w_in, w_out, cut, "backward_first"
    )
    got = direct(sent, total)
    own_values = block_of(acts[0], me, rows).astype(F32)
    sums = own_values + own_gate * (kept + sum(value.astype(F32) for value in got))
    out_rows = sums.astype(BF16)

    out_half = jnp.where(is_control, out_rows[:, :half], swap_grp(out_rows[:, half:]))
    far = gather_dp(out_half)[1:]
    sent, kept, token_sums = backward_last(
        order, after(grad, out_half), total, slope_a, slope_b, acts, stats, mod, w_in, w_out, cut, blocks, "backward_last"
    )
    near = [out_half, step(out_half, 0)]
    far, near, sent, kept, token_sums = lax.optimization_barrier((far, near, sent, kept, token_sums))
    for level in range(1, levels):
        near = near + steps(near, level)
    near_other = [swap_grp(value) for value in near]
    residual = residual_rows(order, zero_weight, near)
    cots = gather_dp(after(cot1, token_sums))
    cots_other = [swap_grp(value) for value in cots]

    gathers = [[far[0]], [jnp.stack(far[1:])]]
    for level in range(levels):
        got = steps(sent, level)
        gathers = [blocks_so_far + steps(blocks_so_far, level) for blocks_so_far in gathers]
        if level + 1 < levels:
            sent, kept, token_sums = fold(got, kept, token_sums)
    more = unpack_sums(got[0][-16:])
    plain, along = token_sums[0:1] + more[0], token_sums[1:2] + more[1]
    kept = [kept[0] + got[0][:rows].astype(F32)]
    mean, inv = stats[0:1], stats[1:2]
    back = inv * (
        kept[0] * (1.0 + own_mod[:, 1:2]) - plain / features - (own_values - mean) * inv * (along / features)
    )
    residual = jnp.concatenate([swap_grp(residual), residual], 1)
    block_rows = jnp.where(is_control, out_rows, (sums + residual).astype(BF16))

    stacks = [(near, near_other)] + [(mine, [swap_grp(value) for value in mine]) for mine in gathers]
    zero_grad = zero_projection_grad(
        order, dp_order, 0, cots[:2], cots_other[:2], stacks[:2], None, "zero_projection_grad_first"
    )
    zero_grad = zero_projection_grad(
        order, dp_order, 2, cots[2:], cots_other[2:], stacks[2:], zero_grad, "zero_projection_grad_last"
    )
    return (block_rows[None], (up_rows + back)[None], zero_grad)


def solution(mesh):
    placed = (
        P("grp", None, "dp"),
        P("grp", None, None),
        P("grp", "fsdp", None),
        P("grp", "fsdp", None),
        P("fsdp", None),
        P("grp", "fsdp", "dp"),
    )
    return jax.shard_map(
        local,
        mesh=mesh,
        in_specs=placed,
        out_specs=(P("grp", "fsdp", "dp"), P("grp", "fsdp", "dp"), P("fsdp", None)),
        check_vma=False,
    )
```
